32 devices in a mesh: dp: 2 (over y), expert: 16 (over z, x, core).
Axes of the slice: x: 2, y: 2, z: 4, core: 2. Of those that a mesh axis runs over, the one named last changes fastest.
Arguments:
- inputs: bfloat16 [2, 32, 128, 1536], P(None, ('dp', 'expert')), may hold values from -6 to 6
- cotangent: bfloat16 [2, 32, 128, 1536], P(None, ('dp', 'expert')), may hold values from -6 to 6
- routes: int32 [2, 32, 128, 4], P(None, ('dp', 'expert')), may hold values from 0 to 15, all different within a row
- attention_gain: bfloat16 [1536], P(('dp', 'expert')), may hold values from 0.25 to 1.75
- query_weight: bfloat16 [1536, 1536], P(('dp', 'expert')), may hold values from -0.15625 to 0.15625
- key_matrix: bfloat16 [1536, 256], P(('dp', 'expert')), may hold values from -0.15625 to 0.15625
- value_matrix: bfloat16 [1536, 256], P(('dp', 'expert')), may hold values from -0.15625 to 0.15625
- output_weight: bfloat16 [1536, 1536], P(None, ('dp', 'expert')), may hold values from -0.625 to 0.625
- mixture_gain: bfloat16 [1536], P(('dp', 'expert')), may hold values from 0.25 to 1.75
- router_weight: bfloat16 [1536, 16], P(('dp', 'expert')), may hold values from -0.078125 to 0.078125
- gate_weight: bfloat16 [16, 1536, 768], P('expert', 'dp'), may hold values from -0.15625 to 0.15625
- up_weight: bfloat16 [16, 1536, 768], P('expert', 'dp'), may hold values from -0.15625 to 0.15625
- down_weight: bfloat16 [16, 768, 1536], P('expert', 'dp'), may hold values from -0.875 to 0.875
Outputs:
- outputs: bfloat16 [2, 32, 128, 1536], P(None, ('dp', 'expert'))
- input_grad: float32 [2, 32, 128, 1536], P(None, ('dp', 'expert'))
- attention_gain_grad: float32 [1536], P(('dp', 'expert'))
- query_grad: float32 [1536, 1536], P(('dp', 'expert'))
- key_grad: float32 [1536, 256], P(('dp', 'expert'))
- value_grad: float32 [1536, 256], P(('dp', 'expert'))
- output_grad: float32 [1536, 1536], P(None, ('dp', 'expert'))
- mixture_gain_grad: float32 [1536], P(('dp', 'expert'))
- router_grad: float32 [1536, 16], P(('dp', 'expert'))
- gate_grad: float32 [16, 1536, 768], P('expert', 'dp')
- up_grad: float32 [16, 1536, 768], P('expert', 'dp')
- down_grad: float32 [16, 768, 1536], P('expert', 'dp')
The draws below stay inside these ranges and needn't reach their ends.
Inputs may be any that keep to these rules, and one draw needn't show every extreme that they name: `routes`: each token names 4 different experts, the first of highest priority.
All inputs are finite; a program needn't handle non-finite values.
Results may differ from the reference program's by a relative error of at most 0.018.
Values may be sent and summed in bfloat16 or wider, within the bound.
No kernel may reach another device: no remote copies, remote signals or barrier semaphores. Data moves between devices by JAX's collectives and lax.ppermute only.
A program may use at most 192 MiB of HBM per device.

```python
import math
import jax
import jax.numpy as jnp
from jax import lax

MODEL_WIDTH = 1536
QUERY_HEADS = 12
KEY_VALUE_HEADS = 2
HEAD_SIZE = 128
FF = 768
TOPK = 4
MB = 2
SEQUENCE_TOKENS = 128
E = 16
SEQS = 32
CAP = 40


def levels(key, dims, cuts, low, top_value):
    loudness, own = 1.0, jax.random.fold_in(key, 6)
    for dim, parts in cuts:
        heights = jnp.exp(jax.random.uniform(jax.random.fold_in(own, dim), (parts,), jnp.float32, low / len(cuts), top_value / len(cuts)))
        loudness = loudness * jnp.repeat(heights, dims[dim] // parts).reshape([-1 if axis == dim else 1 for axis in range(len(dims))])
    return loudness


def different_ones(stream_key, rows, amount, top, lift):
    order = jax.random.permutation(jax.random.fold_in(stream_key, 1), amount)
    favour = order
    for power in range(3):
        favour = favour * favour // amount
    favour = favour * lift // amount
    tickets = jax.random.randint(jax.random.fold_in(stream_key, 2), (rows, amount), 0, 4096) + favour
    fixed_rows = jax.random.permutation(jax.random.fold_in(stream_key, 3), rows)[jnp.arange(amount) % rows]
    tickets = jnp.where(jnp.arange(rows)[:, None] == fixed_rows[None, :], 1 << 14, tickets)
    score = tickets * amount + jnp.arange(amount)
    return lax.top_k(score.astype(jnp.int32), top)[1].astype(jnp.int32)


def noise(own_key, shape, deviation, most, split=(), held_as=jnp.bfloat16):
    gain = levels(own_key, shape, split, -0.22, 0.18) if split else 1.0
    drawn = jax.random.normal(own_key, shape, jnp.float32) * deviation * gain
    return jnp.minimum(jnp.maximum(drawn, -most), most).astype(held_as)


def setup_inputs(seed: int = 0) -> dict:
    seeds = jax.random.split(jax.random.key(seed), 14)
    inputs = noise(seeds[0], (MB, SEQS, SEQUENCE_TOKENS, MODEL_WIDTH), 1.0, 6.0, ((1, 32),))
    cotangent = noise(seeds[1], (MB, SEQS, SEQUENCE_TOKENS, MODEL_WIDTH), 1.0, 6.0, ((1, 32),))
    routes = different_ones(seeds[2], MB * SEQS * SEQUENCE_TOKENS, E, TOPK, 2048).reshape((MB, SEQS, SEQUENCE_TOKENS, TOPK))
    attention_gain = jnp.clip(1.0 + 0.15 * jax.random.normal(seeds[3], (MODEL_WIDTH,), jnp.float32), 0.25, 1.75).astype(jnp.bfloat16)
    query_weight = noise(seeds[4], (MODEL_WIDTH, QUERY_HEADS * HEAD_SIZE), MODEL_WIDTH ** -0.5, 0.15625, ((0, 32),))
    key_matrix = noise(seeds[5], (MODEL_WIDTH, KEY_VALUE_HEADS * HEAD_SIZE), MODEL_WIDTH ** -0.5, 0.15625, ((0, 32),))
    value_matrix = noise(seeds[6], (MODEL_WIDTH, KEY_VALUE_HEADS * HEAD_SIZE), MODEL_WIDTH ** -0.5, 0.15625, ((0, 32),))
    output_weight = noise(seeds[7], (QUERY_HEADS * HEAD_SIZE, MODEL_WIDTH), (QUERY_HEADS * HEAD_SIZE // 16) ** -0.5, 0.625, ((1, 32),))
    mixture_gain = jnp.clip(1.0 + 0.15 * jax.random.normal(seeds[8], (MODEL_WIDTH,), jnp.float32), 0.25, 1.75).astype(jnp.bfloat16)
    router_weight = noise(seeds[9], (MODEL_WIDTH, E), (4 * MODEL_WIDTH) ** -0.5, 0.078125, ((0, 32),))
    gate_weight = noise(seeds[10], (E, MODEL_WIDTH, FF), MODEL_WIDTH ** -0.5, 0.15625, ((0, 16), (1, 2)))
    up_weight = noise(seeds[11], (E, MODEL_WIDTH, FF), MODEL_WIDTH ** -0.5, 0.15625, ((0, 16), (1, 2)))
    down_weight = noise(seeds[12], (E, FF, MODEL_WIDTH), (FF // 16) ** -0.5, 0.875, ((0, 16), (1, 2)))
    return {"inputs": inputs, "cotangent": cotangent, "routes": routes, "attention_gain": attention_gain, "query_weight": query_weight, "key_matrix": key_matrix, "value_matrix": value_matrix, "output_weight": output_weight, "mixture_gain": mixture_gain, "router_weight": router_weight, "gate_weight": gate_weight, "up_weight": up_weight, "down_weight": down_weight}


epsilon = 1e-06
rope_base = 10000.0
masked_score = -1e+30
highest = lax.Precision.HIGHEST

@jax.custom_vjp
def lower_half(v):
    return lax.optimization_barrier(v.astype(jnp.bfloat16)).astype(jnp.float32)

@jax.custom_vjp
def low_back(v):
    return v

def low_keep(v):
    return (lower_half(v), None)

def low_pass(kept, grad):
    return (grad,)

def back_keep(v):
    return (v, None)

def back_low(kept, grad):
    return (lower_half(grad),)
lower_half.defvjp(low_keep, low_pass)
low_back.defvjp(back_keep, back_low)

def rms_scale(values):
    return lax.rsqrt(lax.optimization_barrier(jnp.mean(values * values, axis=-1, keepdims=True)) + epsilon)

def rope_tables(sequence_length, head_width):
    halfway = head_width // 2
    frequency = rope_base ** (-(jnp.arange(halfway, dtype=jnp.float32) * 2.0 / head_width))
    angles = jnp.arange(sequence_length, dtype=jnp.float32)[:, None] * frequency[None, :]
    cosine_table = jnp.concatenate([jnp.cos(angles), jnp.cos(angles)], axis=-1)
    sine_table = jnp.concatenate([jnp.sin(angles), jnp.sin(angles)], axis=-1)
    return (cosine_table, sine_table)

def apply_rotation(values, cosine_table, sine_table):
    halfway = values.shape[-1] // 2
    turned = jnp.concatenate([-values[..., halfway:], values[..., :halfway]], axis=-1)
    return values * cosine_table + turned * sine_table

def route_tables(route_rows, experts, capacity, topk_count):
    expert_ids = route_rows.reshape(-1).astype(jnp.int32)
    onehot_table = (expert_ids[:, None] == jnp.arange(experts, dtype=jnp.int32)[None, :]).astype(jnp.int32)
    position = lax.optimization_barrier(jnp.sum(jnp.cumsum(onehot_table, axis=0) * onehot_table, axis=1)) - 1
    kept_pairs = position < capacity
    slot_raw = jnp.where(kept_pairs, expert_ids * capacity + position, experts * capacity).astype(jnp.int32)
    token_ids = (jnp.arange(expert_ids.shape[0], dtype=jnp.int32) // topk_count).astype(jnp.int32)
    slot_token = jnp.zeros((experts * capacity,), jnp.int32).at[slot_raw].set(token_ids, mode='drop')
    slot_valid = jnp.zeros((experts * capacity,), jnp.int32).at[slot_raw].set(1, mode='drop')
    return (slot_token, slot_valid, slot_raw, kept_pairs.astype(jnp.int32))

def reference(inputs, cotangent, routes, attention_gain, query_weight, key_matrix, value_matrix, output_weight, mixture_gain, router_weight, gate_weight, up_weight, down_weight):
    sequence_count = MB * SEQS
    queries_per_group = math.gcd(sequence_count, max(1, 4096 // SEQUENCE_TOKENS))
    score_scale = 1.0 / math.sqrt(HEAD_SIZE)
    cosine_table, sine_table = rope_tables(SEQUENCE_TOKENS, HEAD_SIZE)
    cosine_expanded = cosine_table[None, :, None, :]
    sine_expanded = sine_table[None, :, None, :]
    causal = jnp.arange(SEQUENCE_TOKENS)[:, None] >= jnp.arange(SEQUENCE_TOKENS)[None, :]
    flat_routes = routes.reshape(sequence_count, SEQUENCE_TOKENS, TOPK).astype(jnp.int32)
    slot_token, slot_valid, slot_raw, kept_pairs = jax.vmap(lambda rows_in: route_tables(rows_in, E, CAP, TOPK))(flat_routes)
    sequence_ids = jnp.arange(sequence_count, dtype=jnp.int32)[:, None]
    row_index = (slot_token + sequence_ids * SEQUENCE_TOKENS).reshape(sequence_count, E, CAP).transpose(1, 0, 2).reshape(E, sequence_count * CAP).astype(jnp.int32)
    row_valid = slot_valid.reshape(sequence_count, E, CAP).transpose(1, 0, 2).reshape(E, sequence_count * CAP).astype(jnp.float32)
    clipped = jnp.minimum(slot_raw, E * CAP - 1)
    pair_index = ((clipped // CAP * sequence_count + sequence_ids) * CAP + clipped % CAP).reshape(sequence_count, SEQUENCE_TOKENS, TOPK).astype(jnp.int32)
    pair_keep = kept_pairs.reshape(sequence_count, SEQUENCE_TOKENS, TOPK).astype(jnp.float32)

    def forward(tokens, gain_first, query_full, key_full, value_full, output_full, gain_second, router_full, gate_full, up_full, down_full):

        def attend(sequence_block):
            first_hat = sequence_block * rms_scale(sequence_block)
            normed_one = lower_half(first_hat * gain_first)
            query_pre = low_back(jnp.einsum('bld,de->ble', normed_one, query_full, precision=highest))
            key_before_rotation = low_back(jnp.einsum('bld,de->ble', normed_one, key_full, precision=highest))
            value_projected = lower_half(low_back(jnp.einsum('bld,de->ble', normed_one, value_full, precision=highest)))
            query_rotated = lower_half(apply_rotation(query_pre.reshape(queries_per_group, SEQUENCE_TOKENS, QUERY_HEADS, HEAD_SIZE), cosine_expanded, sine_expanded))
            key_rotated = lower_half(apply_rotation(key_before_rotation.reshape(queries_per_group, SEQUENCE_TOKENS, KEY_VALUE_HEADS, HEAD_SIZE), cosine_expanded, sine_expanded))
            grouped_query = query_rotated.reshape(queries_per_group, SEQUENCE_TOKENS, KEY_VALUE_HEADS, QUERY_HEADS // KEY_VALUE_HEADS, HEAD_SIZE)
            value_per_head = value_projected.reshape(queries_per_group, SEQUENCE_TOKENS, KEY_VALUE_HEADS, HEAD_SIZE)
            scores = low_back(jnp.einsum('blcgd,bmcd->bcglm', grouped_query, key_rotated, precision=highest) * score_scale)
            scores = jnp.where(causal, scores, masked_score)
            softmax_rows = lower_half(jax.nn.softmax(scores, axis=-1))
            mixed_heads = jnp.einsum('bcglm,bmcd->blcgd', softmax_rows, value_per_head, precision=highest)
            mixed_heads = lower_half(low_back(mixed_heads.reshape(queries_per_group, SEQUENCE_TOKENS, QUERY_HEADS * HEAD_SIZE)))
            branch = low_back(jnp.einsum('ble,ed->bld', mixed_heads, output_full, precision=highest))
            return sequence_block + branch
        hidden = lax.map(jax.checkpoint(attend), tokens.reshape(sequence_count // queries_per_group, queries_per_group, SEQUENCE_TOKENS, MODEL_WIDTH))
        hidden = hidden.reshape(sequence_count, SEQUENCE_TOKENS, MODEL_WIDTH)
        second_hat = hidden * rms_scale(hidden)
        normed_two = lower_half(second_hat * gain_second)
        logits = low_back(jnp.einsum('bld,de->ble', normed_two, router_full, precision=highest))
        gate_values = jax.nn.softmax(jnp.take_along_axis(logits, flat_routes, axis=-1), axis=-1)
        flat_normed = normed_two.reshape(sequence_count * SEQUENCE_TOKENS, MODEL_WIDTH)

        def expert_block(pieces):
            index_part, valid_part, gate_one, up_one, down_one = pieces
            expert_rows = low_back(flat_normed[index_part] * valid_part[:, None])
            gate_pre = low_back(jnp.dot(expert_rows, gate_one, precision=highest, preferred_element_type=jnp.float32))
            up_pre = low_back(jnp.dot(expert_rows, up_one, precision=highest, preferred_element_type=jnp.float32))
            activated = lower_half(jax.nn.silu(gate_pre) * up_pre)
            return lower_half(low_back(jnp.dot(activated, down_one, precision=highest, preferred_element_type=jnp.float32)))
        produced = lax.map(jax.checkpoint(expert_block), (row_index, row_valid, gate_full, up_full, down_full))
        produced = produced.reshape(E * sequence_count * CAP, MODEL_WIDTH)
        mixture = hidden
        for rank_index in range(TOPK):
            weight_now = gate_values[:, :, rank_index] * pair_keep[:, :, rank_index]
            mixture = mixture + weight_now[:, :, None] * produced[pair_index[:, :, rank_index]]
        return mixture
    result, pullback = jax.vjp(forward, inputs.astype(jnp.float32).reshape(sequence_count, SEQUENCE_TOKENS, MODEL_WIDTH), attention_gain.astype(jnp.float32), query_weight.astype(jnp.float32), key_matrix.astype(jnp.float32), value_matrix.astype(jnp.float32), output_weight.astype(jnp.float32), mixture_gain.astype(jnp.float32), router_weight.astype(jnp.float32), gate_weight.astype(jnp.float32), up_weight.astype(jnp.float32), down_weight.astype(jnp.float32))
    gradients = pullback(cotangent.astype(jnp.float32).reshape(sequence_count, SEQUENCE_TOKENS, MODEL_WIDTH))
    return (result.reshape(MB, SEQS, SEQUENCE_TOKENS, MODEL_WIDTH).astype(jnp.bfloat16), gradients[0].reshape(MB, SEQS, SEQUENCE_TOKENS, MODEL_WIDTH), gradients[1], gradients[2], gradients[3], gradients[4], gradients[5], gradients[6], gradients[7], gradients[8], gradients[9], gradients[10])
```

```python
import functools
import math

import jax
import jax.numpy as jnp
import numpy as np
from jax import lax
from jax.experimental import pallas as pl
from jax.experimental.pallas import tpu as pltpu
from jax.sharding import PartitionSpec as P

WIDTH = 1536
QUERY_HEADS = 12
KEY_VALUE_HEADS = 2
HEAD = 128
GROUP = QUERY_HEADS // KEY_VALUE_HEADS
Q_COLS = QUERY_HEADS * HEAD
KV_COLS = KEY_VALUE_HEADS * HEAD
MISC = Q_COLS + 2 * KV_COLS
EXTRA = 16
LANES = 128
EPSILON = 1e-06
ROPE_BASE = 10000.0
MASKED = -1e30
SCALE = 1.0 / math.sqrt(HEAD)

f32 = jnp.float32
bf16 = jnp.bfloat16


def dot(a, b, ca=1, cb=0):
    return lax.dot_general(a, b, (((ca,), (cb,)), ((), ())), preferred_element_type=f32)


def vmem(n):
    return [pl.BlockSpec(memory_space=pltpu.VMEM)] * n


def smem():
    return pl.BlockSpec(memory_space=pltpu.SMEM)


def call(body, outs, ins, args, name, flops, scratch=()):
    size = sum(math.prod(a.shape) * a.dtype.itemsize for a in args)
    size += sum(math.prod(o.shape) * o.dtype.itemsize for o in outs)
    return pl.pallas_call(
        body,
        out_shape=outs,
        in_specs=ins,
        out_specs=vmem(len(outs)),
        scratch_shapes=list(scratch),
        compiler_params=pltpu.CompilerParams(vmem_limit_bytes=60 * 1024 * 1024),
        cost_estimate=pl.CostEstimate(flops=flops, bytes_accessed=size, transcendentals=0),
        name=name,
    )(*args)


def sds(shape, dtype):
    return jax.ShapeDtypeStruct(shape, dtype)


def rope_tables(length):
    half = HEAD // 2
    frequency = ROPE_BASE ** (-(np.arange(half, dtype=np.float64) * 2.0 / HEAD))
    angles = np.arange(length, dtype=np.float64)[:, None] * frequency[None, :]
    cos, sin = np.cos(angles), np.sin(angles)
    cosine = np.concatenate([cos, cos], axis=1).astype(np.float32)
    signed = np.concatenate([-sin, sin], axis=1).astype(np.float32)
    return cosine, signed


def place(where_ref, scratch, piece_refs, first=0):
    at = first
    for ref in piece_refs:
        blocks, rows, _ = ref.shape
        for j in range(blocks):
            start = pl.multiple_of(where_ref[at] * rows, 16 if rows % 16 == 0 else 8)
            scratch[pl.ds(start, rows), :] = ref[j]
            at += 1


def scale_of(z):
    return lax.rsqrt(jnp.mean(z * z, axis=-1, keepdims=True) + EPSILON)


def heads_of(ref, b, length, c):
    return jnp.concatenate(
        [ref[b * length : (b + 1) * length, h * HEAD : (h + 1) * HEAD] for h in range(c * GROUP, (c + 1) * GROUP)],
        axis=0,
    )


def causal_mask(length):
    row = lax.broadcasted_iota(jnp.int32, (length, length), 0)
    column = lax.broadcasted_iota(jnp.int32, (length, length), 1)
    return jnp.concatenate([row >= column] * GROUP, axis=0)


def softmax_of(q, k, keep):
    s = jnp.where(keep, dot(q, k, 1, 1) * SCALE, MASKED)
    e = jnp.exp(s - jnp.max(s, axis=-1, keepdims=True))
    return e / jnp.sum(e, axis=-1, keepdims=True)


def attend_body(seqs, experts, n_pieces, where_ref, x_ref, cos_ref, sin_ref, *refs):
    pieces = refs[:n_pieces]
    w_ref, gain_ref, n1_ref, q_ref, k_ref, v_ref, mixed_ref = refs[n_pieces:]
    length = x_ref.shape[0] // seqs
    place(where_ref, w_ref, pieces)
    gains = jnp.transpose(w_ref[:, MISC : MISC + LANES].astype(f32))[experts : experts + 8]
    gain_ref[...] = gains
    x = x_ref[...].astype(f32)
    n1 = (x * scale_of(x) * gains[0:1]).astype(bf16)
    n1_ref[...] = n1
    cos = jnp.concatenate([cos_ref[...]] * seqs, axis=0)
    sin = jnp.concatenate([sin_ref[...]] * seqs, axis=0)

    def rotated(u):
        return (u * cos + pltpu.roll(u, HEAD // 2, 1) * sin).astype(bf16)

    kv = dot(n1, w_ref[:, Q_COLS:MISC])
    v_ref[...] = kv[:, KV_COLS:].astype(bf16)
    for c in range(KEY_VALUE_HEADS):
        k_ref[:, c * HEAD : (c + 1) * HEAD] = rotated(kv[:, c * HEAD : (c + 1) * HEAD])
    keep = causal_mask(length)
    for c in range(KEY_VALUE_HEADS):
        cols = GROUP * HEAD
        q = dot(n1, w_ref[:, c * cols : (c + 1) * cols])
        for h in range(GROUP):
            at = c * cols + h * HEAD
            q_ref[:, at : at + HEAD] = rotated(q[:, h * HEAD : (h + 1) * HEAD])
        for b in range(seqs):
            rows = slice(b * length, (b + 1) * length)
            k = k_ref[rows, c * HEAD : (c + 1) * HEAD]
            v = v_ref[rows, c * HEAD : (c + 1) * HEAD]
            p = softmax_of(heads_of(q_ref, b, length, c), k, keep).astype(bf16)
            o = dot(p, v).astype(bf16)
            for h in range(GROUP):
                at = c * cols + h * HEAD
                mixed_ref[rows, at : at + HEAD] = o[h * length : (h + 1) * length]


def project_body(experts, n_pieces, where_ref, x_ref, mixed_ref, gain_ref, misc_ref, routes_ref, *refs):
    pieces = refs[:n_pieces]
    o_ref, hidden_ref, send_ref, gate_ref = refs[n_pieces:]
    place(where_ref, o_ref, pieces)
    tokens = x_ref.shape[0]
    h = x_ref[...].astype(f32) + dot(mixed_ref[...], o_ref[...], 1, 1)
    hidden_ref[...] = h
    n2 = (h * scale_of(h) * gain_ref[1:2]).astype(bf16)
    send_ref[0:tokens] = n2
    z = dot(n2, misc_ref[...])
    lane = lax.broadcasted_iota(jnp.int32, (tokens, LANES), 1)
    chosen = lane == routes_ref[:, 0:1]
    for j in range(1, routes_ref.shape[1]):
        chosen = chosen | (lane == routes_ref[:, j : j + 1])
    top = jnp.max(jnp.where(chosen, z, MASKED), axis=-1, keepdims=True)
    e = jnp.where(chosen, jnp.exp(jnp.where(chosen, z - top, 0.0)), 0.0)
    gate = e / jnp.sum(e, axis=-1, keepdims=True)
    gate_ref[...] = gate
    high = gate.astype(bf16).astype(f32)
    tables = [jnp.transpose(t) for t in (high, gate - high, chosen.astype(f32))]
    blank = jnp.zeros((EXTRA, tokens), f32)
    parts = []
    for first in range(0, experts, EXTRA):
        parts += [t[first : first + EXTRA] for t in tables]
    parts += [blank] * (WIDTH // tokens - len(parts))
    send_ref[tokens:] = jnp.concatenate(parts, axis=1).astype(bf16)


def expert_body(layout, capacity, slots, tokens, seqs, which_ref, *refs):
    arrays, n_in = layout
    count = len(arrays)
    ins = refs[:n_in]
    gate_ref, up_ref, down_ref = refs[n_in : n_in + 3]
    outs = refs[n_in + 3 :]
    out_refs, dx_refs = outs[:count], outs[count : 2 * count]
    xs_ref, dy_ref, act_ref, du_ref, dw_ref, gs_ref, gcol_ref = outs[2 * count :]
    length = tokens // seqs
    me = which_ref[0]
    row_in = lax.rem(me, EXTRA)
    row = lax.broadcasted_iota(jnp.int32, (EXTRA, tokens), 0)
    mine = row == row_in
    block = lax.div(me, EXTRA)

    def table(extra, k):
        t = jnp.zeros((EXTRA, tokens), f32)
        for b in range(WIDTH // (3 * tokens)):
            at = (3 * b + k) * tokens
            t = jnp.where(block == b, extra[:, at : at + tokens].astype(f32), t)
        return jnp.sum(jnp.where(mine, t, 0.0), axis=0, keepdims=True)

    def read(pieces, first, rows):
        got = []
        for index, start, size, offset in pieces:
            lo, hi = max(first, start), min(first + rows, start + size)
            if lo < hi:
                got.append(ins[index][offset + lo - start : offset + hi - start])
        return got[0] if len(got) == 1 else jnp.concatenate(got, axis=0)

    tri_a = lax.broadcasted_iota(jnp.int32, (length, length), 0)
    tri_b = lax.broadcasted_iota(jnp.int32, (length, length), 1)
    before = (tri_a < tri_b).astype(bf16)
    slot = lax.broadcasted_iota(jnp.int32, (slots, tokens), 0).astype(f32)
    gates, masks = [], []
    for n2_pieces, _ in arrays:
        extra = read(n2_pieces, tokens, EXTRA)
        gates.append(table(extra, 0) + table(extra, 1))
        masks.append(table(extra, 2))
    picks = []
    for i, (n2_pieces, g_pieces) in enumerate(arrays):
        at = []
        for b in range(seqs):
            m = masks[i][:, b * length : (b + 1) * length]
            earlier = dot(jnp.broadcast_to(m, (16, length)).astype(bf16), before)[0:1]
            keep = (m > 0.5) & (earlier < capacity)
            at.append(jnp.where(keep, earlier + b * (slots // seqs), -1.0))
        pick = (slot == jnp.concatenate(at, axis=1)).astype(f32)
        gcol_ref[i * slots : (i + 1) * slots, :] = jnp.broadcast_to(
            jnp.sum(pick * gates[i], axis=1, keepdims=True), (slots, LANES)
        )
        pick = pick.astype(bf16)
        picks.append(pick)
        rows = slice(i * slots, (i + 1) * slots)
        xs_ref[rows, :] = dot(pick, read(n2_pieces, 0, tokens)).astype(bf16)
        gs_ref[rows, :] = dot(pick, read(g_pieces, 0, tokens)).astype(bf16)
    xs = xs_ref[...]
    u = dot(xs, gate_ref[...])
    w = dot(xs, up_ref[...])
    s = 1.0 / (1.0 + jnp.exp(-u))
    act = (u * s * w).astype(bf16)
    act_ref[...] = act
    y = dot(act, down_ref[...]).astype(bf16).astype(f32)
    gcol = gcol_ref[:, 0:1]
    gs = gs_ref[...].astype(f32)
    dy = (gcol * gs).astype(bf16)
    dy_ref[...] = dy
    dg = jnp.sum(gs * y, axis=1, keepdims=True)
    weighted = (gcol * y).astype(bf16)
    dact = dot(dy, down_ref[...], 1, 1)
    du = (dact * w * s * (1.0 + u * (1.0 - s))).astype(bf16)
    dw = (dact * (u * s)).astype(bf16)
    du_ref[...] = du
    dw_ref[...] = dw
    dx = (dot(du, gate_ref[...], 1, 1) + dot(dw, up_ref[...], 1, 1)).astype(bf16)
    for i in range(count):
        rows = slice(i * slots, (i + 1) * slots)
        out_refs[i][...] = dot(picks[i], weighted[rows], 0, 0).astype(bf16)
        dx_refs[i][0:tokens] = dot(picks[i], dx[rows], 0, 0).astype(bf16)
        back = jnp.sum(picks[i].astype(f32) * dg[rows], axis=0, keepdims=True)
        high = back.astype(bf16).astype(f32)
        blank = jnp.zeros((EXTRA, tokens), f32)
        parts = []
        for b in range(WIDTH // (3 * tokens)):
            here = mine & (block == b)
            parts += [jnp.where(here, high, 0.0), jnp.where(here, back - high, 0.0), blank]
        dx_refs[i][tokens:] = jnp.concatenate(parts, axis=1).astype(bf16)


def weights_body(n, half, adds, which_ref, *refs):
    lists = [refs[k * n : (k + 1) * n] for k in range(5)]
    xs, dys, acts, dus, dws = lists
    more = refs[5 * n : 5 * n + 3 * adds]
    gate_out, up_out, down_out = refs[5 * n + 3 * adds :]
    wide, narrow = half
    x_at = pl.multiple_of(which_ref[0] * wide, LANES)
    a_at = pl.multiple_of(which_ref[0] * narrow, LANES)
    totals = [None, None, None]
    for i in range(n):
        x = xs[i][:, pl.ds(x_at, wide)]
        a = acts[i][:, pl.ds(a_at, narrow)]
        for k, (left, right) in enumerate(((x, dus[i]), (x, dws[i]), (a, dys[i]))):
            now = dot(left, right[...], 0, 0)
            totals[k] = now if totals[k] is None else totals[k] + now
    for k, out in enumerate((gate_out, up_out, down_out)):
        total = totals[k]
        for j in range(adds):
            total = total + more[3 * j + k][...].astype(f32)
        out[...] = total.astype(out.dtype)


def norm_back(up, hat, scale, gain):
    w = up * gain
    return scale * (w - hat * jnp.mean(w * hat, axis=-1, keepdims=True)), jnp.sum(up * hat, axis=0, keepdims=True)


def hidden_back_body(experts, a_ref, b_ref, c_ref, d_ref, g_ref, hidden_ref, gain_ref, gate_ref, misc_ref, o_ref, mixed_ref, *outs):
    dh_ref, dmixed_ref, og_ref, rg_ref, gg_ref = outs
    tokens = g_ref.shape[0]
    got = a_ref[...].astype(f32) + b_ref[...].astype(f32) + c_ref[...].astype(f32) + d_ref[...].astype(f32)
    extra = got[tokens:]
    rows = []
    for first in range(experts // EXTRA):
        at = 3 * first * tokens
        rows.append(extra[:, at : at + tokens] + extra[:, at + tokens : at + 2 * tokens])
    rows.append(jnp.zeros((LANES - experts, tokens), f32))
    dg = jnp.transpose(jnp.concatenate(rows, axis=0))
    gate = gate_ref[...]
    dl = gate * (dg - jnp.sum(gate * dg, axis=-1, keepdims=True))
    dz = dl.astype(bf16)
    dn = got[0:tokens] + dot(dz, misc_ref[...], 1, 1)
    h = hidden_ref[...]
    scale = scale_of(h)
    hat = h * scale
    gain = gain_ref[1:2]
    n2 = (hat * gain).astype(bf16)
    rg_ref[...] = dot(n2, dz, 0, 0)
    back, grad = norm_back(dn, hat, scale, gain)
    gg_ref[...] = jnp.broadcast_to(grad, gg_ref.shape)
    dh = g_ref[...].astype(f32) + back
    dh_ref[...] = dh
    da = dh.astype(bf16)
    dmixed_ref[...] = dot(da, o_ref[...]).astype(bf16)
    og_ref[...] = dot(da, mixed_ref[...], 0, 0).astype(bf16)


def attend_back_body(seqs, experts, x_ref, cos_ref, sin_ref, w_ref, gain_ref, n1_ref, q_ref, k_ref, v_ref, do_ref, dh_ref, rg_ref, gg_ref, dx_ref, wg_ref, dqkv_ref):
    length = x_ref.shape[0] // seqs
    cos = cos_ref[...]
    sin = sin_ref[...]
    keep = causal_mask(length)

    def back(u):
        return (u * cos - pltpu.roll(u, HEAD // 2, 1) * sin).astype(bf16)

    for b in range(seqs):
        rows = slice(b * length, (b + 1) * length)
        for c in range(KEY_VALUE_HEADS):
            cols = slice(c * HEAD, (c + 1) * HEAD)
            k = k_ref[rows, cols]
            v = v_ref[rows, cols]
            q = heads_of(q_ref, b, length, c)
            do = heads_of(do_ref, b, length, c)
            p = softmax_of(q, k, keep)
            dqkv_ref[rows, Q_COLS + KV_COLS + c * HEAD : Q_COLS + KV_COLS + (c + 1) * HEAD] = dot(
                p.astype(bf16), do, 0, 0
            ).astype(bf16)
            dp = dot(do, v, 1, 1)
            ds = (p * (dp - jnp.sum(p * dp, axis=-1, keepdims=True))).astype(bf16)
            dq = dot(ds, k) * SCALE
            for h in range(GROUP):
                at = (c * GROUP + h) * HEAD
                dqkv_ref[rows, at : at + HEAD] = back(dq[h * length : (h + 1) * length])
            dqkv_ref[rows, Q_COLS + c * HEAD : Q_COLS + (c + 1) * HEAD] = back(dot(ds, q, 0, 0) * SCALE)
    dqkv = dqkv_ref[...]
    wg_ref[:, 0:MISC] = dot(n1_ref[...], dqkv, 0, 0).astype(bf16)
    dn = dot(dqkv, w_ref[:, 0:MISC], 1, 1)
    x = x_ref[...].astype(f32)
    scale = scale_of(x)
    back_x, grad = norm_back(dn, x * scale, scale, gain_ref[0:1])
    dx_ref[...] = dh_ref[...] + back_x
    row = lax.broadcasted_iota(jnp.int32, (LANES, x.shape[1]), 0)
    gains = jnp.where(row == experts, grad, jnp.where(row == experts + 1, gg_ref[0:1], 0.0))
    wg_ref[:, MISC:] = (rg_ref[...] + jnp.transpose(gains)).astype(bf16)


def chip_ring(chips):
    if chips % 4 or chips < 8:
        return list(range(chips))
    high, low = 4, chips // 4
    order = [a * low for a in range(high)]
    for step, a in enumerate(reversed(range(high))):
        rest = list(range(1, low))
        order += [a * low + b for b in (rest if step % 2 == 0 else reversed(rest))]
    return order


class Ring:
    def __init__(self, devices):
        self.devices = devices
        self.chips = devices // 2
        self.half = self.chips // 2
        self.order = chip_ring(self.chips)
        n = self.chips
        self.up = [
            (2 * self.order[p] + lane, 2 * self.order[(p + 1) % n] + lane) for p in range(n) for lane in (0, 1)
        ]
        self.down = [(b, a) for a, b in self.up]
        self.swap = [(d, d ^ 1) for d in range(devices)]
        self.place = np.argsort(np.array(self.order)).astype(np.int32)
        self.offsets = [0] + [s * o for o in range(1, self.half) for s in (-1, 1)] + [self.half]

    def send_up(self, x):
        return lax.ppermute(x, "expert", self.up)

    def send_down(self, x):
        return lax.ppermute(x, "expert", self.down)

    def send_core(self, x):
        return lax.ppermute(x, "expert", self.swap)

    def device(self, offset, other):
        me = lax.axis_index("expert")
        at = (jnp.asarray(self.place)[me // 2] + offset) % self.chips
        return 2 * jnp.asarray(np.array(self.order, np.int32))[at] + lax.rem(me + other, 2)

    def gather(self, x, split=None):
        got = {0: [x]}
        up = down = x
        for s in range(1, self.half):
            up, down = self.send_up(up), self.send_down(down)
            got[-s], got[s] = [up], [down]
        if split is None:
            got[self.half] = [self.send_up(up)]
        else:
            got[self.half] = [self.send_up(up[:split]), self.send_down(down[split:])]
        return got

    def scatter(self, own, other, split):
        partner = {o: self.send_core(other[o]) for o in [self.half] + self.offsets[:-1][::-1]}

        def total(*terms):
            out = terms[0].astype(f32)
            for t in terms[1:]:
                out = out + t.astype(f32)
            return out.astype(bf16)

        h = self.half
        first = total(own[h], partner[h])
        up, down = self.send_up(first[:split]), self.send_down(first[split:])
        for s in range(h - 1, 0, -1):
            if s == h - 1:
                up = jnp.concatenate(
                    [total(own[s][:split], partner[s][:split], up), total(own[s][split:], partner[s][split:])]
                )
                down = jnp.concatenate(
                    [total(own[-s][:split], partner[-s][:split]), total(own[-s][split:], partner[-s][split:], down)]
                )
            else:
                up, down = total(own[s], partner[s], up), total(own[-s], partner[-s], down)
            up, down = self.send_up(up), self.send_down(down)
        return own[0], partner[0], up, down


def dp_pairs(shift):
    n = lax.axis_size("dp")
    return [(i, (i + shift) % n) for i in range(n)]


def from_dp(x, shift):
    return lax.ppermute(x, "dp", dp_pairs(shift))


def whole_from_dp(x):
    parts = lax.axis_size("dp")
    if parts != 2:
        return lax.all_gather(x, "dp", axis=0, tiled=True)
    other = from_dp(x, 1)
    low = lax.axis_index("dp") == 0
    return jnp.concatenate([jnp.where(low, x, other), jnp.where(low, other, x)], axis=0)


def on_device(
    inputs,
    cotangent,
    routes,
    attention_gain,
    query_weight,
    key_matrix,
    value_matrix,
    output_weight,
    mixture_gain,
    router_weight,
    gate_weight,
    up_weight,
    down_weight,
):
    seqs, _, length, _ = inputs.shape
    tokens = seqs * length
    topk = routes.shape[3]
    dp, experts = lax.axis_size("dp"), lax.axis_size("expert")
    assert gate_weight.shape[0] == 1 and experts % EXTRA == 0 and experts * 3 * tokens <= EXTRA * WIDTH * 2
    ring = Ring(experts)
    my_dp, me = lax.axis_index("dp"), lax.axis_index("expert")
    capacity = (5 * length * topk + 4 * experts - 1) // (4 * experts)
    slots = seqs * ((capacity + 7) // 8 * 8)
    x = inputs.reshape(tokens, WIDTH)
    g = cotangent.reshape(tokens, WIDTH)
    cos, sin = (jnp.asarray(t) for t in rope_tables(length))
    split = length

    rows = query_weight.shape[0]
    misc = jnp.concatenate(
        [
            router_weight,
            attention_gain[:, None],
            mixture_gain[:, None],
            jnp.zeros((rows, LANES - experts - 2), bf16),
        ],
        axis=1,
    )
    qkv_own = jnp.concatenate([query_weight, key_matrix, value_matrix, misc], axis=1)
    o_own = output_weight.T
    pieces_apart = dp == 2 and rows % 16 == 0
    if pieces_apart:
        pair = jnp.stack([qkv_own, from_dp(qkv_own, 1)])
        got = ring.gather(pair)
        qkv, where = [], []
        for o in ring.offsets:
            for other, piece in ((0, got[o][0]), (1, ring.send_core(got[o][0]))):
                qkv.append(piece)
                d = ring.device(o, other)
                where += [my_dp * experts + d, (1 - my_dp) * experts + d]
        qkv_where = jnp.stack(where).astype(jnp.int32)
        got = ring.gather(o_own)
        stack = jnp.stack([got[o][0] for o in ring.offsets])
        far = from_dp(stack, 1)
        o_full = [stack, ring.send_core(stack), far, ring.send_core(far)]
        o_where = jnp.stack(
            [
                y * experts + ring.device(o, other)
                for y in (my_dp, 1 - my_dp)
                for other in (0, 1)
                for o in ring.offsets
            ]
        ).astype(jnp.int32)
    else:
        both = lax.all_gather(jnp.concatenate([qkv_own, o_own], axis=1), ("dp", "expert"), axis=0, tiled=True)
        qkv, o_full = [both[None, :, : MISC + LANES]], [both[None, :, MISC + LANES :]]
        qkv_where = o_where = jnp.zeros((1,), jnp.int32)

    gate_full = whole_from_dp(gate_weight[0])
    up_full = whole_from_dp(up_weight[0])
    down_full = whole_from_dp(down_weight[0])

    g_all = ring.gather(g, split)
    g_far = {o: [ring.send_core(p) for p in g_all[o]] for o in ring.offsets}

    w_full, gains, n1, q, k, v, mixed = call(
        functools.partial(attend_body, seqs, experts, len(qkv)),
        [
            sds((WIDTH, MISC + LANES), bf16),
            sds((8, WIDTH), f32),
            sds((tokens, WIDTH), bf16),
            sds((tokens, Q_COLS), bf16),
            sds((tokens, KV_COLS), bf16),
            sds((tokens, KV_COLS), bf16),
            sds((tokens, Q_COLS), bf16),
        ],
        [smem()] + vmem(3 + len(qkv)),
        [qkv_where, x, cos, sin, *qkv],
        "attend",
        2 * tokens * WIDTH * MISC,
    )
    misc_full = w_full[:, MISC:]
    o_t, hidden, send, gate_values = call(
        functools.partial(project_body, experts, len(o_full)),
        [
            sds((WIDTH, Q_COLS), bf16),
            sds((tokens, WIDTH), f32),
            sds((tokens + EXTRA, WIDTH), bf16),
            sds((tokens, LANES), f32),
        ],
        [smem()] + vmem(5 + len(o_full)),
        [o_where, x, mixed, gains, misc_full, routes.reshape(tokens, topk), *o_full],
        "project",
        2 * tokens * WIDTH * Q_COLS,
    )

    n_all = ring.gather(send, split)
    n_far = {o: [ring.send_core(p) for p in n_all[o]] for o in ring.offsets}
    which = me.astype(jnp.int32)[None]
    out_own, out_far, dx_own, dx_far = {}, {}, {}, {}
    kept = [[], [], [], [], []]
    groups = [[0]] + [[-s, s] for s in range(1, ring.half)] + [[ring.half]]
    hidden_size = gate_full.shape[1]
    for group in groups:
        args, arrays = [], []
        for o in group:
            for n_side, g_side in ((n_all, g_all), (n_far, g_far)):
                described = []
                for pieces in (n_side[o], g_side[o]):
                    parts, start = [], 0
                    for p in pieces:
                        parts.append((len(args), start, p.shape[0], 0))
                        args.append(p)
                        start += p.shape[0]
                    described.append(parts)
                arrays.append(tuple(described))
        count = len(arrays)
        total = count * slots
        outs = call(
            functools.partial(expert_body, (arrays, len(args)), capacity, slots, tokens, seqs),
            [sds((tokens, WIDTH), bf16)] * count
            + [sds((tokens + EXTRA, WIDTH), bf16)] * count
            + [sds((total, WIDTH), bf16)] * 2
            + [sds((total, hidden_size), bf16)] * 3,
            [smem()] + vmem(len(args) + 3),
            [which, *args, gate_full, up_full, down_full],
            "experts",
            2 * total * WIDTH * hidden_size * 6,
            [pltpu.VMEM((total, WIDTH), bf16), pltpu.VMEM((total, LANES), f32)],
        )
        for i, o in enumerate(group):
            out_own[o], out_far[o] = outs[2 * i], outs[2 * i + 1]
            dx_own[o], dx_far[o] = outs[count + 2 * i], outs[count + 2 * i + 1]
        for k_, value in zip(kept, outs[2 * count :], strict=True):
            k_.append(value)
    dx_terms = ring.scatter(dx_own, dx_far, split)
    out_terms = ring.scatter(out_own, out_far, split)

    saved = [a for k_ in kept for a in k_]
    wide, narrow = WIDTH // dp, hidden_size // dp
    if wide % LANES == 0 and narrow % LANES == 0:

        def part(index, dtype, more):
            return call(
                functools.partial(weights_body, len(groups), (wide, narrow), len(more) // 3),
                [sds((wide, hidden_size), dtype)] * 2 + [sds((narrow, WIDTH), dtype)],
                [smem()] + vmem(len(saved) + len(more)),
                [index.astype(jnp.int32)[None], *saved, *more],
                "expert_weights",
                2 * experts * slots * wide * hidden_size * 3,
            )

        more = []
        for shift in range(1, dp):
            more += [from_dp(p, shift) for p in part(lax.rem(my_dp + shift, dp), bf16, [])]
        gate_grad, up_grad, down_grad = part(my_dp, f32, more)
    else:
        xs, dys, acts, dus, dws = (jnp.concatenate(k_) for k_ in kept)
        gate_grad, up_grad, down_grad = (
            lax.psum_scatter(dot(a, b, 0, 0).astype(bf16), "dp", scatter_dimension=0, tiled=True).astype(f32)
            for a, b in ((xs, dus), (xs, dws), (acts, dys))
        )

    dh, dmixed, o_part, router_part, gain_part = call(
        functools.partial(hidden_back_body, experts),
        [
            sds((tokens, WIDTH), f32),
            sds((tokens, Q_COLS), bf16),
            sds((WIDTH, Q_COLS), bf16),
            sds((WIDTH, LANES), f32),
            sds((8, WIDTH), f32),
        ],
        vmem(11),
        [*dx_terms, g, hidden, gains, gate_values, misc_full, o_t, mixed],
        "hidden_back",
        4 * tokens * WIDTH * Q_COLS,
    )
    input_grad, qkv_part, _ = call(
        functools.partial(attend_back_body, seqs, experts),
        [sds((tokens, WIDTH), f32), sds((WIDTH, MISC + LANES), bf16), sds((tokens, MISC), bf16)],
        vmem(13),
        [x, cos, sin, w_full, gains, n1, q, k, v, dmixed, dh, router_part, gain_part],
        "attend_back",
        4 * tokens * WIDTH * MISC,
    )

    def reduced(part):
        columns = part.shape[1]
        if dp != 2:
            return lax.psum_scatter(part, ("dp", "expert"), scatter_dimension=0, tiled=True).astype(f32)
        blocks = part.reshape(dp, ring.chips, 2, rows, columns)
        lane = lax.rem(me, 2)

        def of_lane(index):
            return lax.dynamic_index_in_dim(blocks, index, axis=2, keepdims=False)

        swapped = ring.send_core(of_lane(1 - lane))
        mine = of_lane(lane)

        def of_y(index):
            a = lax.dynamic_index_in_dim(mine, index, axis=0, keepdims=False).astype(f32)
            b = lax.dynamic_index_in_dim(swapped, index, axis=0, keepdims=False).astype(f32)
            return a + b

        far = from_dp(of_y(1 - my_dp).astype(bf16), 1)
        both = (of_y(my_dp) + far.astype(f32)).astype(bf16)

        def of_chip(offset):
            return lax.dynamic_index_in_dim(both, ring.device(offset, 0) // 2, axis=0, keepdims=False)

        up = ring.send_up(of_chip(ring.half))
        down = None
        for s in range(ring.half - 1, 0, -1):
            up = ring.send_up((up.astype(f32) + of_chip(s).astype(f32)).astype(bf16))
            term = of_chip(-s)
            down = ring.send_down(term if down is None else (down.astype(f32) + term.astype(f32)).astype(bf16))
        return up.astype(f32) + down.astype(f32) + of_chip(0).astype(f32)

    o_grad = reduced(o_part)
    qkv_grad = reduced(qkv_part)

    total = hidden
    for t in out_terms:
        total = total + t.astype(f32)
    outputs = total.astype(bf16).reshape(inputs.shape)
    return (
        outputs,
        input_grad.reshape(inputs.shape),
        qkv_grad[:, MISC + experts],
        qkv_grad[:, :Q_COLS],
        qkv_grad[:, Q_COLS : Q_COLS + KV_COLS],
        qkv_grad[:, Q_COLS + KV_COLS : MISC],
        o_grad.T,
        qkv_grad[:, MISC + experts + 1],
        qkv_grad[:, MISC : MISC + experts],
        gate_grad[None],
        up_grad[None],
        down_grad[None],
    )


def solution(mesh):
    both = ("dp", "expert")
    tokens = P(None, both, None, None)
    expert = P("expert", "dp", None)
    in_specs = (
        tokens,
        tokens,
        tokens,
        P(both),
        P(both, None),
        P(both, None),
        P(both, None),
        P(None, both),
        P(both),
        P(both, None),
        expert,
        expert,
        expert,
    )
    out_specs = (
        tokens,
        tokens,
        P(both),
        P(both, None),
        P(both, None),
        P(both, None),
        P(None, both),
        P(both),
        P(both, None),
        expert,
        expert,
        expert,
    )
    return jax.shard_map(on_device, mesh=mesh, in_specs=in_specs, out_specs=out_specs, check_vma=False)
```

```python
import functools
import math

import jax
import jax.numpy as jnp
import numpy as np
from jax import lax
from jax.experimental import pallas as pl
from jax.experimental.pallas import tpu as pltpu
from jax.sharding import PartitionSpec as P

WIDTH = 1536
QUERY_HEADS = 12
KEY_VALUE_HEADS = 2
HEAD = 128
GROUP = QUERY_HEADS // KEY_VALUE_HEADS
Q_COLS = QUERY_HEADS * HEAD
KV_COLS = KEY_VALUE_HEADS * HEAD
MISC = Q_COLS + 2 * KV_COLS
EXTRA = 16
LANES = 128
CHUNKS = 4
EPSILON = 1e-06
ROPE_BASE = 10000.0
MASKED = -1e30
SCALE = 1.0 / math.sqrt(HEAD)

f32 = jnp.float32
bf16 = jnp.bfloat16


def dot(a, b, ca=1, cb=0):
    return lax.dot_general(a, b, (((ca,), (cb,)), ((), ())), preferred_element_type=f32)


def vmem(n):
    return [pl.BlockSpec(memory_space=pltpu.VMEM)] * n


def smem():
    return pl.BlockSpec(memory_space=pltpu.SMEM)


def call(body, outs, ins, args, name, flops, scratch=()):
    return pl.pallas_call(
        body,
        out_shape=outs,
        in_specs=ins,
        out_specs=vmem(len(outs)),
        scratch_shapes=list(scratch),
        compiler_params=pltpu.CompilerParams(vmem_limit_bytes=60 * 1024 * 1024),
        cost_estimate=pl.CostEstimate(flops=1 << 20, bytes_accessed=1 << 20, transcendentals=0),
        name=name,
    )(*args)


def sds(shape, dtype):
    return jax.ShapeDtypeStruct(shape, dtype)


def rope_tables(length):
    half = HEAD // 2
    frequency = ROPE_BASE ** (-(np.arange(half, dtype=np.float64) * 2.0 / HEAD))
    angles = np.arange(length, dtype=np.float64)[:, None] * frequency[None, :]
    cos, sin = np.cos(angles), np.sin(angles)
    cosine = np.concatenate([cos, cos], axis=1).astype(np.float32)
    signed = np.concatenate([-sin, sin], axis=1).astype(np.float32)
    return cosine, signed


def place(where_ref, device, piece_refs, targets):
    at = 0
    for ref in piece_refs:
        blocks, rows, _ = ref.shape
        for j in range(blocks):
            start = pl.multiple_of(where_ref[device, at] * rows, 16 if rows % 16 == 0 else 8)
            for target, column in targets:
                target[pl.ds(start, rows), :] = ref[j, :, column : column + target.shape[1]]
            at += 1


def scale_of(z):
    return lax.rsqrt(jnp.mean(z * z, axis=-1, keepdims=True) + EPSILON)


def heads_of(ref, b, length, c):
    return jnp.concatenate(
        [ref[b * length : (b + 1) * length, h * HEAD : (h + 1) * HEAD] for h in range(c * GROUP, (c + 1) * GROUP)],
        axis=0,
    )


def causal_mask(length):
    row = lax.broadcasted_iota(jnp.int32, (length, length), 0)
    column = lax.broadcasted_iota(jnp.int32, (length, length), 1)
    return jnp.concatenate([row >= column] * GROUP, axis=0)


def softmax_of(q, k, keep):
    s = jnp.where(keep, dot(q, k, 1, 1) * SCALE, MASKED)
    e = jnp.exp(s - jnp.max(s, axis=-1, keepdims=True))
    return e / jnp.sum(e, axis=-1, keepdims=True)


def forward_body(seqs, experts, n_pieces, me_ref, where_ref, x_ref, cos_ref, sin_ref, routes_ref, *refs):
    pieces = refs[:n_pieces]
    w_ref, o_ref, misc_ref, gain_ref, n1_ref, q_ref, k_ref, v_ref, mixed_ref, hidden_ref, send_ref, gate_ref = refs[n_pieces:]
    length = x_ref.shape[0] // seqs
    place(where_ref, me_ref[0], pieces, ((w_ref, 0), (misc_ref, MISC), (o_ref, MISC + LANES)))
    gains = jnp.transpose(misc_ref[...].astype(f32))[experts : experts + 8]
    gain_ref[...] = gains
    x = x_ref[...].astype(f32)
    n1 = (x * scale_of(x) * gains[0:1]).astype(bf16)
    n1_ref[...] = n1
    cos = jnp.concatenate([cos_ref[...]] * seqs, axis=0)
    sin = jnp.concatenate([sin_ref[...]] * seqs, axis=0)

    def rotated(u):
        return (u * cos + pltpu.roll(u, HEAD // 2, 1) * sin).astype(bf16)

    kv = dot(n1, w_ref[:, Q_COLS:])
    v_ref[...] = kv[:, KV_COLS:].astype(bf16)
    for c in range(KEY_VALUE_HEADS):
        k_ref[:, c * HEAD : (c + 1) * HEAD] = rotated(kv[:, c * HEAD : (c + 1) * HEAD])
    keep = causal_mask(length)
    for c in range(KEY_VALUE_HEADS):
        cols = GROUP * HEAD
        q = dot(n1, w_ref[:, c * cols : (c + 1) * cols])
        for h in range(GROUP):
            at = c * cols + h * HEAD
            q_ref[:, at : at + HEAD] = rotated(q[:, h * HEAD : (h + 1) * HEAD])
        for b in range(seqs):
            rows = slice(b * length, (b + 1) * length)
            k = k_ref[rows, c * HEAD : (c + 1) * HEAD]
            v = v_ref[rows, c * HEAD : (c + 1) * HEAD]
            p = softmax_of(heads_of(q_ref, b, length, c), k, keep).astype(bf16)
            o = dot(p, v).astype(bf16)
            for h in range(GROUP):
                at = c * cols + h * HEAD
                mixed_ref[rows, at : at + HEAD] = o[h * length : (h + 1) * length]
    tokens = x_ref.shape[0]
    h = x + dot(mixed_ref[...], o_ref[...], 1, 1)
    hidden_ref[...] = h
    n2 = (h * scale_of(h) * gains[1:2]).astype(bf16)
    send_ref[0:tokens] = n2
    z = dot(n2, misc_ref[...])
    lane = lax.broadcasted_iota(jnp.int32, (tokens, LANES), 1)
    chosen = lane == routes_ref[:, 0:1]
    for j in range(1, routes_ref.shape[1]):
        chosen = chosen | (lane == routes_ref[:, j : j + 1])
    top = jnp.max(jnp.where(chosen, z, MASKED), axis=-1, keepdims=True)
    e = jnp.where(chosen, jnp.exp(jnp.where(chosen, z - top, 0.0)), 0.0)
    gate = e / jnp.sum(e, axis=-1, keepdims=True)
    gate_ref[...] = gate
    high = gate.astype(bf16).astype(f32)
    tables = [jnp.transpose(t) for t in (high, gate - high, chosen.astype(f32))]
    blank = jnp.zeros((EXTRA, tokens), f32)
    parts = []
    for first in range(0, experts, EXTRA):
        parts += [t[first : first + EXTRA] for t in tables]
    parts += [blank] * (WIDTH // tokens - len(parts))
    send_ref[tokens:] = jnp.concatenate(parts, axis=1).astype(bf16)


def expert_body(layout, capacity, slots, tokens, seqs, me_ref, *refs):
    arrays, n_in, parts_in = layout
    count = len(arrays)
    ins = refs[:n_in]
    if parts_in == 1:
        weights = [tuple(refs[n_in : n_in + 3])]
        outs = refs[n_in + 3 :]
    else:
        gate_ref, up_ref, down_ref, far_ref, far_down_ref = refs[n_in : n_in + 5]
        hidden = gate_ref.shape[1]
        weights = [
            (gate_ref, up_ref, down_ref),
            (far_ref.at[:, 0:hidden], far_ref.at[:, hidden : 2 * hidden], far_down_ref),
        ]
        outs = refs[n_in + 5 :]
    deep, narrow = weights[0][0].shape[0], weights[0][2].shape[0]
    if parts_in == 1:
        spans = [(slice(0, deep), slice(0, narrow))]
    else:
        spans = [
            (pl.ds(pl.multiple_of(p * deep, LANES), deep), pl.ds(pl.multiple_of(p * narrow, LANES), narrow))
            for p in (me_ref[1], 1 - me_ref[1])
        ]
    half = count // 2
    far_out, far_dx = outs[2 * half : 2 * half + 2]
    out_refs, dx_refs = [], []
    for j in range(half):
        out_refs += [outs[j], far_out.at[j]]
        dx_refs += [outs[half + j], far_dx.at[j]]
    xs_ref, dy_ref, act_ref, du_ref, dw_ref, gs_ref, gcol_ref, dact_ref, dx_ref = outs[2 * half + 2 :]
    length = tokens // seqs
    me = me_ref[2]
    row_in = lax.rem(me, EXTRA)
    row = lax.broadcasted_iota(jnp.int32, (EXTRA, tokens), 0)
    mine = row == row_in
    block = lax.div(me, EXTRA)

    def table(extra, k):
        t = jnp.zeros((EXTRA, tokens), f32)
        for b in range(WIDTH // (3 * tokens)):
            at = (3 * b + k) * tokens
            t = jnp.where(block == b, extra[:, at : at + tokens].astype(f32), t)
        return jnp.sum(jnp.where(mine, t, 0.0), axis=0, keepdims=True)

    def read(pieces, first, rows):
        got = []
        for index, start, size, offset in pieces:
            lo, hi = max(first, start), min(first + rows, start + size)
            if lo < hi:
                got.append(ins[index][offset + lo - start : offset + hi - start])
        return got[0] if len(got) == 1 else jnp.concatenate(got, axis=0)

    tri_a = lax.broadcasted_iota(jnp.int32, (length, length), 0)
    tri_b = lax.broadcasted_iota(jnp.int32, (length, length), 1)
    before = (tri_a < tri_b).astype(bf16)
    slot = lax.broadcasted_iota(jnp.int32, (slots, tokens), 0).astype(f32)
    gates, masks = [], []
    for n2_pieces, _ in arrays:
        extra = read(n2_pieces, tokens, EXTRA)
        gates.append(table(extra, 0) + table(extra, 1))
        masks.append(table(extra, 2))
    picks = []
    for i, (n2_pieces, g_pieces) in enumerate(arrays):
        at = []
        for b in range(seqs):
            m = masks[i][:, b * length : (b + 1) * length]
            earlier = dot(jnp.broadcast_to(m, (16, length)).astype(bf16), before)[0:1]
            keep = (m > 0.5) & (earlier < capacity)
            at.append(jnp.where(keep, earlier + b * (slots // seqs), -1.0))
        pick = (slot == jnp.concatenate(at, axis=1)).astype(f32)
        gcol_ref[i * slots : (i + 1) * slots, :] = jnp.broadcast_to(
            jnp.sum(pick * gates[i], axis=1, keepdims=True), (slots, LANES)
        )
        pick = pick.astype(bf16)
        picks.append(pick)
        rows = slice(i * slots, (i + 1) * slots)
        xs_ref[rows, :] = dot(pick, read(n2_pieces, 0, tokens)).astype(bf16)
        gs_ref[rows, :] = dot(pick, read(g_pieces, 0, tokens)).astype(bf16)
    u = w = y = None
    for (gate_part, up_part, _), (rows, _) in zip(weights, spans, strict=True):
        xs = xs_ref[:, rows]
        more_u, more_w = dot(xs, gate_part[...]), dot(xs, up_part[...])
        u, w = (more_u, more_w) if u is None else (u + more_u, w + more_w)
    s = 1.0 / (1.0 + jnp.exp(-u))
    act_ref[...] = (u * s * w).astype(bf16)
    for (_, _, down_part), (_, rows) in zip(weights, spans, strict=True):
        more = dot(act_ref[:, rows], down_part[...])
        y = more if y is None else y + more
    y = y.astype(bf16).astype(f32)
    gcol = gcol_ref[:, 0:1]
    gs = gs_ref[...].astype(f32)
    dy = (gcol * gs).astype(bf16)
    dy_ref[...] = dy
    dg = jnp.sum(gs * y, axis=1, keepdims=True)
    weighted = (gcol * y).astype(bf16)
    for (_, _, down_part), (_, rows) in zip(weights, spans, strict=True):
        dact_ref[:, rows] = dot(dy, down_part[...], 1, 1)
    dact = dact_ref[...]
    du = (dact * w * s * (1.0 + u * (1.0 - s))).astype(bf16)
    dw = (dact * (u * s)).astype(bf16)
    du_ref[...] = du
    dw_ref[...] = dw
    for (gate_part, up_part, _), (rows, _) in zip(weights, spans, strict=True):
        dx_ref[:, rows] = (dot(du, gate_part[...], 1, 1) + dot(dw, up_part[...], 1, 1)).astype(bf16)
    dx = dx_ref[...]
    for i in range(count):
        rows = slice(i * slots, (i + 1) * slots)
        out_refs[i][...] = dot(picks[i], weighted[rows], 0, 0).astype(bf16)
        dx_refs[i][0:tokens] = dot(picks[i], dx[rows], 0, 0).astype(bf16)
        back = jnp.sum(picks[i].astype(f32) * dg[rows], axis=0, keepdims=True)
        high = back.astype(bf16).astype(f32)
        blank = jnp.zeros((EXTRA, tokens), f32)
        parts = []
        for b in range(WIDTH // (3 * tokens)):
            here = mine & (block == b)
            parts += [jnp.where(here, high, 0.0), jnp.where(here, back - high, 0.0), blank]
        dx_refs[i][tokens:] = jnp.concatenate(parts, axis=1).astype(bf16)


def weights_body(n, half, shift, adds, me_ref, *refs):
    lists = [refs[k * n : (k + 1) * n] for k in range(5)]
    xs, dys, acts, dus, dws = lists
    more = refs[5 * n : 5 * n + adds]
    outs = refs[5 * n + adds :]
    wide, narrow = half
    index = lax.rem(me_ref[1] + shift, me_ref[3])
    x_at = pl.multiple_of(index * wide, LANES)
    a_at = pl.multiple_of(index * narrow, LANES)
    totals = [None, None, None]
    for i in range(n):
        x = xs[i][:, pl.ds(x_at, wide)]
        a = acts[i][:, pl.ds(a_at, narrow)]
        for k, (left, right) in enumerate(((x, dus[i]), (x, dws[i]), (a, dys[i]))):
            now = dot(left, right[...], 0, 0)
            totals[k] = now if totals[k] is None else totals[k] + now
    hidden = totals[0].shape[1]
    columns = (slice(0, hidden), slice(hidden, 2 * hidden), slice(None))
    chunks = outs if shift else more
    rows = (wide + narrow) // CHUNKS
    for k, c in enumerate(columns):
        base, size = (wide, narrow) if k == 2 else (0, wide)
        for j, ref in enumerate(chunks):
            first = (j % CHUNKS) * rows
            lo, hi = max(first, base), min(first + rows, base + size)
            if lo < hi and shift:
                ref[lo - first : hi - first, c] = totals[k][lo - base : hi - base].astype(bf16)
            elif lo < hi and j < CHUNKS:
                value = totals[k][lo - base : hi - base]
                for other in chunks[j::CHUNKS]:
                    value = value + other[lo - first : hi - first, c].astype(f32)
                outs[k][lo - base : hi - base] = value


def blocks_out(where_ref, device, whole_ref, outs):
    keep_ref, send_ref = outs
    sides, count, rows, _ = keep_ref.shape
    for lane, out in enumerate((keep_ref, send_ref)):
        for side in range(sides):
            for k in range(count):
                at = where_ref[device, (2 * k + lane) * sides + side]
                out[side, k] = whole_ref[pl.ds(pl.multiple_of(at * rows, 16), rows), :]


def norm_back(up, hat, scale, gain):
    w = up * gain
    return scale * (w - hat * jnp.mean(w * hat, axis=-1, keepdims=True)), jnp.sum(up * hat, axis=0, keepdims=True)


def hidden_back_body(experts, apart, me_ref, where_ref, a_ref, b_ref, c_ref, d_ref, g_ref, hidden_ref, gain_ref, gate_ref, misc_ref, o_ref, mixed_ref, *outs):
    dh_ref, dmixed_ref, rg_ref, gg_ref, og_ref = outs[:4] + outs[-1:]
    tokens = g_ref.shape[0]
    got = a_ref[...].astype(f32) + b_ref[...].astype(f32) + c_ref[...].astype(f32) + d_ref[...].astype(f32)
    extra = got[tokens:]
    rows = []
    for first in range(experts // EXTRA):
        at = 3 * first * tokens
        rows.append(extra[:, at : at + tokens] + extra[:, at + tokens : at + 2 * tokens])
    rows.append(jnp.zeros((LANES - experts, tokens), f32))
    dg = jnp.transpose(jnp.concatenate(rows, axis=0))
    gate = gate_ref[...]
    dl = gate * (dg - jnp.sum(gate * dg, axis=-1, keepdims=True))
    dz = dl.astype(bf16)
    dn = got[0:tokens] + dot(dz, misc_ref[...], 1, 1)
    h = hidden_ref[...]
    scale = scale_of(h)
    hat = h * scale
    gain = gain_ref[1:2]
    n2 = (hat * gain).astype(bf16)
    rg_ref[...] = dot(n2, dz, 0, 0)
    back, grad = norm_back(dn, hat, scale, gain)
    gg_ref[...] = jnp.broadcast_to(grad, gg_ref.shape)
    dh = g_ref[...].astype(f32) + back
    dh_ref[...] = dh
    da = dh.astype(bf16)
    dmixed_ref[...] = dot(da, o_ref[...]).astype(bf16)
    og_ref[...] = dot(da, mixed_ref[...], 0, 0).astype(bf16)
    if apart:
        blocks_out(where_ref, me_ref[0], og_ref, outs[4:6])


def attend_back_body(seqs, experts, apart, me_ref, where_ref, x_ref, cos_ref, sin_ref, w_ref, gain_ref, n1_ref, q_ref, k_ref, v_ref, do_ref, dh_ref, rg_ref, gg_ref, dx_ref, *outs):
    wg_ref, dqkv_ref = outs[-2:]
    length = x_ref.shape[0] // seqs
    cos = cos_ref[...]
    sin = sin_ref[...]
    keep = causal_mask(length)

    def back(u):
        return (u * cos - pltpu.roll(u, HEAD // 2, 1) * sin).astype(bf16)

    for b in range(seqs):
        rows = slice(b * length, (b + 1) * length)
        for c in range(KEY_VALUE_HEADS):
            cols = slice(c * HEAD, (c + 1) * HEAD)
            k = k_ref[rows, cols]
            v = v_ref[rows, cols]
            q = heads_of(q_ref, b, length, c)
            do = heads_of(do_ref, b, length, c)
            p = softmax_of(q, k, keep)
            dqkv_ref[rows, Q_COLS + KV_COLS + c * HEAD : Q_COLS + KV_COLS + (c + 1) * HEAD] = dot(
                p.astype(bf16), do, 0, 0
            ).astype(bf16)
            dp = dot(do, v, 1, 1)
            ds = (p * (dp - jnp.sum(p * dp, axis=-1, keepdims=True))).astype(bf16)
            dq = dot(ds, k) * SCALE
            for h in range(GROUP):
                at = (c * GROUP + h) * HEAD
                dqkv_ref[rows, at : at + HEAD] = back(dq[h * length : (h + 1) * length])
            dqkv_ref[rows, Q_COLS + c * HEAD : Q_COLS + (c + 1) * HEAD] = back(dot(ds, q, 0, 0) * SCALE)
    dqkv = dqkv_ref[...]
    wg_ref[:, 0:MISC] = dot(n1_ref[...], dqkv, 0, 0).astype(bf16)
    dn = dot(dqkv, w_ref[...], 1, 1)
    x = x_ref[...].astype(f32)
    scale = scale_of(x)
    back_x, grad = norm_back(dn, x * scale, scale, gain_ref[0:1])
    dx_ref[...] = dh_ref[...] + back_x
    row = lax.broadcasted_iota(jnp.int32, (LANES, x.shape[1]), 0)
    gains = jnp.where(row == experts, grad, jnp.where(row == experts + 1, gg_ref[0:1], 0.0))
    wg_ref[:, MISC:] = (rg_ref[...] + jnp.transpose(gains)).astype(bf16)
    if apart:
        blocks_out(where_ref, me_ref[0], wg_ref, outs[:2])


def chip_ring(chips):
    if chips % 4 or chips < 8:
        return list(range(chips))
    high, low = 4, chips // 4
    order = [a * low for a in range(high)]
    for step, a in enumerate(reversed(range(high))):
        rest = list(range(1, low))
        order += [a * low + b for b in (rest if step % 2 == 0 else reversed(rest))]
    return order


class Ring:
    def __init__(self, devices):
        self.devices = devices
        self.chips = devices // 2
        self.half = self.chips // 2
        self.order = chip_ring(self.chips)
        n = self.chips
        self.up = [
            (2 * self.order[p] + lane, 2 * self.order[(p + 1) % n] + lane) for p in range(n) for lane in (0, 1)
        ]
        self.down = [(b, a) for a, b in self.up]
        self.swap = [(d, d ^ 1) for d in range(devices)]
        self.place = np.argsort(np.array(self.order)).astype(np.int32)
        self.offsets = [0] + [s * o for o in range(1, self.half) for s in (-1, 1)] + [self.half]

    def send_up(self, x):
        return lax.ppermute(x, "expert", self.up)

    def send_down(self, x):
        return lax.ppermute(x, "expert", self.down)

    def send_core(self, x):
        return lax.ppermute(x, "expert", self.swap)

    def table(self, dp):
        rows = []
        for y in range(dp):
            for e in range(self.devices):
                row = []
                for o in self.offsets:
                    chip = self.order[(int(self.place[e // 2]) + o) % self.chips]
                    for lane in (e % 2, 1 - e % 2):
                        row += [y * self.devices + 2 * chip + lane, (1 - y) * self.devices + 2 * chip + lane]
                rows.append(row)
        return np.array(rows, np.int32)

    def gather(self, x, split=None):
        return Gather(self, x, split)

    def scatter(self, own, far, split):
        return Scatter(self, own, far, split)


def after(x, *events):
    return lax.optimization_barrier((x, events))[0] if events else x


def total(*terms):
    out = terms[0].astype(f32)
    for t in terms[1:]:
        out = out + t.astype(f32)
    return out.astype(bf16)


class Gather:
    def __init__(self, ring, x, split):
        self.ring, self.split = ring, split
        self.got, self.far = {0: [x]}, {}
        self.hops = 0

    def hop(self, *events):
        ring, s = self.ring, self.hops
        self.hops += 1
        up, down = after((self.got[-s][0], self.got[s][0]), *events)
        if self.hops < ring.half:
            self.got[-self.hops], self.got[self.hops] = [ring.send_up(up)], [ring.send_down(down)]
        elif self.split is None:
            self.got[ring.half] = [ring.send_up(up)]
        else:
            self.got[ring.half] = [ring.send_up(up[: self.split]), ring.send_down(down[self.split :])]

    def swap(self, *offsets):
        for o in offsets:
            if o not in self.far:
                self.far[o] = [self.ring.send_core(p) for p in self.got[o]]


def fence(*things):
    rings = [t for t in things if isinstance(t, Gather)]
    arrays = [t for t in things if not isinstance(t, Gather)]
    held, arrays = lax.optimization_barrier(([(r.got, r.far) for r in rings], arrays))
    for r, (got, far) in zip(rings, held, strict=True):
        r.got, r.far = got, far
    return arrays


class Scatter:
    def __init__(self, ring, own, far, split):
        self.ring, self.own, self.far, self.split = ring, own, far, split
        self.partner, self.left = {}, ring.half

    def swap(self, offsets, *events):
        got = self.ring.send_core(after(self.far[offsets[0]], *events))
        for i, o in enumerate(offsets):
            self.partner[o] = got[i]

    def hop(self, *events):
        ring, own, partner, split, s = self.ring, self.own, self.partner, self.split, self.left
        self.left -= 1
        if s == ring.half:
            first = total(own[s], partner[s])
            up, down = first[:split], first[split:]
        elif s == ring.half - 1:
            more = own[s].shape[0] - split
            up = total(own[s], partner[s], jnp.pad(self.up, ((0, more), (0, 0))))
            down = total(own[-s], partner[-s], jnp.pad(self.down, ((split, 0), (0, 0))))
        else:
            up, down = total(own[s], partner[s], self.up), total(own[-s], partner[-s], self.down)
        self.sent = up, down = after((up, down), *events)
        self.up, self.down = ring.send_up(up), ring.send_down(down)
        return self.up, self.down

    def step(self, *events):
        there = self.hop(*events)
        self.swap([-self.left, self.left] if self.left else [0], *self.sent)
        return there

    def terms(self):
        return self.own[0], self.partner[0], self.up, self.down


def dp_pairs(shift):
    n = lax.axis_size("dp")
    return [(i, (i + shift) % n) for i in range(n)]


def from_dp(x, shift):
    return lax.ppermute(x, "dp", dp_pairs(shift))


def on_device(
    inputs,
    cotangent,
    routes,
    attention_gain,
    query_weight,
    key_matrix,
    value_matrix,
    output_weight,
    mixture_gain,
    router_weight,
    gate_weight,
    up_weight,
    down_weight,
):
    seqs, _, length, _ = inputs.shape
    tokens = seqs * length
    topk = routes.shape[3]
    dp, experts = lax.axis_size("dp"), lax.axis_size("expert")
    assert gate_weight.shape[0] == 1 and experts % EXTRA == 0 and experts * 3 * tokens <= EXTRA * WIDTH * 2
    ring = Ring(experts)
    my_dp, me = lax.axis_index("dp"), lax.axis_index("expert")
    capacity = (5 * length * topk + 4 * experts - 1) // (4 * experts)
    slots = seqs * ((capacity + 7) // 8 * 8)
    x = inputs.reshape(tokens, WIDTH)
    g = cotangent.reshape(tokens, WIDTH)
    cos, sin = (jnp.asarray(t) for t in rope_tables(length))
    split = length
    where_i = jnp.stack([my_dp * experts + me, my_dp, me, jnp.full_like(me, dp)]).astype(jnp.int32)

    rows = query_weight.shape[0]
    misc = jnp.concatenate(
        [
            router_weight,
            attention_gain[:, None],
            mixture_gain[:, None],
            jnp.zeros((rows, LANES - experts - 2), bf16),
        ],
        axis=1,
    )
    dense_own = jnp.concatenate([query_weight, key_matrix, value_matrix, misc, output_weight.T], axis=1)
    g_ring = ring.gather(g, split)
    g_ring.hop()
    apart = dp == 2 and rows % 16 == 0
    if apart:
        table = jnp.asarray(ring.table(dp))
        far = from_dp(dense_own, 1)
        d_ring = ring.gather(jnp.stack([dense_own, far]), 1)
        d_ring.hop()
        expert_start = (far,)
    else:
        table = jnp.zeros((dp * experts, 1), jnp.int32)
        both = lax.all_gather(dense_own, ("dp", "expert"), axis=0, tiled=True)
        dense = [both[None]]
        expert_start = (both,)

    hidden_size = gate_weight.shape[2]
    wide, narrow = WIDTH // dp, hidden_size // dp
    in_parts = dp == 2 and wide % LANES == 0 and narrow % LANES == 0
    if in_parts:
        flat = [jnp.concatenate([gate_weight[0], up_weight[0]], axis=1)]
        halves = [from_dp(after(flat[0], *expert_start), 1)]
        halves.append(from_dp(after(down_weight[0], *halves), 1))
        expert_weights = [gate_weight[0], up_weight[0], down_weight[0], *halves]
    else:
        expert_weights = [
            lax.all_gather(after(w[0], *expert_start), "dp", axis=0, tiled=True)
            for w in (gate_weight, up_weight, down_weight)
        ]
        flat, halves = [], []

    if apart:
        d_ring.hop(g_ring.got[-1], g_ring.got[1], *flat)
        while d_ring.hops < ring.half:
            d_ring.hop(*(halves[:1] if d_ring.hops == ring.half - 1 else ()))
        d_ring.swap(*ring.offsets)
        fence(d_ring, g_ring)
        dense = []
        for o in ring.offsets:
            dense += d_ring.got[o] + d_ring.far[o]
    g_ring.hop()

    w_full, o_t, misc_full, gains, n1, q, k, v, mixed, hidden, send, gate_values = call(
        functools.partial(forward_body, seqs, experts, len(dense)),
        [
            sds((WIDTH, MISC), bf16),
            sds((WIDTH, Q_COLS), bf16),
            sds((WIDTH, LANES), bf16),
            sds((8, WIDTH), f32),
            sds((tokens, WIDTH), bf16),
            sds((tokens, Q_COLS), bf16),
            sds((tokens, KV_COLS), bf16),
            sds((tokens, KV_COLS), bf16),
            sds((tokens, Q_COLS), bf16),
            sds((tokens, WIDTH), f32),
            sds((tokens + EXTRA, WIDTH), bf16),
            sds((tokens, LANES), f32),
        ],
        [smem(), smem()] + vmem(4 + len(dense)),
        [where_i, table, x, cos, sin, routes.reshape(tokens, topk), *dense],
        "forward",
        2 * tokens * WIDTH * (MISC + Q_COLS),
    )

    n_ring = ring.gather(send, split)
    out_own, out_far, dx_own, dx_far = {}, {}, {}, {}
    kept = {}
    groups = [[0]] + [[-s, s] for s in range(1, ring.half)] + [[ring.half]]

    def far_of(group):
        return ring.send_core(jnp.concatenate([p for o in group for r in (n_ring, g_ring) for p in r.got[o]]))

    def experts_on(group, far, *events):
        args, arrays, offset = [far], [], 0
        for o in group:
            own, other = [], []
            for pieces in (n_ring.got[o], g_ring.got[o]):
                start, first = 0, len(args)
                own.append([])
                other.append([])
                for j, p in enumerate(pieces):
                    args.append(p)
                    own[-1].append((first + j, start, p.shape[0], 0))
                    other[-1].append((0, start, p.shape[0], offset))
                    start += p.shape[0]
                    offset += p.shape[0]
            arrays += [tuple(own), tuple(other)]
        count = len(arrays)
        rows_ = count * slots
        outs = call(
            functools.partial(expert_body, (arrays, len(args), 2 if in_parts else 1), capacity, slots, tokens, seqs),
            [sds((tokens, WIDTH), bf16)] * len(group)
            + [sds((tokens + EXTRA, WIDTH), bf16)] * len(group)
            + [sds((len(group), tokens, WIDTH), bf16), sds((len(group), tokens + EXTRA, WIDTH), bf16)]
            + [sds((rows_, WIDTH), bf16)] * 2
            + [sds((rows_, hidden_size), bf16)] * 3,
            [smem()] + vmem(len(args) + len(expert_weights)),
            [after(where_i, *events), *args, *expert_weights],
            "experts",
            2 * rows_ * WIDTH * hidden_size * 6,
            [
                pltpu.VMEM((rows_, WIDTH), bf16),
                pltpu.VMEM((rows_, LANES), f32),
                pltpu.VMEM((rows_, hidden_size), f32),
                pltpu.VMEM((rows_, WIDTH), bf16),
            ],
        )
        n = len(group)
        for i, o in enumerate(group):
            out_own[o], dx_own[o] = outs[i], outs[n + i]
        out_far[group[0]], dx_far[group[0]] = outs[2 * n : 2 * n + 2]
        kept[group[0]] = outs[2 * n + 2 :]
        return kept[group[0]]

    fence(g_ring, n_ring, expert_weights[-1])
    far = []
    for hop in range(1, ring.half + 1):
        n_ring.hop()
        if g_ring.hops < ring.half:
            g_ring.hop()
        near, far = far, far_of(groups[hop - 1])
        if hop > 1:
            group = groups[hop - 2]
            far, kept[group[0]] = fence(n_ring, g_ring, far, experts_on(group, near))
        else:
            (far,) = fence(n_ring, g_ring, far)
    (last,) = fence(n_ring, g_ring, far_of(groups[-1]))
    experts_on(groups[-1], last)
    dx_ring = ring.scatter(dx_own, dx_far, split)
    dx_ring.swap(groups[-1])
    there = dx_ring.hop()
    experts_on(groups[-2], far, *dx_ring.sent)
    dx_ring.swap(groups[-2], *there)
    dx_ring.hop()
    dx_ring.swap(groups[-3], *dx_ring.sent)
    kept = [[kept[group[0]][i] for group in groups] for i in range(5)]

    saved = [a for k_ in kept for a in k_]
    if wide % LANES == 0 and narrow % LANES == 0:

        def part(shift, outs, more, *events):
            return call(
                functools.partial(weights_body, len(groups), (wide, narrow), shift, len(more)),
                outs,
                [smem()] + vmem(len(saved) + len(more)),
                [after(where_i, *events), *saved, *more],
                "expert_weights",
                2 * experts * slots * wide * hidden_size * 3,
            )

        more = []
        for shift in range(1, dp):
            parts = part(shift, [sds(((wide + narrow) // CHUNKS, WIDTH), bf16)] * CHUNKS, [], *dx_ring.sent, *more)
            for p in parts:
                more.append(from_dp(after(p, *more[-1:]), shift))
        weights_sent = (parts[0],)
    else:
        xs, dys, acts, dus, dws = (jnp.concatenate(k_) for k_ in kept)
        expert_grads = tuple(
            lax.psum_scatter(dot(a, b, 0, 0).astype(bf16), "dp", scatter_dimension=0, tiled=True).astype(f32)
            for a, b in ((xs, dus), (xs, dws), (acts, dys))
        )
        weights_sent, more = (), []
    dx_ring.step(*weights_sent)
    while dx_ring.left:
        dx_ring.step(*more[:1])
    dx_terms = dx_ring.terms()
    out_ring = ring.scatter(out_own, out_far, split)
    out_ring.swap(groups[-1], *dx_ring.sent)
    out_ring.step(*dx_terms[2:], *more[1:2])

    def block_outs(columns):
        return [sds((dp, ring.chips, rows, columns), bf16)] * 2

    dh, dmixed, router_part, gain_part, *o_part = call(
        functools.partial(hidden_back_body, experts, apart),
        [sds((tokens, WIDTH), f32), sds((tokens, Q_COLS), bf16), sds((WIDTH, LANES), f32), sds((8, WIDTH), f32)]
        + (block_outs(Q_COLS) if apart else [sds((WIDTH, Q_COLS), bf16)]),
        [smem(), smem()] + vmem(11),
        [after(where_i, *out_ring.sent), table, *dx_terms, g, hidden, gains, gate_values, misc_full, o_t, mixed],
        "hidden_back",
        4 * tokens * WIDTH * Q_COLS,
        [pltpu.VMEM((WIDTH, Q_COLS), bf16)] if apart else [],
    )
    out_ring.step(dh, *more[2:3])
    o_got = [ring.send_core(after(o_part[1], *out_ring.sent))] if apart else []
    input_grad, *qkv_part = call(
        functools.partial(attend_back_body, seqs, experts, apart),
        [sds((tokens, WIDTH), f32)]
        + (block_outs(MISC + LANES) if apart else [sds((WIDTH, MISC + LANES), bf16)]),
        [smem(), smem()] + vmem(13),
        [after(where_i, *out_ring.sent), table, x, cos, sin, w_full, gains, n1, q, k, v, dmixed, dh, router_part, gain_part],
        "attend_back",
        4 * tokens * WIDTH * MISC,
        ([pltpu.VMEM((WIDTH, MISC + LANES), bf16)] if apart else []) + [pltpu.VMEM((tokens, MISC), bf16)],
    )

    out_ring.step(input_grad, *more, *o_got)
    if wide % LANES == 0 and narrow % LANES == 0:
        expert_grads = part(
            0, [sds((wide, hidden_size), f32)] * 2 + [sds((narrow, WIDTH), f32)], more, *out_ring.sent
        )
    gate_grad, up_grad, down_grad = expert_grads

    def over_y(keep, got, *events):
        far = from_dp(after(total(keep[1], got[1]), *events), 1)
        return total(keep[0], got[0], far)

    class Blocks:
        def __init__(self, both):
            self.term = {o: both[k_] for k_, o in enumerate(ring.offsets)}
            self.up, self.down, self.left = None, None, ring.half

        def hop(self, *events):
            s = self.left
            self.left -= 1
            up = self.term[s] if self.up is None else total(self.up, self.term[s])
            if s == ring.half:
                self.up = ring.send_up(after(up, *events))
                return (self.up,)
            down = self.term[-s] if self.down is None else total(self.down, self.term[-s])
            up, down = after((up, down), *events)
            self.up, self.down = ring.send_up(up), ring.send_down(down)
            return self.up, self.down

        def result(self):
            while self.left:
                self.hop()
            return self.up.astype(f32) + self.down.astype(f32) + self.term[0].astype(f32)

    if apart:
        qkv_got = ring.send_core(after(qkv_part[1], *out_ring.sent))
        o_sum = over_y(o_part[0], *o_got, *out_ring.sent)
        while out_ring.left:
            there = out_ring.step(gate_grad, o_sum, qkv_got)
        qkv_sum = over_y(qkv_part[0], qkv_got, *out_ring.sent)
        o_blocks, qkv_blocks = Blocks(o_sum), Blocks(qkv_sum)
        there += o_blocks.hop(*out_ring.sent)
        qkv_blocks.hop(*there)
        o_grad, qkv_grad = o_blocks.result(), qkv_blocks.result()
    else:
        while out_ring.left:
            out_ring.step()
        o_grad, qkv_grad = (
            lax.psum_scatter(p[0], ("dp", "expert"), scatter_dimension=0, tiled=True).astype(f32)
            for p in (o_part, qkv_part)
        )

    outputs = total(hidden, *out_ring.terms()).reshape(inputs.shape)
    return (
        outputs,
        input_grad.reshape(inputs.shape),
        qkv_grad[:, MISC + experts],
        qkv_grad[:, :Q_COLS],
        qkv_grad[:, Q_COLS : Q_COLS + KV_COLS],
        qkv_grad[:, Q_COLS + KV_COLS : MISC],
        o_grad.T,
        qkv_grad[:, MISC + experts + 1],
        qkv_grad[:, MISC : MISC + experts],
        gate_grad[None],
        up_grad[None],
        down_grad[None],
    )


def solution(mesh):
    both = ("dp", "expert")
    tokens = P(None, both, None, None)
    expert = P("expert", "dp", None)
    in_specs = (
        tokens,
        tokens,
        tokens,
        P(both),
        P(both, None),
        P(both, None),
        P(both, None),
        P(None, both),
        P(both),
        P(both, None),
        expert,
        expert,
        expert,
    )
    out_specs = (
        tokens,
        tokens,
        P(both),
        P(both, None),
        P(both, None),
        P(both, None),
        P(None, both),
        P(both),
        P(both, None),
        expert,
        expert,
        expert,
    )
    return jax.shard_map(on_device, mesh=mesh, in_specs=in_specs, out_specs=out_specs, check_vma=False)
```

```python
import functools
import math

import jax
import jax.numpy as jnp
import numpy as np
from jax import lax
from jax.experimental import pallas as pl
from jax.experimental.pallas import tpu as pltpu
from jax.sharding import PartitionSpec as P

WIDTH = 1536
QUERY_HEADS = 12
KEY_VALUE_HEADS = 2
HEAD = 128
GROUP = QUERY_HEADS // KEY_VALUE_HEADS
Q_COLS = QUERY_HEADS * HEAD
KV_COLS = KEY_VALUE_HEADS * HEAD
MISC = Q_COLS + 2 * KV_COLS
EXTRA = 16
LANES = 128
CHUNKS = 4
EPSILON = 1e-06
ROPE_BASE = 10000.0
MASKED = -1e30
SCALE = 1.0 / math.sqrt(HEAD)

f32 = jnp.float32
bf16 = jnp.bfloat16


def dot(a, b, ca=1, cb=0):
    return lax.dot_general(a, b, (((ca,), (cb,)), ((), ())), preferred_element_type=f32)


def vmem(n):
    return [pl.BlockSpec(memory_space=pltpu.VMEM)] * n


def smem():
    return pl.BlockSpec(memory_space=pltpu.SMEM)


def call(body, outs, ins, args, name, vmem_mb, scratch=()):
    return pl.pallas_call(
        body,
        out_shape=outs,
        in_specs=ins,
        out_specs=vmem(len(outs)),
        scratch_shapes=list(scratch),
        compiler_params=pltpu.CompilerParams(vmem_limit_bytes=vmem_mb * 1024 * 1024),
        cost_estimate=pl.CostEstimate(flops=1 << 20, bytes_accessed=1 << 20, transcendentals=0),
        name=name,
    )(*args)


def sds(shape, dtype):
    return jax.ShapeDtypeStruct(shape, dtype)


def rope_tables(length):
    half = HEAD // 2
    frequency = ROPE_BASE ** (-(np.arange(half, dtype=np.float64) * 2.0 / HEAD))
    angles = np.arange(length, dtype=np.float64)[:, None] * frequency[None, :]
    cos, sin = np.cos(angles), np.sin(angles)
    cosine = np.concatenate([cos, cos], axis=1).astype(np.float32)
    signed = np.concatenate([-sin, sin], axis=1).astype(np.float32)
    return cosine, signed


def place(where_ref, device, piece_refs, targets):
    at = 0
    for ref in piece_refs:
        blocks, rows, _ = ref.shape
        for j in range(blocks):
            start = pl.multiple_of(where_ref[device, at] * rows, 16 if rows % 16 == 0 else 8)
            for target, column in targets:
                target[pl.ds(start, rows), :] = ref[j, :, column : column + target.shape[1]]
            at += 1


def scale_of(z):
    return lax.rsqrt(jnp.mean(z * z, axis=-1, keepdims=True) + EPSILON)


def heads_of(ref, b, length, c):
    return jnp.concatenate(
        [ref[b * length : (b + 1) * length, h * HEAD : (h + 1) * HEAD] for h in range(c * GROUP, (c + 1) * GROUP)],
        axis=0,
    )


def causal_mask(length):
    row = lax.broadcasted_iota(jnp.int32, (length, length), 0)
    column = lax.broadcasted_iota(jnp.int32, (length, length), 1)
    return jnp.concatenate([row >= column] * GROUP, axis=0)


def softmax_of(q, k, keep):
    s = jnp.where(keep, dot(q, k, 1, 1) * SCALE, MASKED)
    e = jnp.exp(s - jnp.max(s, axis=-1, keepdims=True))
    return e / jnp.sum(e, axis=-1, keepdims=True)


def forward_body(seqs, experts, n_pieces, me_ref, where_ref, x_ref, cos_ref, sin_ref, routes_ref, *refs):
    pieces = refs[:n_pieces]
    w_ref, o_ref, misc_ref, gain_ref, n1_ref, q_ref, k_ref, v_ref, mixed_ref, hidden_ref, send_ref, gate_ref = refs[n_pieces:]
    length = x_ref.shape[0] // seqs
    place(where_ref, me_ref[0], pieces, ((w_ref, 0), (misc_ref, MISC), (o_ref, MISC + LANES)))
    gains = jnp.transpose(misc_ref[...].astype(f32))[experts : experts + 8]
    gain_ref[...] = gains
    x = x_ref[...].astype(f32)
    n1 = (x * scale_of(x) * gains[0:1]).astype(bf16)
    n1_ref[...] = n1
    cos = jnp.concatenate([cos_ref[...]] * seqs, axis=0)
    sin = jnp.concatenate([sin_ref[...]] * seqs, axis=0)

    def rotated(u):
        return (u * cos + pltpu.roll(u, HEAD // 2, 1) * sin).astype(bf16)

    kv = dot(n1, w_ref[:, Q_COLS:])
    v_ref[...] = kv[:, KV_COLS:].astype(bf16)
    for c in range(KEY_VALUE_HEADS):
        k_ref[:, c * HEAD : (c + 1) * HEAD] = rotated(kv[:, c * HEAD : (c + 1) * HEAD])
    keep = causal_mask(length)
    for c in range(KEY_VALUE_HEADS):
        cols = GROUP * HEAD
        q = dot(n1, w_ref[:, c * cols : (c + 1) * cols])
        for h in range(GROUP):
            at = c * cols + h * HEAD
            q_ref[:, at : at + HEAD] = rotated(q[:, h * HEAD : (h + 1) * HEAD])
        for b in range(seqs):
            rows = slice(b * length, (b + 1) * length)
            k = k_ref[rows, c * HEAD : (c + 1) * HEAD]
            v = v_ref[rows, c * HEAD : (c + 1) * HEAD]
            p = softmax_of(heads_of(q_ref, b, length, c), k, keep).astype(bf16)
            o = dot(p, v).astype(bf16)
            for h in range(GROUP):
                at = c * cols + h * HEAD
                mixed_ref[rows, at : at + HEAD] = o[h * length : (h + 1) * length]
    tokens = x_ref.shape[0]
    h = x + dot(mixed_ref[...], o_ref[...], 1, 1)
    hidden_ref[...] = h
    n2 = (h * scale_of(h) * gains[1:2]).astype(bf16)
    send_ref[0:tokens] = n2
    z = dot(n2, misc_ref[...])
    lane = lax.broadcasted_iota(jnp.int32, (tokens, LANES), 1)
    chosen = lane == routes_ref[:, 0:1]
    for j in range(1, routes_ref.shape[1]):
        chosen = chosen | (lane == routes_ref[:, j : j + 1])
    top = jnp.max(jnp.where(chosen, z, MASKED), axis=-1, keepdims=True)
    e = jnp.where(chosen, jnp.exp(jnp.where(chosen, z - top, 0.0)), 0.0)
    gate = e / jnp.sum(e, axis=-1, keepdims=True)
    gate_ref[...] = gate
    high = gate.astype(bf16).astype(f32)
    tables = [jnp.transpose(t) for t in (high, gate - high, chosen.astype(f32))]
    blank = jnp.zeros((EXTRA, tokens), f32)
    parts = []
    for first in range(0, experts, EXTRA):
        parts += [t[first : first + EXTRA] for t in tables]
    parts += [blank] * (WIDTH // tokens - len(parts))
    send_ref[tokens:] = jnp.concatenate(parts, axis=1).astype(bf16)


def expert_body(layout, capacity, slots, tokens, seqs, me_ref, *refs):
    arrays, n_in, parts_in = layout
    count = len(arrays)
    ins = refs[:n_in]
    if parts_in == 1:
        weights = [tuple(refs[n_in : n_in + 3])]
        outs = refs[n_in + 3 :]
    else:
        gate_ref, up_ref, down_ref, far_ref, far_down_ref = refs[n_in : n_in + 5]
        hidden = gate_ref.shape[1]
        weights = [
            (gate_ref, up_ref, down_ref),
            (far_ref.at[:, 0:hidden], far_ref.at[:, hidden : 2 * hidden], far_down_ref),
        ]
        outs = refs[n_in + 5 :]
    deep, narrow = weights[0][0].shape[0], weights[0][2].shape[0]
    if parts_in == 1:
        spans = [(slice(0, deep), slice(0, narrow))]
    else:
        spans = [
            (pl.ds(pl.multiple_of(p * deep, LANES), deep), pl.ds(pl.multiple_of(p * narrow, LANES), narrow))
            for p in (me_ref[1], 1 - me_ref[1])
        ]
    half = count // 2
    far_out, far_dx = outs[2 * half : 2 * half + 2]
    out_refs, dx_refs = [], []
    for j in range(half):
        out_refs += [outs[j], far_out.at[j]]
        dx_refs += [outs[half + j], far_dx.at[j]]
    xs_ref, dy_ref, act_ref, du_ref, dw_ref, gs_ref, gcol_ref, dact_ref, dx_ref = outs[2 * half + 2 :]
    length = tokens // seqs
    me = me_ref[2]
    row_in = lax.rem(me, EXTRA)
    row = lax.broadcasted_iota(jnp.int32, (EXTRA, tokens), 0)
    mine = row == row_in
    block = lax.div(me, EXTRA)

    def table(extra, k):
        t = jnp.zeros((EXTRA, tokens), f32)
        for b in range(WIDTH // (3 * tokens)):
            at = (3 * b + k) * tokens
            t = jnp.where(block == b, extra[:, at : at + tokens].astype(f32), t)
        return jnp.sum(jnp.where(mine, t, 0.0), axis=0, keepdims=True)

    def read(pieces, first, rows):
        got = []
        for index, start, size, offset in pieces:
            lo, hi = max(first, start), min(first + rows, start + size)
            if lo < hi:
                got.append(ins[index][offset + lo - start : offset + hi - start])
        return got[0] if len(got) == 1 else jnp.concatenate(got, axis=0)

    tri_a = lax.broadcasted_iota(jnp.int32, (length, length), 0)
    tri_b = lax.broadcasted_iota(jnp.int32, (length, length), 1)
    before = (tri_a < tri_b).astype(bf16)
    slot = lax.broadcasted_iota(jnp.int32, (slots, tokens), 0).astype(f32)
    gates, masks = [], []
    for n2_pieces, _ in arrays:
        extra = read(n2_pieces, tokens, EXTRA)
        gates.append(table(extra, 0) + table(extra, 1))
        masks.append(table(extra, 2))
    picks = []
    for i, (n2_pieces, g_pieces) in enumerate(arrays):
        at = []
        for b in range(seqs):
            m = masks[i][:, b * length : (b + 1) * length]
            earlier = dot(jnp.broadcast_to(m, (16, length)).astype(bf16), before)[0:1]
            keep = (m > 0.5) & (earlier < capacity)
            at.append(jnp.where(keep, earlier + b * (slots // seqs), -1.0))
        pick = (slot == jnp.concatenate(at, axis=1)).astype(f32)
        gcol_ref[i * slots : (i + 1) * slots, :] = jnp.broadcast_to(
            jnp.sum(pick * gates[i], axis=1, keepdims=True), (slots, LANES)
        )
        pick = pick.astype(bf16)
        picks.append(pick)
        rows = slice(i * slots, (i + 1) * slots)
        xs_ref[rows, :] = dot(pick, read(n2_pieces, 0, tokens)).astype(bf16)
        gs_ref[rows, :] = dot(pick, read(g_pieces, 0, tokens)).astype(bf16)
    u = w = y = None
    for (gate_part, up_part, _), (rows, _) in zip(weights, spans, strict=True):
        xs = xs_ref[:, rows]
        more_u, more_w = dot(xs, gate_part[...]), dot(xs, up_part[...])
        u, w = (more_u, more_w) if u is None else (u + more_u, w + more_w)
    s = 1.0 / (1.0 + jnp.exp(-u))
    act_ref[...] = (u * s * w).astype(bf16)
    for (_, _, down_part), (_, rows) in zip(weights, spans, strict=True):
        more = dot(act_ref[:, rows], down_part[...])
        y = more if y is None else y + more
    y = y.astype(bf16).astype(f32)
    gcol = gcol_ref[:, 0:1]
    gs = gs_ref[...].astype(f32)
    dy = (gcol * gs).astype(bf16)
    dy_ref[...] = dy
    dg = jnp.sum(gs * y, axis=1, keepdims=True)
    weighted = (gcol * y).astype(bf16)
    for (_, _, down_part), (_, rows) in zip(weights, spans, strict=True):
        dact_ref[:, rows] = dot(dy, down_part[...], 1, 1)
    dact = dact_ref[...]
    du = (dact * w * s * (1.0 + u * (1.0 - s))).astype(bf16)
    dw = (dact * (u * s)).astype(bf16)
    du_ref[...] = du
    dw_ref[...] = dw
    for (gate_part, up_part, _), (rows, _) in zip(weights, spans, strict=True):
        dx_ref[:, rows] = (dot(du, gate_part[...], 1, 1) + dot(dw, up_part[...], 1, 1)).astype(bf16)
    dx = dx_ref[...]
    for i in range(count):
        rows = slice(i * slots, (i + 1) * slots)
        out_refs[i][...] = dot(picks[i], weighted[rows], 0, 0).astype(bf16)
        dx_refs[i][0:tokens] = dot(picks[i], dx[rows], 0, 0).astype(bf16)
        back = jnp.sum(picks[i].astype(f32) * dg[rows], axis=0, keepdims=True)
        high = back.astype(bf16).astype(f32)
        blank = jnp.zeros((EXTRA, tokens), f32)
        parts = []
        for b in range(WIDTH // (3 * tokens)):
            here = mine & (block == b)
            parts += [jnp.where(here, high, 0.0), jnp.where(here, back - high, 0.0), blank]
        dx_refs[i][tokens:] = jnp.concatenate(parts, axis=1).astype(bf16)


def weights_body(n, half, shift, adds, me_ref, *refs):
    lists = [refs[k * n : (k + 1) * n] for k in range(5)]
    xs, dys, acts, dus, dws = lists
    more = refs[5 * n : 5 * n + adds]
    outs = refs[5 * n + adds :]
    wide, narrow = half
    index = lax.rem(me_ref[1] + shift, me_ref[3])
    x_at = pl.multiple_of(index * wide, LANES)
    a_at = pl.multiple_of(index * narrow, LANES)
    totals = [None, None, None]
    for i in range(n):
        x = xs[i][:, pl.ds(x_at, wide)]
        a = acts[i][:, pl.ds(a_at, narrow)]
        for k, (left, right) in enumerate(((x, dus[i]), (x, dws[i]), (a, dys[i]))):
            now = dot(left, right[...], 0, 0)
            totals[k] = now if totals[k] is None else totals[k] + now
    hidden = totals[0].shape[1]
    columns = (slice(0, hidden), slice(hidden, 2 * hidden), slice(None))
    chunks = outs if shift else more
    rows = (wide + narrow) // CHUNKS
    for k, c in enumerate(columns):
        base, size = (wide, narrow) if k == 2 else (0, wide)
        for j, ref in enumerate(chunks):
            first = (j % CHUNKS) * rows
            lo, hi = max(first, base), min(first + rows, base + size)
            if lo < hi and shift:
                ref[lo - first : hi - first, c] = totals[k][lo - base : hi - base].astype(bf16)
            elif lo < hi and j < CHUNKS:
                value = totals[k][lo - base : hi - base]
                for other in chunks[j::CHUNKS]:
                    value = value + other[lo - first : hi - first, c].astype(f32)
                outs[k][lo - base : hi - base] = value


def blocks_out(where_ref, device, whole_ref, outs):
    keep_ref, send_ref = outs
    sides, count, rows, _ = keep_ref.shape
    for lane, out in enumerate((keep_ref, send_ref)):
        for side in range(sides):
            for k in range(count):
                at = where_ref[device, (2 * k + lane) * sides + side]
                out[side, k] = whole_ref[pl.ds(pl.multiple_of(at * rows, 16), rows), :]


def norm_back(up, hat, scale, gain):
    w = up * gain
    return scale * (w - hat * jnp.mean(w * hat, axis=-1, keepdims=True)), jnp.sum(up * hat, axis=0, keepdims=True)


def hidden_back_body(experts, apart, me_ref, where_ref, a_ref, b_ref, c_ref, d_ref, g_ref, hidden_ref, gain_ref, gate_ref, misc_ref, o_ref, mixed_ref, *outs):
    dh_ref, dmixed_ref, rg_ref, gg_ref, og_ref = outs[:4] + outs[-1:]
    tokens = g_ref.shape[0]
    got = a_ref[...].astype(f32) + b_ref[...].astype(f32) + c_ref[...].astype(f32) + d_ref[...].astype(f32)
    extra = got[tokens:]
    rows = []
    for first in range(experts // EXTRA):
        at = 3 * first * tokens
        rows.append(extra[:, at : at + tokens] + extra[:, at + tokens : at + 2 * tokens])
    rows.append(jnp.zeros((LANES - experts, tokens), f32))
    dg = jnp.transpose(jnp.concatenate(rows, axis=0))
    gate = gate_ref[...]
    dl = gate * (dg - jnp.sum(gate * dg, axis=-1, keepdims=True))
    dz = dl.astype(bf16)
    dn = got[0:tokens] + dot(dz, misc_ref[...], 1, 1)
    h = hidden_ref[...]
    scale = scale_of(h)
    hat = h * scale
    gain = gain_ref[1:2]
    n2 = (hat * gain).astype(bf16)
    rg_ref[...] = dot(n2, dz, 0, 0)
    back, grad = norm_back(dn, hat, scale, gain)
    gg_ref[...] = jnp.broadcast_to(grad, gg_ref.shape)
    dh = g_ref[...].astype(f32) + back
    dh_ref[...] = dh
    da = dh.astype(bf16)
    dmixed_ref[...] = dot(da, o_ref[...]).astype(bf16)
    og_ref[...] = dot(da, mixed_ref[...], 0, 0).astype(bf16)
    if apart:
        blocks_out(where_ref, me_ref[0], og_ref, outs[4:6])


def attend_back_body(seqs, experts, apart, me_ref, where_ref, x_ref, cos_ref, sin_ref, w_ref, gain_ref, n1_ref, q_ref, k_ref, v_ref, do_ref, dh_ref, rg_ref, gg_ref, dx_ref, *outs):
    wg_ref, dqkv_ref = outs[-2:]
    length = x_ref.shape[0] // seqs
    cos = cos_ref[...]
    sin = sin_ref[...]
    keep = causal_mask(length)

    def back(u):
        return (u * cos - pltpu.roll(u, HEAD // 2, 1) * sin).astype(bf16)

    for b in range(seqs):
        rows = slice(b * length, (b + 1) * length)
        for c in range(KEY_VALUE_HEADS):
            cols = slice(c * HEAD, (c + 1) * HEAD)
            k = k_ref[rows, cols]
            v = v_ref[rows, cols]
            q = heads_of(q_ref, b, length, c)
            do = heads_of(do_ref, b, length, c)
            p = softmax_of(q, k, keep)
            dqkv_ref[rows, Q_COLS + KV_COLS + c * HEAD : Q_COLS + KV_COLS + (c + 1) * HEAD] = dot(
                p.astype(bf16), do, 0, 0
            ).astype(bf16)
            dp = dot(do, v, 1, 1)
            ds = (p * (dp - jnp.sum(p * dp, axis=-1, keepdims=True))).astype(bf16)
            dq = dot(ds, k) * SCALE
            for h in range(GROUP):
                at = (c * GROUP + h) * HEAD
                dqkv_ref[rows, at : at + HEAD] = back(dq[h * length : (h + 1) * length])
            dqkv_ref[rows, Q_COLS + c * HEAD : Q_COLS + (c + 1) * HEAD] = back(dot(ds, q, 0, 0) * SCALE)
    dqkv = dqkv_ref[...]
    wg_ref[:, 0:MISC] = dot(n1_ref[...], dqkv, 0, 0).astype(bf16)
    dn = dot(dqkv, w_ref[...], 1, 1)
    x = x_ref[...].astype(f32)
    scale = scale_of(x)
    back_x, grad = norm_back(dn, x * scale, scale, gain_ref[0:1])
    dx_ref[...] = dh_ref[...] + back_x
    row = lax.broadcasted_iota(jnp.int32, (LANES, x.shape[1]), 0)
    gains = jnp.where(row == experts, grad, jnp.where(row == experts + 1, gg_ref[0:1], 0.0))
    wg_ref[:, MISC:] = (rg_ref[...] + jnp.transpose(gains)).astype(bf16)
    if apart:
        blocks_out(where_ref, me_ref[0], wg_ref, outs[:2])


def chip_ring(chips):
    if chips % 4 or chips < 8:
        return list(range(chips))
    high, low = 4, chips // 4
    order = [a * low for a in range(high)]
    for step, a in enumerate(reversed(range(high))):
        rest = list(range(1, low))
        order += [a * low + b for b in (rest if step % 2 == 0 else reversed(rest))]
    return order


class Ring:
    def __init__(self, devices):
        self.devices = devices
        self.chips = devices // 2
        self.half = self.chips // 2
        self.order = chip_ring(self.chips)
        n = self.chips
        self.up = [
            (2 * self.order[p] + lane, 2 * self.order[(p + 1) % n] + lane) for p in range(n) for lane in (0, 1)
        ]
        self.down = [(b, a) for a, b in self.up]
        self.swap = [(d, d ^ 1) for d in range(devices)]
        self.place = np.argsort(np.array(self.order)).astype(np.int32)
        self.offsets = [0] + [s * o for o in range(1, self.half) for s in (-1, 1)] + [self.half]

    def send_up(self, x):
        return lax.ppermute(x, "expert", self.up)

    def send_down(self, x):
        return lax.ppermute(x, "expert", self.down)

    def send_core(self, x):
        return lax.ppermute(x, "expert", self.swap)

    def table(self, dp):
        rows = []
        for y in range(dp):
            for e in range(self.devices):
                row = []
                for o in self.offsets:
                    chip = self.order[(int(self.place[e // 2]) + o) % self.chips]
                    for lane in (e % 2, 1 - e % 2):
                        row += [y * self.devices + 2 * chip + lane, (1 - y) * self.devices + 2 * chip + lane]
                rows.append(row)
        return np.array(rows, np.int32)

    def gather(self, x, split=None):
        return Gather(self, x, split)

    def scatter(self, own, far, split):
        return Scatter(self, own, far, split)


def after(x, *events):
    return lax.optimization_barrier((x, events))[0] if events else x


def total(*terms):
    out = terms[0].astype(f32)
    for t in terms[1:]:
        out = out + t.astype(f32)
    return out.astype(bf16)


class Gather:
    def __init__(self, ring, x, split):
        self.ring, self.split = ring, split
        self.got, self.far = {0: [x]}, {}
        self.hops = 0

    def hop(self, *events):
        ring, s = self.ring, self.hops
        self.hops += 1
        up, down = after((self.got[-s][0], self.got[s][0]), *events)
        if self.hops < ring.half:
            self.got[-self.hops], self.got[self.hops] = [ring.send_up(up)], [ring.send_down(down)]
        elif self.split is None:
            self.got[ring.half] = [ring.send_up(up)]
        else:
            self.got[ring.half] = [ring.send_up(up[: self.split]), ring.send_down(down[self.split :])]

    def swap(self, *offsets):
        for o in offsets:
            if o not in self.far:
                self.far[o] = [self.ring.send_core(p) for p in self.got[o]]


def fence(*things):
    rings = [t for t in things if isinstance(t, Gather)]
    arrays = [t for t in things if not isinstance(t, Gather)]
    held, arrays = lax.optimization_barrier(([(r.got, r.far) for r in rings], arrays))
    for r, (got, far) in zip(rings, held, strict=True):
        r.got, r.far = got, far
    return arrays


class Scatter:
    def __init__(self, ring, own, far, split):
        self.ring, self.own, self.far, self.split = ring, own, far, split
        self.partner, self.left = {}, ring.half

    def swap(self, offsets, *events):
        got = self.ring.send_core(after(self.far[offsets[0]], *events))
        for i, o in enumerate(offsets):
            self.partner[o] = got[i]

    def hop(self, *events):
        ring, own, partner, split, s = self.ring, self.own, self.partner, self.split, self.left
        self.left -= 1
        if s == ring.half:
            first = total(own[s], partner[s])
            up, down = first[:split], first[split:]
        elif s == ring.half - 1:
            more = own[s].shape[0] - split
            up = total(own[s], partner[s], jnp.pad(self.up, ((0, more), (0, 0))))
            down = total(own[-s], partner[-s], jnp.pad(self.down, ((split, 0), (0, 0))))
        else:
            up, down = total(own[s], partner[s], self.up), total(own[-s], partner[-s], self.down)
        self.sent = up, down = after((up, down), *events)
        self.up, self.down = ring.send_up(up), ring.send_down(down)
        return self.up, self.down

    def step(self, *events):
        there = self.hop(*events)
        self.swap([-self.left, self.left] if self.left else [0], *self.sent)
        return there

    def terms(self):
        return self.own[0], self.partner[0], self.up, self.down


def dp_pairs(shift):
    n = lax.axis_size("dp")
    return [(i, (i + shift) % n) for i in range(n)]


def from_dp(x, shift):
    return lax.ppermute(x, "dp", dp_pairs(shift))


def on_device(
    inputs,
    cotangent,
    routes,
    attention_gain,
    query_weight,
    key_matrix,
    value_matrix,
    output_weight,
    mixture_gain,
    router_weight,
    gate_weight,
    up_weight,
    down_weight,
):
    seqs, _, length, _ = inputs.shape
    tokens = seqs * length
    topk = routes.shape[3]
    dp, experts = lax.axis_size("dp"), lax.axis_size("expert")
    assert gate_weight.shape[0] == 1 and experts % EXTRA == 0 and experts * 3 * tokens <= EXTRA * WIDTH * 2
    ring = Ring(experts)
    my_dp, me = lax.axis_index("dp"), lax.axis_index("expert")
    capacity = (5 * length * topk + 4 * experts - 1) // (4 * experts)
    slots = seqs * ((capacity + 7) // 8 * 8)
    x = inputs.reshape(tokens, WIDTH)
    g = cotangent.reshape(tokens, WIDTH)
    cos, sin = (jnp.asarray(t) for t in rope_tables(length))
    split = length
    where_i = jnp.stack([my_dp * experts + me, my_dp, me, jnp.full_like(me, dp)]).astype(jnp.int32)

    rows = query_weight.shape[0]
    misc = jnp.concatenate(
        [
            router_weight,
            attention_gain[:, None],
            mixture_gain[:, None],
            jnp.zeros((rows, LANES - experts - 2), bf16),
        ],
        axis=1,
    )
    dense_own = jnp.concatenate([query_weight, key_matrix, value_matrix, misc, output_weight.T], axis=1)
    g_ring = ring.gather(g, split)
    g_ring.hop()
    apart = dp == 2 and rows % 16 == 0
    if apart:
        table = jnp.asarray(ring.table(dp))
        far = from_dp(dense_own, 1)
        d_ring = ring.gather(jnp.stack([dense_own, far]), 1)
        d_ring.hop()
        expert_start = (far,)
    else:
        table = jnp.zeros((dp * experts, 1), jnp.int32)
        both = lax.all_gather(dense_own, ("dp", "expert"), axis=0, tiled=True)
        dense = [both[None]]
        expert_start = (both,)

    hidden_size = gate_weight.shape[2]
    wide, narrow = WIDTH // dp, hidden_size // dp
    in_parts = dp == 2 and wide % LANES == 0 and narrow % LANES == 0
    if in_parts:
        flat = [jnp.concatenate([gate_weight[0], up_weight[0]], axis=1)]
        halves = [from_dp(after(flat[0], *expert_start), 1)]
        halves.append(from_dp(after(down_weight[0], *halves), 1))
        expert_weights = [gate_weight[0], up_weight[0], down_weight[0], *halves]
    else:
        expert_weights = [
            lax.all_gather(after(w[0], *expert_start), "dp", axis=0, tiled=True)
            for w in (gate_weight, up_weight, down_weight)
        ]
        flat, halves = [], []

    if apart:
        d_ring.hop(g_ring.got[-1], g_ring.got[1], *flat)
        while d_ring.hops < ring.half:
            d_ring.hop(*(halves[:1] if d_ring.hops == ring.half - 1 else ()))
        d_ring.swap(*ring.offsets)
        fence(d_ring, g_ring)
        dense = []
        for o in ring.offsets:
            dense += d_ring.got[o] + d_ring.far[o]
    g_ring.hop()

    w_full, o_t, misc_full, gains, n1, q, k, v, mixed, hidden, send, gate_values = call(
        functools.partial(forward_body, seqs, experts, len(dense)),
        [
            sds((WIDTH, MISC), bf16),
            sds((WIDTH, Q_COLS), bf16),
            sds((WIDTH, LANES), bf16),
            sds((8, WIDTH), f32),
            sds((tokens, WIDTH), bf16),
            sds((tokens, Q_COLS), bf16),
            sds((tokens, KV_COLS), bf16),
            sds((tokens, KV_COLS), bf16),
            sds((tokens, Q_COLS), bf16),
            sds((tokens, WIDTH), f32),
            sds((tokens + EXTRA, WIDTH), bf16),
            sds((tokens, LANES), f32),
        ],
        [smem(), smem()] + vmem(4 + len(dense)),
        [where_i, table, x, cos, sin, routes.reshape(tokens, topk), *dense],
        "forward",
        60,
    )

    n_ring = ring.gather(send, split)
    out_own, out_far, dx_own, dx_far = {}, {}, {}, {}
    kept = {}
    groups = [[0]] + [[-s, s] for s in range(1, ring.half)] + [[ring.half]]

    def pieces_of(group):
        return jnp.concatenate([p for o in group for r in (n_ring, g_ring) for p in r.got[o]])

    def experts_on(group, far, *events):
        args, arrays, offset = [far], [], 0
        for o in group:
            own, other = [], []
            for pieces in (n_ring.got[o], g_ring.got[o]):
                start, first = 0, len(args)
                own.append([])
                other.append([])
                for j, p in enumerate(pieces):
                    args.append(p)
                    own[-1].append((first + j, start, p.shape[0], 0))
                    other[-1].append((0, start, p.shape[0], offset))
                    start += p.shape[0]
                    offset += p.shape[0]
            arrays += [tuple(own), tuple(other)]
        count = len(arrays)
        rows_ = count * slots
        outs = call(
            functools.partial(expert_body, (arrays, len(args), 2 if in_parts else 1), capacity, slots, tokens, seqs),
            [sds((tokens, WIDTH), bf16)] * len(group)
            + [sds((tokens + EXTRA, WIDTH), bf16)] * len(group)
            + [sds((len(group), tokens, WIDTH), bf16), sds((len(group), tokens + EXTRA, WIDTH), bf16)]
            + [sds((rows_, WIDTH), bf16)] * 2
            + [sds((rows_, hidden_size), bf16)] * 3,
            [smem()] + vmem(len(args) + len(expert_weights)),
            [after(where_i, *events), *args, *expert_weights],
            "experts",
            36,
            [
                pltpu.VMEM((rows_, WIDTH), bf16),
                pltpu.VMEM((rows_, LANES), f32),
                pltpu.VMEM((rows_, hidden_size), f32),
                pltpu.VMEM((rows_, WIDTH), bf16),
            ],
        )
        n = len(group)
        for i, o in enumerate(group):
            out_own[o], dx_own[o] = outs[i], outs[n + i]
        out_far[group[0]], dx_far[group[0]] = outs[2 * n : 2 * n + 2]
        kept[group[0]] = outs[2 * n + 2 :]
        return kept[group[0]]

    waiting, _ = fence(pieces_of(groups[0]), expert_weights[-1], n_ring, g_ring)
    far = []
    for hop in range(1, ring.half + 1):
        n_ring.hop()
        if g_ring.hops < ring.half:
            g_ring.hop()
        near, far = far, ring.send_core(waiting)
        waiting = pieces_of(groups[hop])
        if hop > 1:
            group = groups[hop - 2]
            waiting, far, kept[group[0]] = fence(waiting, far, experts_on(group, near), n_ring, g_ring)
        else:
            waiting, far = fence(waiting, far, n_ring, g_ring)
    (last,) = fence(ring.send_core(waiting))
    experts_on(groups[-1], last)
    dx_ring = ring.scatter(dx_own, dx_far, split)
    dx_ring.swap(groups[-1])
    there = dx_ring.hop()
    experts_on(groups[-2], far, *dx_ring.sent)
    dx_ring.swap(groups[-2], *there)
    dx_ring.hop()
    dx_ring.swap(groups[-3], *dx_ring.sent)
    kept = [[kept[group[0]][i] for group in groups] for i in range(5)]

    saved = [a for k_ in kept for a in k_]
    if wide % LANES == 0 and narrow % LANES == 0:

        def part(shift, outs, more, *events):
            return call(
                functools.partial(weights_body, len(groups), (wide, narrow), shift, len(more)),
                outs,
                [smem()] + vmem(len(saved) + len(more)),
                [after(where_i, *events), *saved, *more],
                "expert_weights",
                36,
            )

        more = []
        for shift in range(1, dp):
            parts = part(shift, [sds(((wide + narrow) // CHUNKS, WIDTH), bf16)] * CHUNKS, [], *dx_ring.sent, *more)
            for p in parts:
                more.append(from_dp(after(p, *more[-1:]), shift))
        weights_sent = (parts[0],)
    else:
        xs, dys, acts, dus, dws = (jnp.concatenate(k_) for k_ in kept)
        expert_grads = tuple(
            lax.psum_scatter(dot(a, b, 0, 0).astype(bf16), "dp", scatter_dimension=0, tiled=True).astype(f32)
            for a, b in ((xs, dus), (xs, dws), (acts, dys))
        )
        weights_sent, more = (), []
    dx_ring.step(*weights_sent)
    while dx_ring.left:
        dx_ring.step(*more[:1])
    dx_terms = dx_ring.terms()
    out_ring = ring.scatter(out_own, out_far, split)
    out_ring.swap(groups[-1], *dx_ring.sent)
    out_ring.step(*dx_terms[2:], *more[1:2])

    def block_outs(columns):
        return [sds((dp, ring.chips, rows, columns), bf16)] * 2

    dh, dmixed, router_part, gain_part, *o_part = call(
        functools.partial(hidden_back_body, experts, apart),
        [sds((tokens, WIDTH), f32), sds((tokens, Q_COLS), bf16), sds((WIDTH, LANES), f32), sds((8, WIDTH), f32)]
        + (block_outs(Q_COLS) if apart else [sds((WIDTH, Q_COLS), bf16)]),
        [smem(), smem()] + vmem(11),
        [after(where_i, *out_ring.sent), table, *dx_terms, g, hidden, gains, gate_values, misc_full, o_t, mixed],
        "hidden_back",
        36,
        [pltpu.VMEM((WIDTH, Q_COLS), bf16)] if apart else [],
    )
    out_ring.step(dh, *more[2:3])
    o_got = [ring.send_core(after(o_part[1], *out_ring.sent))] if apart else []
    input_grad, *qkv_part = call(
        functools.partial(attend_back_body, seqs, experts, apart),
        [sds((tokens, WIDTH), f32)]
        + (block_outs(MISC + LANES) if apart else [sds((WIDTH, MISC + LANES), bf16)]),
        [smem(), smem()] + vmem(13),
        [after(where_i, *out_ring.sent), table, x, cos, sin, w_full, gains, n1, q, k, v, dmixed, dh, router_part, gain_part],
        "attend_back",
        36,
        ([pltpu.VMEM((WIDTH, MISC + LANES), bf16)] if apart else []) + [pltpu.VMEM((tokens, MISC), bf16)],
    )

    out_ring.step(input_grad, *more, *o_got)
    if wide % LANES == 0 and narrow % LANES == 0:
        expert_grads = part(
            0, [sds((wide, hidden_size), f32)] * 2 + [sds((narrow, WIDTH), f32)], more, *out_ring.sent
        )
    gate_grad, up_grad, down_grad = expert_grads

    def over_y(keep, got, *events):
        far = from_dp(after(total(keep[1], got[1]), *events), 1)
        return total(keep[0], got[0], far)

    class Blocks:
        def __init__(self, both):
            self.term = {o: both[k_] for k_, o in enumerate(ring.offsets)}
            self.up, self.down, self.left = None, None, ring.half

        def hop(self, *events):
            s = self.left
            self.left -= 1
            up = self.term[s] if self.up is None else total(self.up, self.term[s])
            if s == ring.half:
                self.up = ring.send_up(after(up, *events))
                return (self.up,)
            down = self.term[-s] if self.down is None else total(self.down, self.term[-s])
            up, down = after((up, down), *events)
            self.up, self.down = ring.send_up(up), ring.send_down(down)
            return self.up, self.down

        def result(self):
            while self.left:
                self.hop()
            return self.up.astype(f32) + self.down.astype(f32) + self.term[0].astype(f32)

    if apart:
        qkv_got = ring.send_core(after(qkv_part[1], *out_ring.sent))
        o_sum = over_y(o_part[0], *o_got, *out_ring.sent)
        while out_ring.left:
            there = out_ring.step(gate_grad, o_sum, qkv_got)
        qkv_sum = over_y(qkv_part[0], qkv_got, *out_ring.sent)
        o_blocks, qkv_blocks = Blocks(o_sum), Blocks(qkv_sum)
        there += o_blocks.hop(*out_ring.sent)
        qkv_blocks.hop(*there)
        o_grad, qkv_grad = o_blocks.result(), qkv_blocks.result()
    else:
        while out_ring.left:
            out_ring.step()
        o_grad, qkv_grad = (
            lax.psum_scatter(p[0], ("dp", "expert"), scatter_dimension=0, tiled=True).astype(f32)
            for p in (o_part, qkv_part)
        )

    outputs = total(hidden, *out_ring.terms()).reshape(inputs.shape)
    return (
        outputs,
        input_grad.reshape(inputs.shape),
        qkv_grad[:, MISC + experts],
        qkv_grad[:, :Q_COLS],
        qkv_grad[:, Q_COLS : Q_COLS + KV_COLS],
        qkv_grad[:, Q_COLS + KV_COLS : MISC],
        o_grad.T,
        qkv_grad[:, MISC + experts + 1],
        qkv_grad[:, MISC : MISC + experts],
        gate_grad[None],
        up_grad[None],
        down_grad[None],
    )


def solution(mesh):
    both = ("dp", "expert")
    tokens = P(None, both, None, None)
    expert = P("expert", "dp", None)
    in_specs = (
        tokens,
        tokens,
        tokens,
        P(both),
        P(both, None),
        P(both, None),
        P(both, None),
        P(None, both),
        P(both),
        P(both, None),
        expert,
        expert,
        expert,
    )
    out_specs = (
        tokens,
        tokens,
        P(both),
        P(both, None),
        P(both, None),
        P(both, None),
        P(None, both),
        P(both),
        P(both, None),
        expert,
        expert,
        expert,
    )
    return jax.shard_map(on_device, mesh=mesh, in_specs=in_specs, out_specs=out_specs, check_vma=False)
```

```python
import functools
import math

import jax
import jax.numpy as jnp
import numpy as np
from jax import lax
from jax.experimental import pallas as pl
from jax.experimental.pallas import tpu as pltpu
from jax.sharding import PartitionSpec as P

WIDTH = 1536
QUERY_HEADS = 12
KEY_VALUE_HEADS = 2
HEAD = 128
GROUP = QUERY_HEADS // KEY_VALUE_HEADS
Q_COLS = QUERY_HEADS * HEAD
KV_COLS = KEY_VALUE_HEADS * HEAD
MISC = Q_COLS + 2 * KV_COLS
EXTRA = 16
LANES = 128
CHUNKS = (9, 9, 7, 11)
EPSILON = 1e-06
ROPE_BASE = 10000.0
MASKED = -1e30
SCALE = 1.0 / math.sqrt(HEAD)

f32 = jnp.float32
bf16 = jnp.bfloat16


def dot(a, b, ca=1, cb=0):
    return lax.dot_general(a, b, (((ca,), (cb,)), ((), ())), preferred_element_type=f32)


def vmem(n):
    return [pl.BlockSpec(memory_space=pltpu.VMEM)] * n


def smem():
    return pl.BlockSpec(memory_space=pltpu.SMEM)


def call(body, outs, ins, args, name, vmem_mb, scratch=()):
    return pl.pallas_call(
        body,
        out_shape=outs,
        in_specs=ins,
        out_specs=vmem(len(outs)),
        scratch_shapes=list(scratch),
        compiler_params=pltpu.CompilerParams(vmem_limit_bytes=vmem_mb * 1024 * 1024),
        cost_estimate=pl.CostEstimate(flops=1 << 20, bytes_accessed=1 << 20, transcendentals=0),
        name=name,
    )(*args)


def sds(shape, dtype):
    return jax.ShapeDtypeStruct(shape, dtype)


def rope_tables(length):
    half = HEAD // 2
    frequency = ROPE_BASE ** (-(np.arange(half, dtype=np.float64) * 2.0 / HEAD))
    angles = np.arange(length, dtype=np.float64)[:, None] * frequency[None, :]
    cos, sin = np.cos(angles), np.sin(angles)
    cosine = np.concatenate([cos, cos], axis=1).astype(np.float32)
    signed = np.concatenate([-sin, sin], axis=1).astype(np.float32)
    return cosine, signed


def place(where_ref, device, piece_refs, targets):
    at = 0
    for ref in piece_refs:
        blocks, rows, _ = ref.shape
        for j in range(blocks):
            start = pl.multiple_of(where_ref[device, at] * rows, 16 if rows % 16 == 0 else 8)
            for target, column in targets:
                target[pl.ds(start, rows), :] = ref[j, :, column : column + target.shape[1]]
            at += 1


def scale_of(z):
    return lax.rsqrt(jnp.mean(z * z, axis=-1, keepdims=True) + EPSILON)


def heads_of(ref, b, length, c):
    return jnp.concatenate(
        [ref[b * length : (b + 1) * length, h * HEAD : (h + 1) * HEAD] for h in range(c * GROUP, (c + 1) * GROUP)],
        axis=0,
    )


def causal_mask(length):
    row = lax.broadcasted_iota(jnp.int32, (length, length), 0)
    column = lax.broadcasted_iota(jnp.int32, (length, length), 1)
    return jnp.concatenate([row >= column] * GROUP, axis=0)


def softmax_of(q, k, keep):
    s = jnp.where(keep, dot(q, k, 1, 1) * SCALE, MASKED)
    e = jnp.exp(s - jnp.max(s, axis=-1, keepdims=True))
    return e / jnp.sum(e, axis=-1, keepdims=True)


def forward_body(seqs, experts, n_pieces, me_ref, where_ref, x_ref, cos_ref, sin_ref, routes_ref, *refs):
    pieces = refs[:n_pieces]
    w_ref, o_ref, misc_ref, gain_ref, n1_ref, q_ref, k_ref, v_ref, mixed_ref, hidden_ref, send_ref, gate_ref = refs[n_pieces:]
    length = x_ref.shape[0] // seqs
    place(where_ref, me_ref[0], pieces, ((w_ref, 0), (misc_ref, MISC), (o_ref, MISC + LANES)))
    gains = jnp.transpose(misc_ref[...].astype(f32))[experts : experts + 8]
    gain_ref[...] = gains
    x = x_ref[...].astype(f32)
    n1 = (x * scale_of(x) * gains[0:1]).astype(bf16)
    n1_ref[...] = n1
    cos = jnp.concatenate([cos_ref[...]] * seqs, axis=0)
    sin = jnp.concatenate([sin_ref[...]] * seqs, axis=0)

    def rotated(u):
        return (u * cos + pltpu.roll(u, HEAD // 2, 1) * sin).astype(bf16)

    kv = dot(n1, w_ref[:, Q_COLS:])
    v_ref[...] = kv[:, KV_COLS:].astype(bf16)
    for c in range(KEY_VALUE_HEADS):
        k_ref[:, c * HEAD : (c + 1) * HEAD] = rotated(kv[:, c * HEAD : (c + 1) * HEAD])
    keep = causal_mask(length)
    for c in range(KEY_VALUE_HEADS):
        cols = GROUP * HEAD
        q = dot(n1, w_ref[:, c * cols : (c + 1) * cols])
        for h in range(GROUP):
            at = c * cols + h * HEAD
            q_ref[:, at : at + HEAD] = rotated(q[:, h * HEAD : (h + 1) * HEAD])
        for b in range(seqs):
            rows = slice(b * length, (b + 1) * length)
            k = k_ref[rows, c * HEAD : (c + 1) * HEAD]
            v = v_ref[rows, c * HEAD : (c + 1) * HEAD]
            p = softmax_of(heads_of(q_ref, b, length, c), k, keep).astype(bf16)
            o = dot(p, v).astype(bf16)
            for h in range(GROUP):
                at = c * cols + h * HEAD
                mixed_ref[rows, at : at + HEAD] = o[h * length : (h + 1) * length]
    tokens = x_ref.shape[0]
    h = x + dot(mixed_ref[...], o_ref[...], 1, 1)
    hidden_ref[...] = h
    n2 = (h * scale_of(h) * gains[1:2]).astype(bf16)
    send_ref[0:tokens] = n2
    z = dot(n2, misc_ref[...])
    lane = lax.broadcasted_iota(jnp.int32, (tokens, LANES), 1)
    chosen = lane == routes_ref[:, 0:1]
    for j in range(1, routes_ref.shape[1]):
        chosen = chosen | (lane == routes_ref[:, j : j + 1])
    top = jnp.max(jnp.where(chosen, z, MASKED), axis=-1, keepdims=True)
    e = jnp.where(chosen, jnp.exp(jnp.where(chosen, z - top, 0.0)), 0.0)
    gate = e / jnp.sum(e, axis=-1, keepdims=True)
    gate_ref[...] = gate
    high = gate.astype(bf16).astype(f32)
    tables = [jnp.transpose(t) for t in (high, gate - high, chosen.astype(f32))]
    blank = jnp.zeros((EXTRA, tokens), f32)
    parts = []
    for first in range(0, experts, EXTRA):
        parts += [t[first : first + EXTRA] for t in tables]
    parts += [blank] * (WIDTH // tokens - len(parts))
    send_ref[tokens:] = jnp.concatenate(parts, axis=1).astype(bf16)


def expert_body(layout, capacity, slots, tokens, seqs, me_ref, *refs):
    arrays, n_in, parts_in = layout
    count = len(arrays)
    ins = refs[:n_in]
    if parts_in == 1:
        weights = [tuple(refs[n_in : n_in + 3])]
        outs = refs[n_in + 3 :]
    else:
        gate_ref, up_ref, down_ref, far_ref, far_down_ref = refs[n_in : n_in + 5]
        hidden = gate_ref.shape[1]
        weights = [
            (gate_ref, up_ref, down_ref),
            (far_ref.at[:, 0:hidden], far_ref.at[:, hidden : 2 * hidden], far_down_ref),
        ]
        outs = refs[n_in + 5 :]
    deep, narrow = weights[0][0].shape[0], weights[0][2].shape[0]
    if parts_in == 1:
        spans = [(slice(0, deep), slice(0, narrow))]
    else:
        spans = [
            (pl.ds(pl.multiple_of(p * deep, LANES), deep), pl.ds(pl.multiple_of(p * narrow, LANES), narrow))
            for p in (me_ref[1], 1 - me_ref[1])
        ]
    half = count // 2
    far_out, far_dx = outs[2 * half : 2 * half + 2]
    out_refs, dx_refs = [], []
    for j in range(half):
        out_refs += [outs[j], far_out.at[j]]
        dx_refs += [outs[half + j], far_dx.at[j]]
    xs_ref, dy_ref, act_ref, du_ref, dw_ref, gs_ref, gcol_ref, dact_ref, dx_ref = outs[2 * half + 2 :]
    length = tokens // seqs
    me = me_ref[2]
    row_in = lax.rem(me, EXTRA)
    row = lax.broadcasted_iota(jnp.int32, (EXTRA, tokens), 0)
    mine = row == row_in
    block = lax.div(me, EXTRA)

    def table(extra, k):
        t = jnp.zeros((EXTRA, tokens), f32)
        for b in range(WIDTH // (3 * tokens)):
            at = (3 * b + k) * tokens
            t = jnp.where(block == b, extra[:, at : at + tokens].astype(f32), t)
        return jnp.sum(jnp.where(mine, t, 0.0), axis=0, keepdims=True)

    def read(pieces, first, rows):
        got = []
        for index, start, size, offset in pieces:
            lo, hi = max(first, start), min(first + rows, start + size)
            if lo < hi:
                got.append(ins[index][offset + lo - start : offset + hi - start])
        return got[0] if len(got) == 1 else jnp.concatenate(got, axis=0)

    tri_a = lax.broadcasted_iota(jnp.int32, (length, length), 0)
    tri_b = lax.broadcasted_iota(jnp.int32, (length, length), 1)
    before = (tri_a < tri_b).astype(bf16)
    slot = lax.broadcasted_iota(jnp.int32, (slots, tokens), 0).astype(f32)
    gates, masks = [], []
    for n2_pieces, _ in arrays:
        extra = read(n2_pieces, tokens, EXTRA)
        gates.append(table(extra, 0) + table(extra, 1))
        masks.append(table(extra, 2))
    picks = []
    for i, (n2_pieces, g_pieces) in enumerate(arrays):
        at = []
        for b in range(seqs):
            m = masks[i][:, b * length : (b + 1) * length]
            earlier = dot(jnp.broadcast_to(m, (16, length)).astype(bf16), before)[0:1]
            keep = (m > 0.5) & (earlier < capacity)
            at.append(jnp.where(keep, earlier + b * (slots // seqs), -1.0))
        pick = (slot == jnp.concatenate(at, axis=1)).astype(f32)
        gcol_ref[i * slots : (i + 1) * slots, :] = jnp.broadcast_to(
            jnp.sum(pick * gates[i], axis=1, keepdims=True), (slots, LANES)
        )
        pick = pick.astype(bf16)
        picks.append(pick)
        rows = slice(i * slots, (i + 1) * slots)
        xs_ref[rows, :] = dot(pick, read(n2_pieces, 0, tokens)).astype(bf16)
        gs_ref[rows, :] = dot(pick, read(g_pieces, 0, tokens)).astype(bf16)
    u = w = y = None
    for (gate_part, up_part, _), (rows, _) in zip(weights, spans, strict=True):
        xs = xs_ref[:, rows]
        more_u, more_w = dot(xs, gate_part[...]), dot(xs, up_part[...])
        u, w = (more_u, more_w) if u is None else (u + more_u, w + more_w)
    s = 1.0 / (1.0 + jnp.exp(-u))
    act_ref[...] = (u * s * w).astype(bf16)
    for (_, _, down_part), (_, rows) in zip(weights, spans, strict=True):
        more = dot(act_ref[:, rows], down_part[...])
        y = more if y is None else y + more
    y = y.astype(bf16).astype(f32)
    gcol = gcol_ref[:, 0:1]
    gs = gs_ref[...].astype(f32)
    dy = (gcol * gs).astype(bf16)
    dy_ref[...] = dy
    dg = jnp.sum(gs * y, axis=1, keepdims=True)
    weighted = (gcol * y).astype(bf16)
    for (_, _, down_part), (_, rows) in zip(weights, spans, strict=True):
        dact_ref[:, rows] = dot(dy, down_part[...], 1, 1)
    dact = dact_ref[...]
    du = (dact * w * s * (1.0 + u * (1.0 - s))).astype(bf16)
    dw = (dact * (u * s)).astype(bf16)
    du_ref[...] = du
    dw_ref[...] = dw
    for (gate_part, up_part, _), (rows, _) in zip(weights, spans, strict=True):
        dx_ref[:, rows] = (dot(du, gate_part[...], 1, 1) + dot(dw, up_part[...], 1, 1)).astype(bf16)
    dx = dx_ref[...]
    for i in range(count):
        rows = slice(i * slots, (i + 1) * slots)
        out_refs[i][...] = dot(picks[i], weighted[rows], 0, 0).astype(bf16)
        dx_refs[i][0:tokens] = dot(picks[i], dx[rows], 0, 0).astype(bf16)
        back = jnp.sum(picks[i].astype(f32) * dg[rows], axis=0, keepdims=True)
        high = back.astype(bf16).astype(f32)
        blank = jnp.zeros((EXTRA, tokens), f32)
        parts = []
        for b in range(WIDTH // (3 * tokens)):
            here = mine & (block == b)
            parts += [jnp.where(here, high, 0.0), jnp.where(here, back - high, 0.0), blank]
        dx_refs[i][tokens:] = jnp.concatenate(parts, axis=1).astype(bf16)


def chunk_edges(rows):
    unit, at, edges = rows // sum(CHUNKS), 0, []
    for c in CHUNKS:
        edges.append((at, at + c * unit))
        at += c * unit
    return edges


def weights_body(n, half, shift, adds, me_ref, *refs):
    lists = [refs[k * n : (k + 1) * n] for k in range(5)]
    xs, dys, acts, dus, dws = lists
    more = refs[5 * n : 5 * n + adds]
    outs = refs[5 * n + adds :]
    wide, narrow = half
    index = lax.rem(me_ref[1] + shift, me_ref[3])
    x_at = pl.multiple_of(index * wide, LANES)
    a_at = pl.multiple_of(index * narrow, LANES)
    totals = [None, None, None]
    for i in range(n):
        x = xs[i][:, pl.ds(x_at, wide)]
        a = acts[i][:, pl.ds(a_at, narrow)]
        for k, (left, right) in enumerate(((x, dus[i]), (x, dws[i]), (a, dys[i]))):
            now = dot(left, right[...], 0, 0)
            totals[k] = now if totals[k] is None else totals[k] + now
    hidden = totals[0].shape[1]
    columns = (slice(0, hidden), slice(hidden, 2 * hidden), slice(None))
    chunks = outs if shift else more
    edges = chunk_edges(wide + narrow)
    for k, c in enumerate(columns):
        base, size = (wide, narrow) if k == 2 else (0, wide)
        for j, ref in enumerate(chunks):
            first, end = edges[j % len(CHUNKS)]
            lo, hi = max(first, base), min(end, base + size)
            if lo < hi and shift:
                ref[lo - first : hi - first, c] = totals[k][lo - base : hi - base].astype(bf16)
            elif lo < hi and j < len(CHUNKS):
                value = totals[k][lo - base : hi - base]
                for other in chunks[j :: len(CHUNKS)]:
                    value = value + other[lo - first : hi - first, c].astype(f32)
                outs[k][lo - base : hi - base] = value


def blocks_out(where_ref, device, whole_ref, outs):
    keep_ref, send_ref = outs
    sides, count, rows, _ = keep_ref.shape
    for lane, out in enumerate((keep_ref, send_ref)):
        for side in range(sides):
            for k in range(count):
                at = where_ref[device, (2 * k + lane) * sides + side]
                out[side, k] = whole_ref[pl.ds(pl.multiple_of(at * rows, 16), rows), :]


def norm_back(up, hat, scale, gain):
    w = up * gain
    return scale * (w - hat * jnp.mean(w * hat, axis=-1, keepdims=True)), jnp.sum(up * hat, axis=0, keepdims=True)


def hidden_back_body(experts, apart, me_ref, where_ref, a_ref, b_ref, c_ref, d_ref, g_ref, hidden_ref, gain_ref, gate_ref, misc_ref, o_ref, mixed_ref, *outs):
    dh_ref, dmixed_ref, rg_ref, gg_ref, og_ref = outs[:4] + outs[-1:]
    tokens = g_ref.shape[0]
    got = a_ref[...].astype(f32) + b_ref[...].astype(f32) + c_ref[...].astype(f32) + d_ref[...].astype(f32)
    extra = got[tokens:]
    rows = []
    for first in range(experts // EXTRA):
        at = 3 * first * tokens
        rows.append(extra[:, at : at + tokens] + extra[:, at + tokens : at + 2 * tokens])
    rows.append(jnp.zeros((LANES - experts, tokens), f32))
    dg = jnp.transpose(jnp.concatenate(rows, axis=0))
    gate = gate_ref[...]
    dl = gate * (dg - jnp.sum(gate * dg, axis=-1, keepdims=True))
    dz = dl.astype(bf16)
    dn = got[0:tokens] + dot(dz, misc_ref[...], 1, 1)
    h = hidden_ref[...]
    scale = scale_of(h)
    hat = h * scale
    gain = gain_ref[1:2]
    n2 = (hat * gain).astype(bf16)
    rg_ref[...] = dot(n2, dz, 0, 0)
    back, grad = norm_back(dn, hat, scale, gain)
    gg_ref[...] = jnp.broadcast_to(grad, gg_ref.shape)
    dh = g_ref[...].astype(f32) + back
    dh_ref[...] = dh
    da = dh.astype(bf16)
    dmixed_ref[...] = dot(da, o_ref[...]).astype(bf16)
    og_ref[...] = dot(da, mixed_ref[...], 0, 0).astype(bf16)
    if apart:
        blocks_out(where_ref, me_ref[0], og_ref, outs[4:6])


def attend_back_body(seqs, experts, apart, me_ref, where_ref, x_ref, cos_ref, sin_ref, w_ref, gain_ref, n1_ref, q_ref, k_ref, v_ref, do_ref, dh_ref, rg_ref, gg_ref, dx_ref, *outs):
    wg_ref, dqkv_ref = outs[-2:]
    length = x_ref.shape[0] // seqs
    cos = cos_ref[...]
    sin = sin_ref[...]
    keep = causal_mask(length)

    def back(u):
        return (u * cos - pltpu.roll(u, HEAD // 2, 1) * sin).astype(bf16)

    for b in range(seqs):
        rows = slice(b * length, (b + 1) * length)
        for c in range(KEY_VALUE_HEADS):
            cols = slice(c * HEAD, (c + 1) * HEAD)
            k = k_ref[rows, cols]
            v = v_ref[rows, cols]
            q = heads_of(q_ref, b, length, c)
            do = heads_of(do_ref, b, length, c)
            p = softmax_of(q, k, keep)
            dqkv_ref[rows, Q_COLS + KV_COLS + c * HEAD : Q_COLS + KV_COLS + (c + 1) * HEAD] = dot(
                p.astype(bf16), do, 0, 0
            ).astype(bf16)
            dp = dot(do, v, 1, 1)
            ds = (p * (dp - jnp.sum(p * dp, axis=-1, keepdims=True))).astype(bf16)
            dq = dot(ds, k) * SCALE
            for h in range(GROUP):
                at = (c * GROUP + h) * HEAD
                dqkv_ref[rows, at : at + HEAD] = back(dq[h * length : (h + 1) * length])
            dqkv_ref[rows, Q_COLS + c * HEAD : Q_COLS + (c + 1) * HEAD] = back(dot(ds, q, 0, 0) * SCALE)
    dqkv = dqkv_ref[...]
    wg_ref[:, 0:MISC] = dot(n1_ref[...], dqkv, 0, 0).astype(bf16)
    dn = dot(dqkv, w_ref[...], 1, 1)
    x = x_ref[...].astype(f32)
    scale = scale_of(x)
    back_x, grad = norm_back(dn, x * scale, scale, gain_ref[0:1])
    dx_ref[...] = dh_ref[...] + back_x
    row = lax.broadcasted_iota(jnp.int32, (LANES, x.shape[1]), 0)
    gains = jnp.where(row == experts, grad, jnp.where(row == experts + 1, gg_ref[0:1], 0.0))
    wg_ref[:, MISC:] = (rg_ref[...] + jnp.transpose(gains)).astype(bf16)
    if apart:
        blocks_out(where_ref, me_ref[0], wg_ref, outs[:2])


def chip_ring(chips):
    if chips % 4 or chips < 8:
        return list(range(chips))
    high, low = 4, chips // 4
    order = [a * low for a in range(high)]
    for step, a in enumerate(reversed(range(high))):
        rest = list(range(1, low))
        order += [a * low + b for b in (rest if step % 2 == 0 else reversed(rest))]
    return order


class Ring:
    def __init__(self, devices):
        self.devices = devices
        self.chips = devices // 2
        self.half = self.chips // 2
        self.order = chip_ring(self.chips)
        n = self.chips
        self.up = [
            (2 * self.order[p] + lane, 2 * self.order[(p + 1) % n] + lane) for p in range(n) for lane in (0, 1)
        ]
        self.down = [(b, a) for a, b in self.up]
        self.swap = [(d, d ^ 1) for d in range(devices)]
        self.place = np.argsort(np.array(self.order)).astype(np.int32)
        self.offsets = [0] + [s * o for o in range(1, self.half) for s in (-1, 1)] + [self.half]

    def send_up(self, x):
        return lax.ppermute(x, "expert", self.up)

    def send_down(self, x):
        return lax.ppermute(x, "expert", self.down)

    def send_core(self, x):
        return lax.ppermute(x, "expert", self.swap)

    def table(self, dp):
        rows = []
        for y in range(dp):
            for e in range(self.devices):
                row = []
                for o in self.offsets:
                    chip = self.order[(int(self.place[e // 2]) + o) % self.chips]
                    for lane in (e % 2, 1 - e % 2):
                        row += [y * self.devices + 2 * chip + lane, (1 - y) * self.devices + 2 * chip + lane]
                rows.append(row)
        return np.array(rows, np.int32)

    def gather(self, x, split=None):
        return Gather(self, x, split)

    def scatter(self, own, far, split):
        return Scatter(self, own, far, split)


def after(x, *events):
    return lax.optimization_barrier((x, events))[0] if events else x


def total(*terms):
    out = terms[0].astype(f32)
    for t in terms[1:]:
        out = out + t.astype(f32)
    return out.astype(bf16)


class Gather:
    def __init__(self, ring, x, split):
        self.ring, self.split = ring, split
        self.got, self.far = {0: [x]}, {}
        self.hops = 0

    def hop(self, *events):
        ring, s = self.ring, self.hops
        self.hops += 1
        up, down = after((self.got[-s][0], self.got[s][0]), *events)
        if self.hops < ring.half:
            self.got[-self.hops], self.got[self.hops] = [ring.send_up(up)], [ring.send_down(down)]
        elif self.split is None:
            self.got[ring.half] = [ring.send_up(up)]
        else:
            self.got[ring.half] = [ring.send_up(up[: self.split]), ring.send_down(down[self.split :])]

    def swap(self, *offsets):
        for o in offsets:
            if o not in self.far:
                self.far[o] = [self.ring.send_core(p) for p in self.got[o]]


def fence(*things):
    rings = [t for t in things if isinstance(t, Gather)]
    arrays = [t for t in things if not isinstance(t, Gather)]
    held, arrays = lax.optimization_barrier(([(r.got, r.far) for r in rings], arrays))
    for r, (got, far) in zip(rings, held, strict=True):
        r.got, r.far = got, far
    return arrays


class Scatter:
    def __init__(self, ring, own, far, split):
        self.ring, self.own, self.far, self.split = ring, own, far, split
        self.partner, self.left = {}, ring.half

    def swap(self, offsets, *events):
        got = self.ring.send_core(after(self.far[offsets[0]], *events))
        for i, o in enumerate(offsets):
            self.partner[o] = got[i]

    def hop(self, *events):
        ring, own, partner, split, s = self.ring, self.own, self.partner, self.split, self.left
        self.left -= 1
        if s == ring.half:
            first = total(own[s], partner[s])
            up, down = first[:split], first[split:]
        elif s == ring.half - 1:
            more = own[s].shape[0] - split
            up = total(own[s], partner[s], jnp.pad(self.up, ((0, more), (0, 0))))
            down = total(own[-s], partner[-s], jnp.pad(self.down, ((split, 0), (0, 0))))
        else:
            up, down = total(own[s], partner[s], self.up), total(own[-s], partner[-s], self.down)
        self.sent = up, down = after((up, down), *events)
        self.up, self.down = ring.send_up(up), ring.send_down(down)
        return self.up, self.down

    def step(self, *events):
        there = self.hop(*events)
        self.swap([-self.left, self.left] if self.left else [0], *self.sent)
        return there

    def terms(self):
        return self.own[0], self.partner[0], self.up, self.down


def dp_pairs(shift):
    n = lax.axis_size("dp")
    return [(i, (i + shift) % n) for i in range(n)]


def from_dp(x, shift):
    return lax.ppermute(x, "dp", dp_pairs(shift))


def on_device(
    inputs,
    cotangent,
    routes,
    attention_gain,
    query_weight,
    key_matrix,
    value_matrix,
    output_weight,
    mixture_gain,
    router_weight,
    gate_weight,
    up_weight,
    down_weight,
):
    seqs, _, length, _ = inputs.shape
    tokens = seqs * length
    topk = routes.shape[3]
    dp, experts = lax.axis_size("dp"), lax.axis_size("expert")
    assert gate_weight.shape[0] == 1 and experts % EXTRA == 0 and experts * 3 * tokens <= EXTRA * WIDTH * 2
    ring = Ring(experts)
    my_dp, me = lax.axis_index("dp"), lax.axis_index("expert")
    capacity = (5 * length * topk + 4 * experts - 1) // (4 * experts)
    slots = seqs * ((capacity + 7) // 8 * 8)
    x = inputs.reshape(tokens, WIDTH)
    g = cotangent.reshape(tokens, WIDTH)
    cos, sin = (jnp.asarray(t) for t in rope_tables(length))
    split = length
    where_i = jnp.stack([my_dp * experts + me, my_dp, me, jnp.full_like(me, dp)]).astype(jnp.int32)

    rows = query_weight.shape[0]
    misc = jnp.concatenate(
        [
            router_weight,
            attention_gain[:, None],
            mixture_gain[:, None],
            jnp.zeros((rows, LANES - experts - 2), bf16),
        ],
        axis=1,
    )
    dense_own = jnp.concatenate([query_weight, key_matrix, value_matrix, misc, output_weight.T], axis=1)
    g_ring = ring.gather(g, split)
    g_ring.hop()
    apart = dp == 2 and rows % 16 == 0
    if apart:
        table = jnp.asarray(ring.table(dp))
        far = from_dp(dense_own, 1)
        d_ring = ring.gather(jnp.stack([dense_own, far]), 1)
        d_ring.hop(g_ring.got[-1], g_ring.got[1])
        expert_start = (far,)
    else:
        table = jnp.zeros((dp * experts, 1), jnp.int32)
        both = lax.all_gather(dense_own, ("dp", "expert"), axis=0, tiled=True)
        dense = [both[None]]
        expert_start = (both,)

    hidden_size = gate_weight.shape[2]
    wide, narrow = WIDTH // dp, hidden_size // dp
    in_parts = dp == 2 and wide % LANES == 0 and narrow % LANES == 0
    if in_parts:
        flat = [jnp.concatenate([gate_weight[0], up_weight[0]], axis=1)]
        halves = [from_dp(after(flat[0], *expert_start), 1)]
        halves.append(from_dp(after(down_weight[0], *halves), 1))
        expert_weights = [gate_weight[0], up_weight[0], down_weight[0], *halves]
    else:
        expert_weights = [
            lax.all_gather(after(w[0], *expert_start), "dp", axis=0, tiled=True)
            for w in (gate_weight, up_weight, down_weight)
        ]
        flat, halves = [], []

    if apart:
        d_ring.hop(g_ring.got[-1], g_ring.got[1], *flat)
        while d_ring.hops < ring.half:
            d_ring.hop(*(halves[:1] if d_ring.hops == ring.half - 1 else ()))
        d_ring.swap(*ring.offsets)
        fence(d_ring, g_ring)
        dense = []
        for o in ring.offsets:
            dense += d_ring.got[o] + d_ring.far[o]
    g_ring.hop()

    w_full, o_t, misc_full, gains, n1, q, k, v, mixed, hidden, send, gate_values = call(
        functools.partial(forward_body, seqs, experts, len(dense)),
        [
            sds((WIDTH, MISC), bf16),
            sds((WIDTH, Q_COLS), bf16),
            sds((WIDTH, LANES), bf16),
            sds((8, WIDTH), f32),
            sds((tokens, WIDTH), bf16),
            sds((tokens, Q_COLS), bf16),
            sds((tokens, KV_COLS), bf16),
            sds((tokens, KV_COLS), bf16),
            sds((tokens, Q_COLS), bf16),
            sds((tokens, WIDTH), f32),
            sds((tokens + EXTRA, WIDTH), bf16),
            sds((tokens, LANES), f32),
        ],
        [smem(), smem()] + vmem(4 + len(dense)),
        [where_i, table, x, cos, sin, routes.reshape(tokens, topk), *dense],
        "forward",
        60,
    )

    n_ring = ring.gather(send, split)
    out_own, out_far, dx_own, dx_far = {}, {}, {}, {}
    kept = {}
    groups = [[0]] + [[-s, s] for s in range(1, ring.half)] + [[ring.half]]

    def pieces_of(group):
        return jnp.concatenate([p for o in group for r in (n_ring, g_ring) for p in r.got[o]])

    def experts_on(group, far, *events):
        args, arrays, offset = [far], [], 0
        for o in group:
            own, other = [], []
            for pieces in (n_ring.got[o], g_ring.got[o]):
                start, first = 0, len(args)
                own.append([])
                other.append([])
                for j, p in enumerate(pieces):
                    args.append(p)
                    own[-1].append((first + j, start, p.shape[0], 0))
                    other[-1].append((0, start, p.shape[0], offset))
                    start += p.shape[0]
                    offset += p.shape[0]
            arrays += [tuple(own), tuple(other)]
        count = len(arrays)
        rows_ = count * slots
        outs = call(
            functools.partial(expert_body, (arrays, len(args), 2 if in_parts else 1), capacity, slots, tokens, seqs),
            [sds((tokens, WIDTH), bf16)] * len(group)
            + [sds((tokens + EXTRA, WIDTH), bf16)] * len(group)
            + [sds((len(group), tokens, WIDTH), bf16), sds((len(group), tokens + EXTRA, WIDTH), bf16)]
            + [sds((rows_, WIDTH), bf16)] * 2
            + [sds((rows_, hidden_size), bf16)] * 3,
            [smem()] + vmem(len(args) + len(expert_weights)),
            [after(where_i, *events), *args, *expert_weights],
            "experts",
            36,
            [
                pltpu.VMEM((rows_, WIDTH), bf16),
                pltpu.VMEM((rows_, LANES), f32),
                pltpu.VMEM((rows_, hidden_size), f32),
                pltpu.VMEM((rows_, WIDTH), bf16),
            ],
        )
        n = len(group)
        for i, o in enumerate(group):
            out_own[o], dx_own[o] = outs[i], outs[n + i]
        out_far[group[0]], dx_far[group[0]] = outs[2 * n : 2 * n + 2]
        kept[group[0]] = outs[2 * n + 2 :]
        return kept[group[0]]

    waiting, _ = fence(pieces_of(groups[0]), expert_weights[-1], n_ring, g_ring)
    far = []
    for hop in range(1, ring.half + 1):
        n_ring.hop()
        if g_ring.hops < ring.half:
            g_ring.hop()
        near, far = far, ring.send_core(waiting)
        waiting = pieces_of(groups[hop])
        if hop > 1:
            group = groups[hop - 2]
            waiting, far, kept[group[0]] = fence(waiting, far, experts_on(group, near), n_ring, g_ring)
        else:
            waiting, far = fence(waiting, far, n_ring, g_ring)
    (last,) = fence(ring.send_core(waiting))
    experts_on(groups[-1], last)
    dx_ring = ring.scatter(dx_own, dx_far, split)
    dx_ring.swap(groups[-1])
    there = dx_ring.hop()
    experts_on(groups[-2], far, *dx_ring.sent)
    dx_ring.swap(groups[-2], *there)
    dx_ring.hop()
    dx_ring.swap(groups[-3], *dx_ring.sent)
    kept = [[kept[group[0]][i] for group in groups] for i in range(5)]

    saved = [a for k_ in kept for a in k_]
    if wide % LANES == 0 and narrow % LANES == 0:

        def part(shift, outs, more, *events):
            return call(
                functools.partial(weights_body, len(groups), (wide, narrow), shift, len(more)),
                outs,
                [smem()] + vmem(len(saved) + len(more)),
                [after(where_i, *events), *saved, *more],
                "expert_weights",
                36,
            )

        more = []
        for shift in range(1, dp):
            parts = part(
                shift, [sds((end - at, WIDTH), bf16) for at, end in chunk_edges(wide + narrow)], [], *dx_ring.sent, *more
            )
            for p in parts:
                more.append(from_dp(after(p, *more[-1:]), shift))
        weights_sent = (parts[0],)
    else:
        xs, dys, acts, dus, dws = (jnp.concatenate(k_) for k_ in kept)
        expert_grads = tuple(
            lax.psum_scatter(dot(a, b, 0, 0).astype(bf16), "dp", scatter_dimension=0, tiled=True).astype(f32)
            for a, b in ((xs, dus), (xs, dws), (acts, dys))
        )
        weights_sent, more = (), []
    dx_ring.step(*weights_sent)
    while dx_ring.left:
        dx_ring.step(*more[:1])
    dx_terms = dx_ring.terms()
    out_ring = ring.scatter(out_own, out_far, split)
    out_ring.swap(groups[-1], *dx_ring.sent)
    out_ring.step(*dx_terms[2:], *more[1:2])

    def block_outs(columns):
        return [sds((dp, ring.chips, rows, columns), bf16)] * 2

    dh, dmixed, router_part, gain_part, *o_part = call(
        functools.partial(hidden_back_body, experts, apart),
        [sds((tokens, WIDTH), f32), sds((tokens, Q_COLS), bf16), sds((WIDTH, LANES), f32), sds((8, WIDTH), f32)]
        + (block_outs(Q_COLS) if apart else [sds((WIDTH, Q_COLS), bf16)]),
        [smem(), smem()] + vmem(11),
        [after(where_i, *out_ring.sent), table, *dx_terms, g, hidden, gains, gate_values, misc_full, o_t, mixed],
        "hidden_back",
        36,
        [pltpu.VMEM((WIDTH, Q_COLS), bf16)] if apart else [],
    )
    out_ring.step(dh, *more[2:3])
    o_got = [ring.send_core(after(o_part[1], *out_ring.sent))] if apart else []
    input_grad, *qkv_part = call(
        functools.partial(attend_back_body, seqs, experts, apart),
        [sds((tokens, WIDTH), f32)]
        + (block_outs(MISC + LANES) if apart else [sds((WIDTH, MISC + LANES), bf16)]),
        [smem(), smem()] + vmem(13),
        [after(where_i, *out_ring.sent), table, x, cos, sin, w_full, gains, n1, q, k, v, dmixed, dh, router_part, gain_part],
        "attend_back",
        36,
        ([pltpu.VMEM((WIDTH, MISC + LANES), bf16)] if apart else []) + [pltpu.VMEM((tokens, MISC), bf16)],
    )

    out_ring.step(input_grad, *more, *o_got)
    if wide % LANES == 0 and narrow % LANES == 0:
        expert_grads = part(
            0, [sds((wide, hidden_size), f32)] * 2 + [sds((narrow, WIDTH), f32)], more, *out_ring.sent
        )
    gate_grad, up_grad, down_grad = expert_grads

    def over_y(keep, got, *events):
        far = from_dp(after(total(keep[1], got[1]), *events), 1)
        return total(keep[0], got[0], far)

    class Blocks:
        def __init__(self, both):
            self.term = {o: both[k_] for k_, o in enumerate(ring.offsets)}
            self.up, self.down, self.left = None, None, ring.half

        def hop(self, *events):
            s = self.left
            self.left -= 1
            up = self.term[s] if self.up is None else total(self.up, self.term[s])
            if s == ring.half:
                self.up = ring.send_up(after(up, *events))
                return (self.up,)
            down = self.term[-s] if self.down is None else total(self.down, self.term[-s])
            up, down = after((up, down), *events)
            self.up, self.down = ring.send_up(up), ring.send_down(down)
            return self.up, self.down

        def result(self):
            while self.left:
                self.hop()
            return self.up.astype(f32) + self.down.astype(f32) + self.term[0].astype(f32)

    if apart:
        qkv_got = ring.send_core(after(qkv_part[1], *out_ring.sent))
        o_sum = over_y(o_part[0], *o_got, *out_ring.sent)
        while out_ring.left:
            there = out_ring.step(gate_grad, o_sum, qkv_got)
        qkv_sum = over_y(qkv_part[0], qkv_got, *out_ring.sent)
        o_blocks, qkv_blocks = Blocks(o_sum), Blocks(qkv_sum)
        there += o_blocks.hop(*out_ring.sent)
        qkv_blocks.hop(*there)
        o_grad, qkv_grad = o_blocks.result(), qkv_blocks.result()
    else:
        while out_ring.left:
            out_ring.step()
        o_grad, qkv_grad = (
            lax.psum_scatter(p[0], ("dp", "expert"), scatter_dimension=0, tiled=True).astype(f32)
            for p in (o_part, qkv_part)
        )

    outputs = total(hidden, *out_ring.terms()).reshape(inputs.shape)
    return (
        outputs,
        input_grad.reshape(inputs.shape),
        qkv_grad[:, MISC + experts],
        qkv_grad[:, :Q_COLS],
        qkv_grad[:, Q_COLS : Q_COLS + KV_COLS],
        qkv_grad[:, Q_COLS + KV_COLS : MISC],
        o_grad.T,
        qkv_grad[:, MISC + experts + 1],
        qkv_grad[:, MISC : MISC + experts],
        gate_grad[None],
        up_grad[None],
        down_grad[None],
    )


def solution(mesh):
    both = ("dp", "expert")
    tokens = P(None, both, None, None)
    expert = P("expert", "dp", None)
    in_specs = (
        tokens,
        tokens,
        tokens,
        P(both),
        P(both, None),
        P(both, None),
        P(both, None),
        P(None, both),
        P(both),
        P(both, None),
        expert,
        expert,
        expert,
    )
    out_specs = (
        tokens,
        tokens,
        P(both),
        P(both, None),
        P(both, None),
        P(both, None),
        P(None, both),
        P(both),
        P(both, None),
        expert,
        expert,
        expert,
    )
    return jax.shard_map(on_device, mesh=mesh, in_specs=in_specs, out_specs=out_specs, check_vma=False)
```

```python
import functools
import math

import jax
import jax.numpy as jnp
import numpy as np
from jax import lax
from jax.experimental import pallas as pl
from jax.experimental.pallas import tpu as pltpu
from jax.sharding import PartitionSpec as P

WIDTH = 1536
QUERY_HEADS = 12
KEY_VALUE_HEADS = 2
HEAD = 128
GROUP = QUERY_HEADS // KEY_VALUE_HEADS
Q_COLS = QUERY_HEADS * HEAD
KV_COLS = KEY_VALUE_HEADS * HEAD
MISC = Q_COLS + 2 * KV_COLS
EXTRA = 16
LANES = 128
CHUNKS = (9, 9, 7, 11)
EPSILON = 1e-06
ROPE_BASE = 10000.0
MASKED = -1e30
SCALE = 1.0 / math.sqrt(HEAD)

f32 = jnp.float32
bf16 = jnp.bfloat16


def dot(a, b, ca=1, cb=0):
    return lax.dot_general(a, b, (((ca,), (cb,)), ((), ())), preferred_element_type=f32)


def vmem(n):
    return [pl.BlockSpec(memory_space=pltpu.VMEM)] * n


def smem():
    return pl.BlockSpec(memory_space=pltpu.SMEM)


def call(body, outs, ins, args, name, vmem_mb, scratch=()):
    return pl.pallas_call(
        body,
        out_shape=outs,
        in_specs=ins,
        out_specs=vmem(len(outs)),
        scratch_shapes=list(scratch),
        compiler_params=pltpu.CompilerParams(vmem_limit_bytes=vmem_mb * 1024 * 1024),
        cost_estimate=pl.CostEstimate(flops=1 << 20, bytes_accessed=1 << 20, transcendentals=0),
        name=name,
    )(*args)


def sds(shape, dtype):
    return jax.ShapeDtypeStruct(shape, dtype)


def rope_tables(length):
    half = HEAD // 2
    frequency = ROPE_BASE ** (-(np.arange(half, dtype=np.float64) * 2.0 / HEAD))
    angles = np.arange(length, dtype=np.float64)[:, None] * frequency[None, :]
    cos, sin = np.cos(angles), np.sin(angles)
    cosine = np.concatenate([cos, cos], axis=1).astype(np.float32)
    signed = np.concatenate([-sin, sin], axis=1).astype(np.float32)
    return cosine, signed


def place(where_ref, device, piece_refs, targets):
    at = 0
    for ref in piece_refs:
        blocks, rows, _ = ref.shape
        for j in range(blocks):
            start = pl.multiple_of(where_ref[device, at] * rows, 16 if rows % 16 == 0 else 8)
            for target, column in targets:
                target[pl.ds(start, rows), :] = ref[j, :, column : column + target.shape[1]]
            at += 1


def scale_of(z):
    return lax.rsqrt(jnp.mean(z * z, axis=-1, keepdims=True) + EPSILON)


def heads_of(ref, b, length, c):
    return jnp.concatenate(
        [ref[b * length : (b + 1) * length, h * HEAD : (h + 1) * HEAD] for h in range(c * GROUP, (c + 1) * GROUP)],
        axis=0,
    )


def causal_mask(length):
    row = lax.broadcasted_iota(jnp.int32, (length, length), 0)
    column = lax.broadcasted_iota(jnp.int32, (length, length), 1)
    return jnp.concatenate([row >= column] * GROUP, axis=0)


def softmax_of(q, k, keep):
    s = jnp.where(keep, dot(q, k, 1, 1) * SCALE, MASKED)
    e = jnp.exp(s - jnp.max(s, axis=-1, keepdims=True))
    return e / jnp.sum(e, axis=-1, keepdims=True)


def forward_body(seqs, experts, n_pieces, me_ref, where_ref, x_ref, cos_ref, sin_ref, routes_ref, *refs):
    pieces = refs[:n_pieces]
    w_ref, o_ref, misc_ref, gain_ref, n1_ref, q_ref, k_ref, v_ref, mixed_ref, hidden_ref, send_ref, gate_ref = refs[n_pieces:]
    length = x_ref.shape[0] // seqs
    place(where_ref, me_ref[0], pieces, ((w_ref, 0), (misc_ref, MISC), (o_ref, MISC + LANES)))
    gains = jnp.transpose(misc_ref[...].astype(f32))[experts : experts + 8]
    gain_ref[...] = gains
    x = x_ref[...].astype(f32)
    n1 = (x * scale_of(x) * gains[0:1]).astype(bf16)
    n1_ref[...] = n1
    cos = jnp.concatenate([cos_ref[...]] * seqs, axis=0)
    sin = jnp.concatenate([sin_ref[...]] * seqs, axis=0)

    def rotated(u):
        return (u * cos + pltpu.roll(u, HEAD // 2, 1) * sin).astype(bf16)

    kv = dot(n1, w_ref[:, Q_COLS:])
    v_ref[...] = kv[:, KV_COLS:].astype(bf16)
    for c in range(KEY_VALUE_HEADS):
        k_ref[:, c * HEAD : (c + 1) * HEAD] = rotated(kv[:, c * HEAD : (c + 1) * HEAD])
    keep = causal_mask(length)
    for c in range(KEY_VALUE_HEADS):
        cols = GROUP * HEAD
        q = dot(n1, w_ref[:, c * cols : (c + 1) * cols])
        for h in range(GROUP):
            at = c * cols + h * HEAD
            q_ref[:, at : at + HEAD] = rotated(q[:, h * HEAD : (h + 1) * HEAD])
        for b in range(seqs):
            rows = slice(b * length, (b + 1) * length)
            k = k_ref[rows, c * HEAD : (c + 1) * HEAD]
            v = v_ref[rows, c * HEAD : (c + 1) * HEAD]
            p = softmax_of(heads_of(q_ref, b, length, c), k, keep).astype(bf16)
            o = dot(p, v).astype(bf16)
            for h in range(GROUP):
                at = c * cols + h * HEAD
                mixed_ref[rows, at : at + HEAD] = o[h * length : (h + 1) * length]
    tokens = x_ref.shape[0]
    h = x + dot(mixed_ref[...], o_ref[...], 1, 1)
    hidden_ref[...] = h
    n2 = (h * scale_of(h) * gains[1:2]).astype(bf16)
    send_ref[0:tokens] = n2
    z = dot(n2, misc_ref[...])
    lane = lax.broadcasted_iota(jnp.int32, (tokens, LANES), 1)
    chosen = lane == routes_ref[:, 0:1]
    for j in range(1, routes_ref.shape[1]):
        chosen = chosen | (lane == routes_ref[:, j : j + 1])
    top = jnp.max(jnp.where(chosen, z, MASKED), axis=-1, keepdims=True)
    e = jnp.where(chosen, jnp.exp(jnp.where(chosen, z - top, 0.0)), 0.0)
    gate = e / jnp.sum(e, axis=-1, keepdims=True)
    gate_ref[...] = gate
    high = gate.astype(bf16).astype(f32)
    tables = [jnp.transpose(t) for t in (high, gate - high, chosen.astype(f32))]
    blank = jnp.zeros((EXTRA, tokens), f32)
    parts = []
    for first in range(0, experts, EXTRA):
        parts += [t[first : first + EXTRA] for t in tables]
    parts += [blank] * (WIDTH // tokens - len(parts))
    send_ref[tokens:] = jnp.concatenate(parts, axis=1).astype(bf16)


def expert_body(layout, capacity, slots, tokens, seqs, me_ref, *refs):
    arrays, n_in, parts_in = layout
    count = len(arrays)
    ins = refs[:n_in]
    if parts_in == 1:
        weights = [tuple(refs[n_in : n_in + 3])]
        outs = refs[n_in + 3 :]
    else:
        gate_ref, up_ref, down_ref, far_ref, far_down_ref = refs[n_in : n_in + 5]
        hidden = gate_ref.shape[1]
        weights = [
            (gate_ref, up_ref, down_ref),
            (far_ref.at[:, 0:hidden], far_ref.at[:, hidden : 2 * hidden], far_down_ref),
        ]
        outs = refs[n_in + 5 :]
    deep, narrow = weights[0][0].shape[0], weights[0][2].shape[0]
    if parts_in == 1:
        spans = [(slice(0, deep), slice(0, narrow))]
    else:
        spans = [
            (pl.ds(pl.multiple_of(p * deep, LANES), deep), pl.ds(pl.multiple_of(p * narrow, LANES), narrow))
            for p in (me_ref[1], 1 - me_ref[1])
        ]
    half = count // 2
    far_out, far_dx = outs[2 * half : 2 * half + 2]
    out_refs, dx_refs = [], []
    for j in range(half):
        out_refs += [outs[j], far_out.at[j]]
        dx_refs += [outs[half + j], far_dx.at[j]]
    xs_ref, dy_ref, act_ref, du_ref, dw_ref, gs_ref, gcol_ref, dact_ref, dx_ref = outs[2 * half + 2 :]
    length = tokens // seqs
    me = me_ref[2]
    row_in = lax.rem(me, EXTRA)
    row = lax.broadcasted_iota(jnp.int32, (EXTRA, tokens), 0)
    mine = row == row_in
    block = lax.div(me, EXTRA)

    def table(extra, k):
        t = jnp.zeros((EXTRA, tokens), f32)
        for b in range(WIDTH // (3 * tokens)):
            at = (3 * b + k) * tokens
            t = jnp.where(block == b, extra[:, at : at + tokens].astype(f32), t)
        return jnp.sum(jnp.where(mine, t, 0.0), axis=0, keepdims=True)

    def read(pieces, first, rows):
        got = []
        for index, start, size, offset in pieces:
            lo, hi = max(first, start), min(first + rows, start + size)
            if lo < hi:
                got.append(ins[index][offset + lo - start : offset + hi - start])
        return got[0] if len(got) == 1 else jnp.concatenate(got, axis=0)

    tri_a = lax.broadcasted_iota(jnp.int32, (length, length), 0)
    tri_b = lax.broadcasted_iota(jnp.int32, (length, length), 1)
    before = (tri_a < tri_b).astype(bf16)
    slot = lax.broadcasted_iota(jnp.int32, (slots, tokens), 0).astype(f32)
    gates, masks = [], []
    for n2_pieces, _ in arrays:
        extra = read(n2_pieces, tokens, EXTRA)
        gates.append(table(extra, 0) + table(extra, 1))
        masks.append(table(extra, 2))
    picks = []
    for i, (n2_pieces, g_pieces) in enumerate(arrays):
        at = []
        for b in range(seqs):
            m = masks[i][:, b * length : (b + 1) * length]
            earlier = dot(jnp.broadcast_to(m, (16, length)).astype(bf16), before)[0:1]
            keep = (m > 0.5) & (earlier < capacity)
            at.append(jnp.where(keep, earlier + b * (slots // seqs), -1.0))
        pick = (slot == jnp.concatenate(at, axis=1)).astype(f32)
        gcol_ref[i * slots : (i + 1) * slots, :] = jnp.broadcast_to(
            jnp.sum(pick * gates[i], axis=1, keepdims=True), (slots, LANES)
        )
        pick = pick.astype(bf16)
        picks.append(pick)
        rows = slice(i * slots, (i + 1) * slots)
        xs_ref[rows, :] = dot(pick, read(n2_pieces, 0, tokens)).astype(bf16)
        gs_ref[rows, :] = dot(pick, read(g_pieces, 0, tokens)).astype(bf16)
    u = w = y = None
    for (gate_part, up_part, _), (rows, _) in zip(weights, spans, strict=True):
        xs = xs_ref[:, rows]
        more_u, more_w = dot(xs, gate_part[...]), dot(xs, up_part[...])
        u, w = (more_u, more_w) if u is None else (u + more_u, w + more_w)
    s = 1.0 / (1.0 + jnp.exp(-u))
    act_ref[...] = (u * s * w).astype(bf16)
    for (_, _, down_part), (_, rows) in zip(weights, spans, strict=True):
        more = dot(act_ref[:, rows], down_part[...])
        y = more if y is None else y + more
    y = y.astype(bf16).astype(f32)
    gcol = gcol_ref[:, 0:1]
    gs = gs_ref[...].astype(f32)
    dy = (gcol * gs).astype(bf16)
    dy_ref[...] = dy
    dg = jnp.sum(gs * y, axis=1, keepdims=True)
    weighted = (gcol * y).astype(bf16)
    for (_, _, down_part), (_, rows) in zip(weights, spans, strict=True):
        dact_ref[:, rows] = dot(dy, down_part[...], 1, 1)
    dact = dact_ref[...]
    du = (dact * w * s * (1.0 + u * (1.0 - s))).astype(bf16)
    dw = (dact * (u * s)).astype(bf16)
    du_ref[...] = du
    dw_ref[...] = dw
    for (gate_part, up_part, _), (rows, _) in zip(weights, spans, strict=True):
        dx_ref[:, rows] = (dot(du, gate_part[...], 1, 1) + dot(dw, up_part[...], 1, 1)).astype(bf16)
    dx = dx_ref[...]
    for i in range(count):
        rows = slice(i * slots, (i + 1) * slots)
        out_refs[i][...] = dot(picks[i], weighted[rows], 0, 0).astype(bf16)
        dx_refs[i][0:tokens] = dot(picks[i], dx[rows], 0, 0).astype(bf16)
        back = jnp.sum(picks[i].astype(f32) * dg[rows], axis=0, keepdims=True)
        high = back.astype(bf16).astype(f32)
        blank = jnp.zeros((EXTRA, tokens), f32)
        parts = []
        for b in range(WIDTH // (3 * tokens)):
            here = mine & (block == b)
            parts += [jnp.where(here, high, 0.0), jnp.where(here, back - high, 0.0), blank]
        dx_refs[i][tokens:] = jnp.concatenate(parts, axis=1).astype(bf16)


def chunk_edges(rows):
    unit, at, edges = rows // sum(CHUNKS), 0, []
    for c in CHUNKS:
        edges.append((at, at + c * unit))
        at += c * unit
    return edges


def weights_body(n, half, shift, adds, me_ref, *refs):
    lists = [refs[k * n : (k + 1) * n] for k in range(5)]
    xs, dys, acts, dus, dws = lists
    more = refs[5 * n : 5 * n + adds]
    outs = refs[5 * n + adds :]
    wide, narrow = half
    index = lax.rem(me_ref[1] + shift, me_ref[3])
    x_at = pl.multiple_of(index * wide, LANES)
    a_at = pl.multiple_of(index * narrow, LANES)
    totals = [None, None, None]
    for i in range(n):
        x = xs[i][:, pl.ds(x_at, wide)]
        a = acts[i][:, pl.ds(a_at, narrow)]
        for k, (left, right) in enumerate(((x, dus[i]), (x, dws[i]), (a, dys[i]))):
            now = dot(left, right[...], 0, 0)
            totals[k] = now if totals[k] is None else totals[k] + now
    hidden = totals[0].shape[1]
    columns = (slice(0, hidden), slice(hidden, 2 * hidden), slice(None))
    chunks = outs if shift else more
    edges = chunk_edges(wide + narrow)
    for k, c in enumerate(columns):
        base, size = (wide, narrow) if k == 2 else (0, wide)
        for j, ref in enumerate(chunks):
            first, end = edges[j % len(CHUNKS)]
            lo, hi = max(first, base), min(end, base + size)
            if lo < hi and shift:
                ref[lo - first : hi - first, c] = totals[k][lo - base : hi - base].astype(bf16)
            elif lo < hi and j < len(CHUNKS):
                value = totals[k][lo - base : hi - base]
                for other in chunks[j :: len(CHUNKS)]:
                    value = value + other[lo - first : hi - first, c].astype(f32)
                outs[k][lo - base : hi - base] = value


def blocks_out(where_ref, device, whole_ref, outs):
    keep_ref, send_ref = outs
    sides, count, rows, _ = keep_ref.shape
    for lane, out in enumerate((keep_ref, send_ref)):
        for side in range(sides):
            for k in range(count):
                at = where_ref[device, (2 * k + lane) * sides + side]
                out[side, k] = whole_ref[pl.ds(pl.multiple_of(at * rows, 16), rows), :]


def norm_back(up, hat, scale, gain):
    w = up * gain
    return scale * (w - hat * jnp.mean(w * hat, axis=-1, keepdims=True)), jnp.sum(up * hat, axis=0, keepdims=True)


def hidden_back_body(experts, apart, me_ref, where_ref, a_ref, b_ref, c_ref, d_ref, g_ref, hidden_ref, gain_ref, gate_ref, misc_ref, o_ref, mixed_ref, *outs):
    dh_ref, dmixed_ref, rg_ref, gg_ref, og_ref = outs[:4] + outs[-1:]
    tokens = g_ref.shape[0]
    got = a_ref[...].astype(f32) + b_ref[...].astype(f32) + c_ref[...].astype(f32) + d_ref[...].astype(f32)
    extra = got[tokens:]
    rows = []
    for first in range(experts // EXTRA):
        at = 3 * first * tokens
        rows.append(extra[:, at : at + tokens] + extra[:, at + tokens : at + 2 * tokens])
    rows.append(jnp.zeros((LANES - experts, tokens), f32))
    dg = jnp.transpose(jnp.concatenate(rows, axis=0))
    gate = gate_ref[...]
    dl = gate * (dg - jnp.sum(gate * dg, axis=-1, keepdims=True))
    dz = dl.astype(bf16)
    dn = got[0:tokens] + dot(dz, misc_ref[...], 1, 1)
    h = hidden_ref[...]
    scale = scale_of(h)
    hat = h * scale
    gain = gain_ref[1:2]
    n2 = (hat * gain).astype(bf16)
    rg_ref[...] = dot(n2, dz, 0, 0)
    back, grad = norm_back(dn, hat, scale, gain)
    gg_ref[...] = jnp.broadcast_to(grad, gg_ref.shape)
    dh = g_ref[...].astype(f32) + back
    dh_ref[...] = dh
    da = dh.astype(bf16)
    dmixed_ref[...] = dot(da, o_ref[...]).astype(bf16)
    og_ref[...] = dot(da, mixed_ref[...], 0, 0).astype(bf16)
    if apart:
        blocks_out(where_ref, me_ref[0], og_ref, outs[4:6])


def attend_back_body(seqs, experts, apart, me_ref, where_ref, x_ref, cos_ref, sin_ref, w_ref, gain_ref, n1_ref, q_ref, k_ref, v_ref, do_ref, dh_ref, rg_ref, gg_ref, dx_ref, *outs):
    wg_ref, dqkv_ref = outs[-2:]
    length = x_ref.shape[0] // seqs
    cos = cos_ref[...]
    sin = sin_ref[...]
    keep = causal_mask(length)

    def back(u):
        return (u * cos - pltpu.roll(u, HEAD // 2, 1) * sin).astype(bf16)

    for b in range(seqs):
        rows = slice(b * length, (b + 1) * length)
        for c in range(KEY_VALUE_HEADS):
            cols = slice(c * HEAD, (c + 1) * HEAD)
            k = k_ref[rows, cols]
            v = v_ref[rows, cols]
            q = heads_of(q_ref, b, length, c)
            do = heads_of(do_ref, b, length, c)
            p = softmax_of(q, k, keep)
            dqkv_ref[rows, Q_COLS + KV_COLS + c * HEAD : Q_COLS + KV_COLS + (c + 1) * HEAD] = dot(
                p.astype(bf16), do, 0, 0
            ).astype(bf16)
            dp = dot(do, v, 1, 1)
            ds = (p * (dp - jnp.sum(p * dp, axis=-1, keepdims=True))).astype(bf16)
            dq = dot(ds, k) * SCALE
            for h in range(GROUP):
                at = (c * GROUP + h) * HEAD
                dqkv_ref[rows, at : at + HEAD] = back(dq[h * length : (h + 1) * length])
            dqkv_ref[rows, Q_COLS + c * HEAD : Q_COLS + (c + 1) * HEAD] = back(dot(ds, q, 0, 0) * SCALE)
    dqkv = dqkv_ref[...]
    wg_ref[:, 0:MISC] = dot(n1_ref[...], dqkv, 0, 0).astype(bf16)
    dn = dot(dqkv, w_ref[...], 1, 1)
    x = x_ref[...].astype(f32)
    scale = scale_of(x)
    back_x, grad = norm_back(dn, x * scale, scale, gain_ref[0:1])
    dx_ref[...] = dh_ref[...] + back_x
    row = lax.broadcasted_iota(jnp.int32, (LANES, x.shape[1]), 0)
    gains = jnp.where(row == experts, grad, jnp.where(row == experts + 1, gg_ref[0:1], 0.0))
    wg_ref[:, MISC:] = (rg_ref[...] + jnp.transpose(gains)).astype(bf16)
    if apart:
        blocks_out(where_ref, me_ref[0], wg_ref, outs[:2])


def chip_ring(chips):
    if chips % 4 or chips < 8:
        return list(range(chips))
    high, low = 4, chips // 4
    order = [a * low for a in range(high)]
    for step, a in enumerate(reversed(range(high))):
        rest = list(range(1, low))
        order += [a * low + b for b in (rest if step % 2 == 0 else reversed(rest))]
    return order


class Ring:
    def __init__(self, devices):
        self.devices = devices
        self.chips = devices // 2
        self.half = self.chips // 2
        self.order = chip_ring(self.chips)
        n = self.chips
        self.up = [
            (2 * self.order[p] + lane, 2 * self.order[(p + 1) % n] + lane) for p in range(n) for lane in (0, 1)
        ]
        self.down = [(b, a) for a, b in self.up]
        self.across = [
            (2 * self.order[p] + lane, 2 * self.order[(p + self.half) % n] + lane) for p in range(n) for lane in (0, 1)
        ]
        self.swap = [(d, d ^ 1) for d in range(devices)]
        self.place = np.argsort(np.array(self.order)).astype(np.int32)
        self.offsets = [0] + [s * o for o in range(1, self.half) for s in (-1, 1)] + [self.half]

    def send_up(self, x):
        return lax.ppermute(x, "expert", self.up)

    def send_down(self, x):
        return lax.ppermute(x, "expert", self.down)

    def send_core(self, x):
        return lax.ppermute(x, "expert", self.swap)

    def table(self, dp):
        rows = []
        for y in range(dp):
            for e in range(self.devices):
                row = []
                for o in self.offsets:
                    chip = self.order[(int(self.place[e // 2]) + o) % self.chips]
                    for lane in (e % 2, 1 - e % 2):
                        row += [y * self.devices + 2 * chip + lane, (1 - y) * self.devices + 2 * chip + lane]
                rows.append(row)
        return np.array(rows, np.int32)

    def gather(self, x, split=None):
        return Gather(self, x, split)

    def scatter(self, own, far, split):
        return Scatter(self, own, far, split)


def after(x, *events):
    return lax.optimization_barrier((x, events))[0] if events else x


def total(*terms):
    out = terms[0].astype(f32)
    for t in terms[1:]:
        out = out + t.astype(f32)
    return out.astype(bf16)


class Gather:
    def __init__(self, ring, x, split):
        self.ring, self.split = ring, split
        self.got, self.far = {0: [x]}, {}
        self.hops = 0

    def hop(self, *events):
        ring, s = self.ring, self.hops
        self.hops += 1
        up, down = after((self.got[-s][0], self.got[s][0]), *events)
        if self.hops < ring.half:
            self.got[-self.hops], self.got[self.hops] = [ring.send_up(up)], [ring.send_down(down)]
        elif self.split is None:
            self.got[ring.half] = [ring.send_up(up)]
        else:
            self.got[ring.half] = [ring.send_up(up[: self.split]), ring.send_down(down[self.split :])]

    def swap(self, *offsets):
        for o in offsets:
            if o not in self.far:
                self.far[o] = [self.ring.send_core(p) for p in self.got[o]]


def fence(*things):
    rings = [t for t in things if isinstance(t, Gather)]
    arrays = [t for t in things if not isinstance(t, Gather)]
    held, arrays = lax.optimization_barrier(([(r.got, r.far) for r in rings], arrays))
    for r, (got, far) in zip(rings, held, strict=True):
        r.got, r.far = got, far
    return arrays


class Scatter:
    def __init__(self, ring, own, far, split):
        self.ring, self.own, self.far, self.split = ring, own, far, split
        self.partner, self.left = {}, ring.half

    def swap(self, offsets, *events):
        got = self.ring.send_core(after(self.far[offsets[0]], *events))
        for i, o in enumerate(offsets):
            self.partner[o] = got[i]

    def hop(self, *events):
        ring, own, partner, split, s = self.ring, self.own, self.partner, self.split, self.left
        self.left -= 1
        if s == ring.half:
            first = total(own[s], partner[s])
            up, down = first[:split], first[split:]
        elif s == ring.half - 1:
            more = own[s].shape[0] - split
            up = total(own[s], partner[s], jnp.pad(self.up, ((0, more), (0, 0))))
            down = total(own[-s], partner[-s], jnp.pad(self.down, ((split, 0), (0, 0))))
        else:
            up, down = total(own[s], partner[s], self.up), total(own[-s], partner[-s], self.down)
        self.sent = up, down = after((up, down), *events)
        self.up, self.down = ring.send_up(up), ring.send_down(down)
        return self.up, self.down

    def step(self, *events):
        there = self.hop(*events)
        self.swap([-self.left, self.left] if self.left else [0], *self.sent)
        return there

    def terms(self):
        return self.own[0], self.partner[0], self.up, self.down


def dp_pairs(shift):
    n = lax.axis_size("dp")
    return [(i, (i + shift) % n) for i in range(n)]


def from_dp(x, shift):
    return lax.ppermute(x, "dp", dp_pairs(shift))


def on_device(
    inputs,
    cotangent,
    routes,
    attention_gain,
    query_weight,
    key_matrix,
    value_matrix,
    output_weight,
    mixture_gain,
    router_weight,
    gate_weight,
    up_weight,
    down_weight,
):
    seqs, _, length, _ = inputs.shape
    tokens = seqs * length
    topk = routes.shape[3]
    dp, experts = lax.axis_size("dp"), lax.axis_size("expert")
    assert gate_weight.shape[0] == 1 and experts % EXTRA == 0 and experts * 3 * tokens <= EXTRA * WIDTH * 2
    ring = Ring(experts)
    my_dp, me = lax.axis_index("dp"), lax.axis_index("expert")
    capacity = (5 * length * topk + 4 * experts - 1) // (4 * experts)
    slots = seqs * ((capacity + 7) // 8 * 8)
    x = inputs.reshape(tokens, WIDTH)
    g = cotangent.reshape(tokens, WIDTH)
    cos, sin = (jnp.asarray(t) for t in rope_tables(length))
    split = length
    where_i = jnp.stack([my_dp * experts + me, my_dp, me, jnp.full_like(me, dp)]).astype(jnp.int32)

    rows = query_weight.shape[0]
    misc = jnp.concatenate(
        [
            router_weight,
            attention_gain[:, None],
            mixture_gain[:, None],
            jnp.zeros((rows, LANES - experts - 2), bf16),
        ],
        axis=1,
    )
    dense_own = jnp.concatenate([query_weight, key_matrix, value_matrix, misc, output_weight.T], axis=1)
    g_ring = ring.gather(g, split)
    g_ring.hop()
    apart = dp == 2 and rows % 16 == 0
    if apart:
        table = jnp.asarray(ring.table(dp))
        far = from_dp(dense_own, 1)
        d_ring = ring.gather(jnp.stack([dense_own, far]), 1)
        d_ring.hop(g_ring.got[-1], g_ring.got[1])
        expert_start = (far,)
    else:
        table = jnp.zeros((dp * experts, 1), jnp.int32)
        both = lax.all_gather(dense_own, ("dp", "expert"), axis=0, tiled=True)
        dense = [both[None]]
        expert_start = (both,)

    hidden_size = gate_weight.shape[2]
    wide, narrow = WIDTH // dp, hidden_size // dp
    in_parts = dp == 2 and wide % LANES == 0 and narrow % LANES == 0
    if in_parts:
        flat = [jnp.concatenate([gate_weight[0], up_weight[0]], axis=1)]
        halves = [from_dp(after(flat[0], *expert_start), 1)]
        halves.append(from_dp(after(down_weight[0], *halves), 1))
        expert_weights = [gate_weight[0], up_weight[0], down_weight[0], *halves]
    else:
        expert_weights = [
            lax.all_gather(after(w[0], *expert_start), "dp", axis=0, tiled=True)
            for w in (gate_weight, up_weight, down_weight)
        ]
        flat, halves = [], []

    if apart:
        d_ring.hop(g_ring.got[-1], g_ring.got[1], *flat)
        while d_ring.hops < ring.half:
            d_ring.hop(*(halves[:1] if d_ring.hops == ring.half - 1 else ()))
        d_ring.swap(*ring.offsets)
        fence(d_ring, g_ring)
        dense = []
        for o in ring.offsets:
            dense += d_ring.got[o] + d_ring.far[o]
    g_ring.hop()

    w_full, o_t, misc_full, gains, n1, q, k, v, mixed, hidden, send, gate_values = call(
        functools.partial(forward_body, seqs, experts, len(dense)),
        [
            sds((WIDTH, MISC), bf16),
            sds((WIDTH, Q_COLS), bf16),
            sds((WIDTH, LANES), bf16),
            sds((8, WIDTH), f32),
            sds((tokens, WIDTH), bf16),
            sds((tokens, Q_COLS), bf16),
            sds((tokens, KV_COLS), bf16),
            sds((tokens, KV_COLS), bf16),
            sds((tokens, Q_COLS), bf16),
            sds((tokens, WIDTH), f32),
            sds((tokens + EXTRA, WIDTH), bf16),
            sds((tokens, LANES), f32),
        ],
        [smem(), smem()] + vmem(4 + len(dense)),
        [where_i, table, x, cos, sin, routes.reshape(tokens, topk), *dense],
        "forward",
        60,
    )

    n_ring = ring.gather(send, split)
    out_own, out_far, dx_own, dx_far = {}, {}, {}, {}
    kept = {}
    groups = [[0]] + [[-s, s] for s in range(1, ring.half)] + [[ring.half]]

    def pieces_of(group):
        return jnp.concatenate([p for o in group for r in (n_ring, g_ring) for p in r.got[o]])

    def experts_on(group, far, *events):
        args, arrays, offset = [far], [], 0
        for o in group:
            own, other = [], []
            for pieces in (n_ring.got[o], g_ring.got[o]):
                start, first = 0, len(args)
                own.append([])
                other.append([])
                for j, p in enumerate(pieces):
                    args.append(p)
                    own[-1].append((first + j, start, p.shape[0], 0))
                    other[-1].append((0, start, p.shape[0], offset))
                    start += p.shape[0]
                    offset += p.shape[0]
            arrays += [tuple(own), tuple(other)]
        count = len(arrays)
        rows_ = count * slots
        outs = call(
            functools.partial(expert_body, (arrays, len(args), 2 if in_parts else 1), capacity, slots, tokens, seqs),
            [sds((tokens, WIDTH), bf16)] * len(group)
            + [sds((tokens + EXTRA, WIDTH), bf16)] * len(group)
            + [sds((len(group), tokens, WIDTH), bf16), sds((len(group), tokens + EXTRA, WIDTH), bf16)]
            + [sds((rows_, WIDTH), bf16)] * 2
            + [sds((rows_, hidden_size), bf16)] * 3,
            [smem()] + vmem(len(args) + len(expert_weights)),
            [after(where_i, *events), *args, *expert_weights],
            "experts",
            36,
            [
                pltpu.VMEM((rows_, WIDTH), bf16),
                pltpu.VMEM((rows_, LANES), f32),
                pltpu.VMEM((rows_, hidden_size), f32),
                pltpu.VMEM((rows_, WIDTH), bf16),
            ],
        )
        n = len(group)
        for i, o in enumerate(group):
            out_own[o], dx_own[o] = outs[i], outs[n + i]
        out_far[group[0]], dx_far[group[0]] = outs[2 * n : 2 * n + 2]
        kept[group[0]] = outs[2 * n + 2 :]
        return kept[group[0]]

    waiting, _ = fence(pieces_of(groups[0]), expert_weights[-1], n_ring, g_ring)
    far = []
    for hop in range(1, ring.half + 1):
        n_ring.hop()
        if g_ring.hops < ring.half:
            g_ring.hop()
        near, far = far, ring.send_core(waiting)
        waiting = pieces_of(groups[hop])
        if hop > 1:
            group = groups[hop - 2]
            waiting, far, kept[group[0]] = fence(waiting, far, experts_on(group, near), n_ring, g_ring)
        else:
            waiting, far = fence(waiting, far, n_ring, g_ring)
    (last,) = fence(ring.send_core(waiting))
    experts_on(groups[-1], last)
    dx_ring = ring.scatter(dx_own, dx_far, split)
    dx_ring.swap(groups[-1])
    there = dx_ring.hop()
    experts_on(groups[-2], far, *dx_ring.sent)
    dx_ring.swap(groups[-2], *there)
    dx_ring.hop()
    dx_ring.swap(groups[-3], *dx_ring.sent)
    kept = [[kept[group[0]][i] for group in groups] for i in range(5)]

    saved = [a for k_ in kept for a in k_]
    if wide % LANES == 0 and narrow % LANES == 0:

        def part(shift, outs, more, *events):
            return call(
                functools.partial(weights_body, len(groups), (wide, narrow), shift, len(more)),
                outs,
                [smem()] + vmem(len(saved) + len(more)),
                [after(where_i, *events), *saved, *more],
                "expert_weights",
                36,
            )

        more = []
        for shift in range(1, dp):
            parts = part(
                shift, [sds((end - at, WIDTH), bf16) for at, end in chunk_edges(wide + narrow)], [], *dx_ring.sent, *more
            )
            for p in parts:
                more.append(from_dp(after(p, *more[-1:]), shift))
        weights_sent = (parts[0],)
    else:
        xs, dys, acts, dus, dws = (jnp.concatenate(k_) for k_ in kept)
        expert_grads = tuple(
            lax.psum_scatter(dot(a, b, 0, 0).astype(bf16), "dp", scatter_dimension=0, tiled=True).astype(f32)
            for a, b in ((xs, dus), (xs, dws), (acts, dys))
        )
        weights_sent, more = (), []
    dx_ring.step(*weights_sent)
    while dx_ring.left:
        dx_ring.step(*more[:1])
    dx_terms = dx_ring.terms()
    out_ring = ring.scatter(out_own, out_far, split)
    out_ring.swap(groups[-1], *dx_ring.sent)
    out_ring.step(*dx_terms[2:], *more[1:2])

    def block_outs(columns):
        return [sds((dp, ring.chips, rows, columns), bf16)] * 2

    dh, dmixed, router_part, gain_part, *o_part = call(
        functools.partial(hidden_back_body, experts, apart),
        [sds((tokens, WIDTH), f32), sds((tokens, Q_COLS), bf16), sds((WIDTH, LANES), f32), sds((8, WIDTH), f32)]
        + (block_outs(Q_COLS) if apart else [sds((WIDTH, Q_COLS), bf16)]),
        [smem(), smem()] + vmem(11),
        [after(where_i, *out_ring.sent), table, *dx_terms, g, hidden, gains, gate_values, misc_full, o_t, mixed],
        "hidden_back",
        36,
        [pltpu.VMEM((WIDTH, Q_COLS), bf16)] if apart else [],
    )
    out_ring.step(dh, *more[2:3])
    o_got = [ring.send_core(after(o_part[1], *out_ring.sent))] if apart else []
    input_grad, *qkv_part = call(
        functools.partial(attend_back_body, seqs, experts, apart),
        [sds((tokens, WIDTH), f32)]
        + (block_outs(MISC + LANES) if apart else [sds((WIDTH, MISC + LANES), bf16)]),
        [smem(), smem()] + vmem(13),
        [after(where_i, *out_ring.sent), table, x, cos, sin, w_full, gains, n1, q, k, v, dmixed, dh, router_part, gain_part],
        "attend_back",
        36,
        ([pltpu.VMEM((WIDTH, MISC + LANES), bf16)] if apart else []) + [pltpu.VMEM((tokens, MISC), bf16)],
    )

    out_ring.step(input_grad, *more, *o_got)
    if wide % LANES == 0 and narrow % LANES == 0:
        expert_grads = part(
            0, [sds((wide, hidden_size), f32)] * 2 + [sds((narrow, WIDTH), f32)], more, *out_ring.sent
        )
    gate_grad, up_grad, down_grad = expert_grads

    def over_y(keep, got, *events):
        far = from_dp(after(total(keep[1], got[1]), *events), 1)
        return total(keep[0], got[0], far)

    class Blocks:
        def __init__(self, both, across=()):
            self.term = {o: both[k_] for k_, o in enumerate(ring.offsets)}
            self.up, self.down, self.left = None, None, ring.half
            self.across = []
            if across:
                self.left -= 1
                self.across = [lax.ppermute(after(self.term[ring.half], *across), "expert", ring.across)]

        def hop(self, *events):
            s = self.left
            self.left -= 1
            up = self.term[s] if self.up is None else total(self.up, self.term[s])
            if s == ring.half:
                self.up = ring.send_up(after(up, *events))
                return (self.up,)
            down = self.term[-s] if self.down is None else total(self.down, self.term[-s])
            up, down = after((up, down), *events)
            self.up, self.down = ring.send_up(up), ring.send_down(down)
            return self.up, self.down

        def result(self):
            while self.left:
                self.hop(*(self.across if self.left == 1 else ()))
            out = self.up.astype(f32) + self.down.astype(f32) + self.term[0].astype(f32)
            for more_ in self.across:
                out = out + more_.astype(f32)
            return out

    if apart:
        qkv_got = ring.send_core(after(qkv_part[1], *out_ring.sent))
        o_sum = over_y(o_part[0], *o_got, *out_ring.sent)
        while out_ring.left:
            there = out_ring.step(gate_grad, o_sum, qkv_got)
        qkv_sum = over_y(qkv_part[0], qkv_got, *out_ring.sent)
        o_blocks = Blocks(o_sum)
        there += o_blocks.hop(*out_ring.sent)
        qkv_blocks = Blocks(qkv_sum, there)
        qkv_blocks.hop(*there)
        o_grad, qkv_grad = o_blocks.result(), qkv_blocks.result()
    else:
        while out_ring.left:
            out_ring.step()
        o_grad, qkv_grad = (
            lax.psum_scatter(p[0], ("dp", "expert"), scatter_dimension=0, tiled=True).astype(f32)
            for p in (o_part, qkv_part)
        )

    outputs = total(hidden, *out_ring.terms()).reshape(inputs.shape)
    return (
        outputs,
        input_grad.reshape(inputs.shape),
        qkv_grad[:, MISC + experts],
        qkv_grad[:, :Q_COLS],
        qkv_grad[:, Q_COLS : Q_COLS + KV_COLS],
        qkv_grad[:, Q_COLS + KV_COLS : MISC],
        o_grad.T,
        qkv_grad[:, MISC + experts + 1],
        qkv_grad[:, MISC : MISC + experts],
        gate_grad[None],
        up_grad[None],
        down_grad[None],
    )


def solution(mesh):
    both = ("dp", "expert")
    tokens = P(None, both, None, None)
    expert = P("expert", "dp", None)
    in_specs = (
        tokens,
        tokens,
        tokens,
        P(both),
        P(both, None),
        P(both, None),
        P(both, None),
        P(None, both),
        P(both),
        P(both, None),
        expert,
        expert,
        expert,
    )
    out_specs = (
        tokens,
        tokens,
        P(both),
        P(both, None),
        P(both, None),
        P(both, None),
        P(None, both),
        P(both),
        P(both, None),
        expert,
        expert,
        expert,
    )
    return jax.shard_map(on_device, mesh=mesh, in_specs=in_specs, out_specs=out_specs, check_vma=False)
```
